32 devices in a mesh: img: 16 (over z, y, core), tok: 2 (over x).
Axes of the slice: x: 2, y: 2, z: 4, core: 2. Of those that a mesh axis runs over, the one named last changes fastest.
Arguments:
- tokens: bfloat16 [16, 256, 1280], P('img', 'tok'), may hold values from -6 to 6
- grad_out: bfloat16 [16, 256, 1280], P('img', 'tok'), may hold values from -6 to 6
- router: bfloat16 [1280, 8], replicated, may hold values from -0.15625 to 0.15625
- slot_scale: float32 [8], replicated, may hold values from 1 to 8
- w_in: bfloat16 [16, 1280, 2048], P('img', None, 'tok'), may hold values from -0.15625 to 0.15625
- w_out: bfloat16 [16, 2048, 1280], P('img', 'tok'), may hold values from -0.09375 to 0.09375
Outputs:
- combined: bfloat16 [16, 256, 1280], P('img', 'tok')
- grad_tokens: bfloat16 [16, 256, 1280], P('img', 'tok')
- grad_router: float32 [1280, 8], replicated
- grad_scale: float32 [8], replicated
- grad_w_in: bfloat16 [16, 1280, 2048], P('img', None, 'tok')
- grad_w_out: bfloat16 [16, 2048, 1280], P('img', 'tok')
The draws below stay inside these ranges and needn't reach their ends.
All inputs are finite; a program needn't handle non-finite values.
Results may differ from the reference program's by a relative error of at most 0.015.
Values may be sent and summed in bfloat16 or wider, within the bound.
No kernel may reach another device: no remote copies, remote signals or barrier semaphores. Data moves between devices by JAX's collectives and lax.ppermute only.
A program may use at most 64 MiB of HBM per device.

```python
import math
import jax
import jax.numpy as jnp
from jax import lax

D = 1280
FF = 4096
TOKENS = 256
EXPERTS = 8
IMAGES = 16


def levels(stream_key, extent, pieces, least, largest):
    loudness, own = 1.0, jax.random.fold_in(stream_key, 6)
    for position, shards_of in pieces:
        heights = jnp.exp(jax.random.uniform(jax.random.fold_in(own, position), (shards_of,), jnp.float32, least / len(pieces), largest / len(pieces)))
        loudness = loudness * jnp.repeat(heights, extent[position] // shards_of).reshape([-1 if axis == position else 1 for axis in range(len(extent))])
    return loudness


def centred(own_key, shape, width, bound, shards=(), dtype=jnp.bfloat16):
    factor_of = levels(own_key, shape, shards, -0.22, 0.18) if shards else 1.0
    array = jax.random.normal(own_key, shape, jnp.float32) * width * factor_of
    return jnp.minimum(jnp.maximum(array, -bound), bound).astype(dtype)


def setup_inputs(seed: int = 0) -> dict:
    streams_of = jax.random.split(jax.random.key(seed), 7)
    return {
        "tokens": centred(streams_of[0], (IMAGES, TOKENS, D), 1.0, 6.0, ((0, 16), (1, 2))),
        "grad_out": centred(streams_of[1], (IMAGES, TOKENS, D), 1.0, 6.0, ((0, 16), (1, 2))),
        "router": centred(streams_of[2], (D, EXPERTS), D ** -0.5, 0.15625),
        "slot_scale": jnp.clip(jnp.exp(jax.random.uniform(streams_of[3], (EXPERTS,), jnp.float32, math.log(1.0), math.log(8.0))), 1.0, 8.0),
        "w_in": centred(streams_of[4], (2 * EXPERTS, D, FF // 2), D ** -0.5, 0.15625, ((0, 16), (2, 2))),
        "w_out": centred(streams_of[5], (2 * EXPERTS, FF // 2, D), FF ** -0.5, 0.09375, ((0, 16), (1, 2))),
    }


EPSILON = 1e-06
ROOT_HALF = 0.7071067811865476
DENSITY = 0.3989422804014327

def gelu_value(values):
    return values * (0.5 * (1.0 + lax.erf(values * ROOT_HALF)))

def gelu_slope(values):
    return 0.5 * (1.0 + lax.erf(values * ROOT_HALF)) + values * jnp.exp(-0.5 * values * values) * DENSITY

def reference(tokens, grad_out, router, slot_scale, w_in, w_out):
    single = jnp.float32
    half_type = jnp.bfloat16
    router_f = router.astype(single)
    inv_p = lax.rsqrt(lax.optimization_barrier(jnp.sum(router_f * router_f, 0)) + EPSILON)
    column = inv_p * slot_scale

    def front(image):
        raw = jnp.dot(image, router, preferred_element_type=single)
        image_f = image.astype(single)
        inv_x = lax.rsqrt(lax.optimization_barrier(jnp.sum(image_f * image_f, 1)) + EPSILON)
        logit = raw * inv_x[:, None] * column[None, :]
        expo = jnp.exp(logit)
        den = lax.optimization_barrier(jnp.sum(expo, 0))
        numer = jnp.dot(expo.astype(half_type).T, image, preferred_element_type=single)
        slots = (numer / den[:, None]).astype(half_type)
        return (slots, logit, den)
    slots, logits, dens = lax.map(front, tokens)
    halves_in = jnp.transpose(w_in.reshape(2, EXPERTS, D, FF // 2), (1, 0, 2, 3))
    halves_out = jnp.transpose(w_out.reshape(2, EXPERTS, FF // 2, D), (1, 0, 2, 3))
    rows = jnp.transpose(slots, (1, 0, 2))

    def expert_fwd(items):
        rows_e, first_w, second_w = items
        total = jnp.zeros((IMAGES, D), single)
        for copy in range(2):
            act = jnp.dot(rows_e, first_w[copy], preferred_element_type=single)
            hidden = gelu_value(act).astype(half_type)
            part = jnp.dot(hidden, second_w[copy], preferred_element_type=single).astype(half_type)
            total = total + part.astype(single)
        return total.astype(half_type)
    ys = jnp.transpose(lax.map(expert_fwd, (rows, halves_in, halves_out)), (1, 0, 2))

    def middle(items):
        logit, ys_image, grad_image = items
        expo = jnp.exp(logit)
        comb = expo / lax.optimization_barrier(jnp.sum(expo, 1, keepdims=True))
        comb_b = comb.astype(half_type)
        output = jnp.dot(comb_b, ys_image, preferred_element_type=single).astype(half_type)
        dys = jnp.dot(comb_b.T, grad_image, preferred_element_type=single).astype(half_type)
        dcomb = jnp.dot(grad_image, ys_image.T, preferred_element_type=single)
        dlc = comb * (dcomb - lax.optimization_barrier(jnp.sum(comb * dcomb, 1, keepdims=True)))
        return (output, dys, dlc)
    combined, dys, dlcs = lax.map(middle, (logits, ys, grad_out))
    dz_all = jnp.transpose(dys, (1, 0, 2))

    def expert_bwd(items):
        rows_e, dz_e, first_w, second_w = items
        total = jnp.zeros((IMAGES, D), single)
        first_list = []
        second_list = []
        for copy in range(2):
            act = jnp.dot(rows_e, first_w[copy], preferred_element_type=single)
            hidden = gelu_value(act).astype(half_type)
            grad_h = jnp.dot(dz_e, second_w[copy].T, preferred_element_type=single)
            dact = (grad_h * gelu_slope(act)).astype(half_type)
            part = jnp.dot(dact, first_w[copy].T, preferred_element_type=single).astype(half_type)
            total = total + part.astype(single)
            first_list.append(jnp.dot(rows_e.T, dact, preferred_element_type=single).astype(half_type))
            second_list.append(jnp.dot(hidden.T, dz_e, preferred_element_type=single).astype(half_type))
        return (total.astype(half_type), jnp.stack(first_list), jnp.stack(second_list))
    drows, first_grads, second_grads = lax.map(expert_bwd, (rows, dz_all, halves_in, halves_out))
    dxs = jnp.transpose(drows, (1, 0, 2))

    def router_bwd(carry, items):
        outer_acc, total_acc = carry
        image, logit, den, dxs_image, dlc = items
        image_f = image.astype(single)
        inv_x = lax.rsqrt(lax.optimization_barrier(jnp.sum(image_f * image_f, 1)) + EPSILON)
        expo = jnp.exp(logit)
        disp_w = expo / den[None, :]
        weights_b = expo.astype(half_type)
        ddisp = jnp.dot(image, dxs_image.T, preferred_element_type=single)
        corr = lax.optimization_barrier(jnp.sum(disp_w * ddisp, 0))
        grad_l = disp_w * (ddisp - corr[None, :]) + dlc
        product = grad_l * logit
        signal = lax.optimization_barrier(jnp.sum(product, 1))
        grad_q = (grad_l * column[None, :] * inv_x[:, None]).astype(half_type)
        scaled = (dxs_image.astype(single) / den[:, None]).astype(half_type)
        grad_image = jnp.dot(weights_b, scaled, preferred_element_type=single)
        grad_image = grad_image + jnp.dot(grad_q, router.T, preferred_element_type=single)
        grad_image = grad_image - (inv_x * inv_x * signal)[:, None] * image_f
        outer_acc = outer_acc + jnp.dot(image.T, grad_q, preferred_element_type=single)
        total_acc = total_acc + lax.optimization_barrier(jnp.sum(product, 0))
        return ((outer_acc, total_acc), grad_image.astype(half_type))
    start = (jnp.zeros((D, EXPERTS), single), jnp.zeros((EXPERTS,), single))
    (outer, total), grad_tokens = lax.scan(router_bwd, start, (tokens, logits, dens, dxs, dlcs))
    grad_router = outer - (inv_p * inv_p * total)[None, :] * router_f
    grad_scale = total / slot_scale
    grad_w_in = jnp.transpose(first_grads, (1, 0, 2, 3)).reshape(2 * EXPERTS, D, FF // 2)
    grad_w_out = jnp.transpose(second_grads, (1, 0, 2, 3)).reshape(2 * EXPERTS, FF // 2, D)
    return (combined, grad_tokens, grad_router, grad_scale, grad_w_in, grad_w_out)
```

```python
import functools

import jax
import jax.numpy as jnp
from jax import lax
from jax.experimental import pallas as pl
from jax.experimental.pallas import tpu as pltpu
from jax.sharding import PartitionSpec as P

EPSILON = 1e-06
ROOT_HALF = 0.7071067811865476
DENSITY = 0.3989422804014327
BF = jnp.bfloat16
F32 = jnp.float32
BOTH = ("img", "tok")
LANES = 128


def dot(left, right, dims):
    return lax.dot_general(left, right, (dims, ((), ())), preferred_element_type=F32)


def log2(size):
    assert size & (size - 1) == 0
    return size.bit_length() - 1


def iota(shape, axis):
    return lax.broadcasted_iota(jnp.int32, shape, axis)


def selection(shape, row_key, column_key):
    hit = row_key(iota(shape, 0)) == column_key(iota(shape, 1))
    return jnp.where(hit, 1.0, 0.0).astype(BF)


def stacked_key(count):
    return lambda row: row


def by_image(images, halves):
    return lambda row: (row & 1) * images + (row >> (1 + log2(halves)))


def by_expert(experts, halves):
    return lambda row: (row & 1) * experts + ((row >> (1 + log2(halves))) & (experts - 1))


def as_column(row):
    size = row.shape[1]
    eye = iota((size, size), 0) == iota((size, size), 1)
    return jnp.sum(jnp.where(eye, row, 0.0), 1, keepdims=True)


def row_of(column):
    return jnp.transpose(jnp.broadcast_to(column, (column.shape[0], LANES)))[:1]


def stack_rows(first, second, extras):
    lane = iota((first.shape[0], LANES), 1)
    high = jnp.zeros(lane.shape, F32)
    low = jnp.zeros(lane.shape, F32)
    for place, value in enumerate(extras):
        top = value.astype(BF).astype(F32)
        high = jnp.where(lane == place, top, high)
        low = jnp.where(lane == place, value - top, low)
    return jnp.concatenate(
        [jnp.concatenate([first, high], 1), jnp.concatenate([second, low], 1)], 0
    ).astype(BF)


def slot_column(router_ref, scale_ref):
    router_f = router_ref[...].astype(F32)
    inv_p = lax.rsqrt(jnp.sum(router_f * router_f, 1, keepdims=True) + EPSILON)
    scale = as_column(scale_ref[...])
    return router_f, inv_p, scale


def softmax(logit):
    expo = jnp.exp(logit)
    return expo, expo / jnp.sum(expo, 0, keepdims=True)


def front_kernel(halves, tok_ref, grad_ref, router_ref, scale_ref, sent_ref, logit_ref, inv_ref):
    experts = router_ref.shape[0]
    tok = tok_ref[0]
    tok_f = tok.astype(F32)
    inv_x = row_of(lax.rsqrt(jnp.sum(tok_f * tok_f, 1, keepdims=True) + EPSILON))
    _, inv_p, scale = slot_column(router_ref, scale_ref)
    raw = dot(router_ref[...], tok, ((1,), (1,)))
    logit = raw * inv_x * (inv_p * scale)
    expo, comb = softmax(logit)
    numer = dot(expo.astype(BF), tok, ((1,), (0,)))
    dys = dot(comb.astype(BF), grad_ref[0], ((1,), (0,)))
    rows = stack_rows(numer, dys, [jnp.sum(expo, 1, keepdims=True)])
    spread = selection(
        (sent_ref.shape[0], 2 * experts), by_expert(experts, halves), stacked_key(experts)
    )
    sent_ref[...] = dot(spread, rows, ((1,), (0,))).astype(BF)
    logit_ref[...] = logit
    inv_ref[...] = inv_x


def expert_kernel(
    images, halves, got_ref, one_ref, two_ref, back_ref, rows_ref, grad_rows_ref, hidden_ref, dact_ref
):
    width = one_ref.shape[1]
    gather = selection(
        (2 * images, got_ref.shape[0]), stacked_key(images), by_image(images, halves)
    )
    sums = dot(gather, got_ref[...], ((1,), (0,)))
    den = sums[:images, width : width + 1] + sums[images:, width : width + 1]
    rows = (sums[:images, :width] / den).astype(BF)
    grad_rows = sums[images:, :width].astype(BF)
    act = dot(rows, one_ref[0], ((1,), (0,)))
    grad_h = dot(grad_rows, two_ref[0], ((1,), (1,)))
    phi = 0.5 * (1.0 + lax.erf(act * ROOT_HALF))
    hidden = (act * phi).astype(BF)
    dact = (grad_h * (phi + act * jnp.exp(-0.5 * act * act) * DENSITY)).astype(BF)
    out_part = dot(hidden, two_ref[0], ((1,), (0,)))
    in_part = dot(dact, one_ref[0], ((1,), (1,)))
    corr = jnp.sum(dact.astype(F32) * act, 1, keepdims=True)
    spread = selection(
        (back_ref.shape[0], 2 * images), by_image(images, halves), stacked_key(images)
    )
    packed = stack_rows(out_part, in_part, [den, corr])
    back_ref[...] = dot(spread, packed, ((1,), (0,))).astype(BF)
    rows_ref[...] = rows
    grad_rows_ref[...] = grad_rows
    hidden_ref[...] = hidden
    dact_ref[...] = dact


def middle_kernel(
    halves, copies, back_ref, tok_ref, grad_ref, logit_ref, inv_ref, router_ref, scale_ref,
    sums_ref, outs_ref, coef_ref, mix_ref, signal_ref,
):
    experts, width = router_ref.shape
    gather = selection(
        (2 * experts, back_ref.shape[0]), stacked_key(experts), by_expert(experts, halves)
    )
    sums = dot(gather, back_ref[...], ((1,), (0,)))
    extras = sums[:experts, width:] + sums[experts:, width:]
    den = extras[:, :1] * (1.0 / (copies * halves))
    corr = extras[:, 1:2]
    ys = sums[:experts, :width].astype(BF)
    dxs = sums[experts:, :width].astype(BF)
    router_f, inv_p, scale = slot_column(router_ref, scale_ref)
    tok = tok_ref[0]
    logit = logit_ref[...]
    inv_x = inv_ref[...]
    expo, comb = softmax(logit)
    dcomb = dot(ys, grad_ref[0], ((1,), (1,)))
    ddisp = dot(dxs, tok, ((1,), (1,)))
    dlc = comb * (dcomb - jnp.sum(comb * dcomb, 0, keepdims=True))
    grad_l = expo / den * (ddisp - corr) + dlc
    product = grad_l * logit
    grad_q = (grad_l * inv_x * (inv_p * scale)).astype(BF)
    outer = dot(grad_q, tok, ((1,), (0,)))
    total = jnp.sum(product, 1, keepdims=True)
    local = outer - inv_p * inv_p * total * router_f
    lane = iota((experts, LANES), 1)
    sums_ref[...] = jnp.concatenate([local, jnp.where(lane == 0, total / scale, 0.0)], 1)
    outs_ref[...] = ys
    coef_ref[...] = jnp.concatenate([expo, grad_q.astype(F32)], 0).astype(BF)
    mix_ref[...] = jnp.concatenate([dxs.astype(F32) / den, router_f], 0).astype(BF)
    signal_ref[...] = inv_x * inv_x * jnp.sum(product, 0, keepdims=True)


def tail_kernel(tok_ref, logit_ref, outs_ref, coef_ref, mix_ref, signal_ref, combined_ref, grads_ref):
    _, comb = softmax(logit_ref[...])
    combined_ref[0] = dot(comb.astype(BF), outs_ref[...], ((0,), (0,))).astype(BF)
    signal = signal_ref[...]
    column = jnp.transpose(jnp.broadcast_to(signal, (LANES, signal.shape[1])))[:, :1]
    grads = dot(coef_ref[...], mix_ref[...], ((0,), (0,)))
    grads_ref[0] = (grads - column * tok_ref[0].astype(F32)).astype(BF)


def call(kernel, outs, *args, flops=10**7, room=24 * 2**20):
    return pl.pallas_call(
        kernel,
        out_shape=[jax.ShapeDtypeStruct(shape, dtype) for shape, dtype in outs],
        in_specs=[pl.BlockSpec(memory_space=pltpu.VMEM)] * len(args),
        out_specs=[pl.BlockSpec(memory_space=pltpu.VMEM)] * len(outs),
        compiler_params=pltpu.CompilerParams(vmem_limit_bytes=room),
        cost_estimate=pl.CostEstimate(
            flops=flops, bytes_accessed=sum(a.size * a.dtype.itemsize for a in args), transcendentals=0
        ),
    )(*args)


def exchange(block, devices):
    moved = lax.all_to_all(
        block.reshape(devices, 2, block.shape[1]), BOTH, split_axis=0, concat_axis=0, tiled=True
    )
    return moved.reshape(block.shape)


def pair(term, mask, devices):
    return lax.ppermute(term, BOTH, [(d, d ^ mask) for d in range(devices)])


def sum_everywhere(term, devices):
    bits = [1 << place for place in range(log2(devices))]
    chip_bits = [bits[0]] + bits[2:]
    term = term + pair(term, bits[1], devices)
    for place in range(0, len(chip_bits), 2):
        group = chip_bits[place : place + 2]
        sent = term.astype(BF)
        near = sent.astype(F32) + pair(sent, group[0], devices).astype(F32)
        if len(group) == 2:
            far = pair(sent, group[1], devices).astype(F32)
            far = far + pair(sent, group[0] ^ group[1], devices).astype(F32)
            near = near + far
        term = near
    return term


def shards(images, halves, tokens, grad_out, router, slot_scale, w_in, w_out):
    devices = images * halves
    tok_rows, width = tokens.shape[1:]
    experts = router.shape[1]
    copies = images // experts
    hidden_dev = w_in.shape[2]
    long = width + LANES
    router_t = router.T
    scale_row = slot_scale.reshape(1, experts)
    sent, logit, inv_x = call(
        functools.partial(front_kernel, halves),
        [((2 * devices, long), BF), ((experts, tok_rows), F32), ((1, tok_rows), F32)],
        tokens, grad_out, router_t, scale_row,
    )
    got = exchange(sent, devices)
    back, rows, grad_rows, hidden, dact = call(
        functools.partial(expert_kernel, images, halves),
        [((2 * devices, long), BF), ((images, width), BF), ((images, width), BF),
         ((images, hidden_dev), BF), ((images, hidden_dev), BF)],
        got, w_in, w_out,
    )
    back = exchange(back, devices)
    grad_w_in = dot(rows, dact, ((0,), (0,))).astype(BF)[None]
    grad_w_out = dot(hidden, grad_rows, ((0,), (0,))).astype(BF)[None]
    sums, ys, coef, mix, signal = call(
        functools.partial(middle_kernel, halves, copies),
        [((experts, long), F32), ((experts, width), BF), ((2 * experts, tok_rows), BF),
         ((2 * experts, width), BF), ((1, tok_rows), F32)],
        back, tokens, grad_out, logit, inv_x, router_t, scale_row,
    )
    combined, grad_tokens = call(
        tail_kernel,
        [(tokens.shape, BF), (tokens.shape, BF)],
        tokens, logit, ys, coef, mix, signal,
    )
    sums = sum_everywhere(sums, devices)
    return (combined, grad_tokens, sums[:, :width].T, sums[:, width], grad_w_in, grad_w_out)


def solution(mesh):
    images, halves = mesh.shape["img"], mesh.shape["tok"]

    def body(*args):
        return shards(images, halves, *args)

    return jax.shard_map(
        body,
        mesh=mesh,
        in_specs=(
            P("img", "tok", None),
            P("img", "tok", None),
            P(),
            P(),
            P("img", None, "tok"),
            P("img", "tok", None),
        ),
        out_specs=(
            P("img", "tok", None),
            P("img", "tok", None),
            P(),
            P(),
            P("img", None, "tok"),
            P("img", "tok", None),
        ),
        check_vma=False,
    )
```

```python
import functools

import jax
import jax.numpy as jnp
from jax import lax
from jax.experimental import pallas as pl
from jax.experimental.pallas import tpu as pltpu
from jax.sharding import PartitionSpec as P

EPSILON = 1e-06
ROOT_HALF = 0.7071067811865476
DENSITY = 0.3989422804014327
BF = jnp.bfloat16
F32 = jnp.float32
BOTH = ("img", "tok")
LANES = 128
FRONT = 4 * 10**9


def dot(left, right, dims):
    return lax.dot_general(left, right, (dims, ((), ())), preferred_element_type=F32)


def log2(size):
    assert size & (size - 1) == 0
    return size.bit_length() - 1


def iota(shape, axis):
    return lax.broadcasted_iota(jnp.int32, shape, axis)


def digits(row, sizes):
    out = []
    for size in reversed(sizes):
        out.append(row & (size - 1))
        row = row >> log2(size)
    return out[::-1]


def selection(shape, row_key, column_key):
    hit = row_key(iota(shape, 0)) == column_key(iota(shape, 1))
    return jnp.where(hit, 1.0, 0.0).astype(BF)


def pick(left_key, left_size, right, right_key):
    return dot(selection((left_size, right.shape[0]), left_key, right_key), right, ((1,), (0,)))


def itself(row):
    return row


def as_column(row):
    size = row.shape[1]
    eye = iota((size, size), 0) == iota((size, size), 1)
    return jnp.sum(jnp.where(eye, row, 0.0), 1, keepdims=True)


def row_of(column):
    return jnp.transpose(jnp.broadcast_to(column, (column.shape[0], LANES)))[:1]


def stack_rows(first, second, extras):
    lane = iota((first.shape[0], LANES), 1)
    high = jnp.zeros(lane.shape, F32)
    low = jnp.zeros(lane.shape, F32)
    for place, value in enumerate(extras):
        top = value.astype(BF).astype(F32)
        high = jnp.where(lane == place, top, high)
        low = jnp.where(lane == place, value - top, low)
    return jnp.concatenate(
        [jnp.concatenate([first, high], 1), jnp.concatenate([second, low], 1)], 0
    ).astype(BF)


def slot_column(router_ref, scale_ref):
    router_f = router_ref[...].astype(F32)
    inv_p = lax.rsqrt(jnp.sum(router_f * router_f, 1, keepdims=True) + EPSILON)
    scale = as_column(scale_ref[...])
    return router_f, inv_p, scale


def softmax(logit):
    expo = jnp.exp(logit)
    return expo, expo / jnp.sum(expo, 0, keepdims=True)


def fetch(sources, targets, sems):
    copies = [
        pltpu.make_async_copy(source, target, sems.at[place])
        for place, (source, target) in enumerate(zip(sources, targets))
    ]
    for copy in copies:
        copy.start()
    return copies


def expert_rows(plan, experts):
    copies, halves = plan

    def key(row):
        _, place, _, kind = digits(row, (copies, experts, halves, 2))
        return kind * experts + place

    return key


def image_rows(images, halves):
    def key(row):
        place, _, kind = digits(row, (images, halves, 2))
        return kind * images + place

    return key


def front_kernel(
    plan, tok_hbm, grad_hbm, router_hbm, scale_hbm, sent_ref, logit_ref, inv_ref,
    tok_ref, grad_ref, router_ref, scale_ref, sems,
):
    arrived = fetch(
        [tok_hbm, router_hbm, scale_hbm, grad_hbm], [tok_ref, router_ref, scale_ref, grad_ref], sems
    )
    for copy in arrived[:3]:
        copy.wait()
    tok = tok_ref[0]
    tok_f = tok.astype(F32)
    inv_x = row_of(lax.rsqrt(jnp.sum(tok_f * tok_f, 1, keepdims=True) + EPSILON))
    _, inv_p, scale = slot_column(router_ref, scale_ref)
    raw = dot(router_ref[...], tok, ((1,), (1,)))
    logit = raw * inv_x * (inv_p * scale)
    expo, comb = softmax(logit)
    numer = dot(expo.astype(BF), tok, ((1,), (0,)))
    arrived[3].wait()
    dys = dot(comb.astype(BF), grad_ref[0], ((1,), (0,)))
    rows = stack_rows(numer, dys, [jnp.sum(expo, 1, keepdims=True)])
    sent_ref[...] = pick(expert_rows(plan, router_ref.shape[0]), sent_ref.shape[0], rows, itself).astype(BF)
    logit_ref[...] = logit
    inv_ref[...] = inv_x


def expert_kernel(
    images, halves, got_ref, one_ref, two_ref, back_ref, rows_ref, grad_rows_ref, hidden_ref, dact_ref
):
    width = one_ref.shape[1]
    key = image_rows(images, halves)
    sums = pick(itself, 2 * images, got_ref[...], key)
    den = sums[:images, width : width + 1] + sums[images:, width : width + 1]
    rows = (sums[:images, :width] / den).astype(BF)
    grad_rows = sums[images:, :width].astype(BF)
    act = dot(rows, one_ref[0], ((1,), (0,)))
    grad_h = dot(grad_rows, two_ref[0], ((1,), (1,)))
    phi = 0.5 * (1.0 + lax.erf(act * ROOT_HALF))
    hidden = (act * phi).astype(BF)
    dact = (grad_h * (phi + act * jnp.exp(-0.5 * act * act) * DENSITY)).astype(BF)
    out_part = dot(hidden, two_ref[0], ((1,), (0,)))
    in_part = dot(dact, one_ref[0], ((1,), (1,)))
    corr = jnp.sum(dact.astype(F32) * act, 1, keepdims=True)
    packed = stack_rows(out_part, in_part, [den, corr])
    back_ref[...] = pick(key, back_ref.shape[0], packed, itself).astype(BF)
    rows_ref[...] = rows
    grad_rows_ref[...] = grad_rows
    hidden_ref[...] = hidden
    dact_ref[...] = dact


def outer_kernel(size, left_ref, right_ref, out_hbm, out_ref, sems):
    copies = []
    for place in range(left_ref.shape[1] // size):
        part = slice(place * size, (place + 1) * size)
        out_ref[0, part] = dot(left_ref[:, part], right_ref[...], ((0,), (0,))).astype(BF)
        copy = pltpu.make_async_copy(
            out_ref.at[:, pl.ds(place * size, size)], out_hbm.at[:, pl.ds(place * size, size)],
            sems.at[place],
        )
        copy.start()
        copies.append(copy)
    for copy in copies:
        copy.wait()


def middle_kernel(
    plan, back_ref, tok_ref, grad_ref, logit_ref, inv_ref, router_ref, scale_ref,
    sums_ref, outs_ref, coef_ref, mix_ref, signal_ref,
):
    experts, width = router_ref.shape
    sums = pick(itself, 2 * experts, back_ref[...], expert_rows(plan, router_ref.shape[0]))
    extras = sums[:experts, width:] + sums[experts:, width:]
    den = extras[:, :1] * (1.0 / (plan[0] * plan[1]))
    corr = extras[:, 1:2]
    ys = sums[:experts, :width].astype(BF)
    dxs = sums[experts:, :width].astype(BF)
    router_f, inv_p, scale = slot_column(router_ref, scale_ref)
    tok = tok_ref[0]
    logit = logit_ref[...]
    inv_x = inv_ref[...]
    expo, comb = softmax(logit)
    dcomb = dot(ys, grad_ref[0], ((1,), (1,)))
    ddisp = dot(dxs, tok, ((1,), (1,)))
    dlc = comb * (dcomb - jnp.sum(comb * dcomb, 0, keepdims=True))
    grad_l = expo / den * (ddisp - corr) + dlc
    product = grad_l * logit
    grad_q = (grad_l * inv_x * (inv_p * scale)).astype(BF)
    outer = dot(grad_q, tok, ((1,), (0,)))
    total = jnp.sum(product, 1, keepdims=True)
    local = outer - inv_p * inv_p * total * router_f
    lane = iota((experts, LANES), 1)
    sums_ref[...] = jnp.concatenate([local, jnp.where(lane == 0, total / scale, 0.0)], 1)
    outs_ref[...] = ys
    coef_ref[...] = jnp.concatenate([expo, grad_q.astype(F32)], 0).astype(BF)
    mix_ref[...] = jnp.concatenate([dxs.astype(F32) / den, router_f], 0).astype(BF)
    signal_ref[...] = inv_x * inv_x * jnp.sum(product, 0, keepdims=True)


def tail_kernel(tok_ref, logit_ref, outs_ref, coef_ref, mix_ref, signal_ref, combined_ref, grads_ref):
    _, comb = softmax(logit_ref[...])
    combined_ref[0] = dot(comb.astype(BF), outs_ref[...], ((0,), (0,))).astype(BF)
    signal = signal_ref[...]
    column = jnp.transpose(jnp.broadcast_to(signal, (LANES, signal.shape[1])))[:, :1]
    grads = dot(coef_ref[...], mix_ref[...], ((0,), (0,)))
    grads_ref[0] = (grads - column * tok_ref[0].astype(F32)).astype(BF)


def last_kernel(own_ref, other_ref, router_ref, scale_ref):
    sums = own_ref[...].astype(F32) + other_ref[...].astype(F32)
    experts, width = router_ref.shape
    router_ref[...] = sums[:, :width]
    eye = iota((experts, experts), 0) == iota((experts, experts), 1)
    scale_ref[...] = jnp.sum(jnp.where(eye, sums[:, width : width + 1], 0.0), 0, keepdims=True)


def call(kernel, outs, *args, stays=(), buffers=(), flops=10**7, room=24 * 2**20, home=pltpu.VMEM):
    specs = [pl.BlockSpec(memory_space=pltpu.VMEM)] * len(args)
    args = list(args)
    for place in stays:
        specs[place] = pl.BlockSpec(memory_space=pltpu.HBM)
        args[place] = pltpu.with_memory_space_constraint(args[place], pltpu.HBM)
    return pl.pallas_call(
        kernel,
        out_shape=[jax.ShapeDtypeStruct(shape, dtype) for shape, dtype in outs],
        in_specs=specs,
        out_specs=[pl.BlockSpec(memory_space=home)] * len(outs),
        scratch_shapes=buffers,
        compiler_params=pltpu.CompilerParams(vmem_limit_bytes=room),
        cost_estimate=pl.CostEstimate(
            flops=flops, bytes_accessed=sum(a.size * a.dtype.itemsize for a in args), transcendentals=0
        ),
    )(*args)


def weight_grad(left, right):
    size = 256
    shape = (1, left.shape[1], right.shape[1])
    (out,) = call(
        functools.partial(outer_kernel, size), [(shape, BF)], left, right,
        buffers=[pltpu.VMEM(shape, BF), pltpu.SemaphoreType.DMA((shape[1] // size,))],
        flops=10**9, home=pltpu.HBM,
    )
    return out


def exchange(block, devices):
    moved = lax.all_to_all(
        block.reshape(devices, 2, block.shape[1]), BOTH, split_axis=0, concat_axis=0, tiled=True
    )
    return moved.reshape(block.shape)


def pair(term, place, devices):
    return lax.ppermute(term, BOTH, [(d, d ^ (1 << place)) for d in range(devices)])


def sum_everywhere(term, devices, beside):
    order = [1, 0] + list(range(2, log2(devices)))
    done = []
    term = term + pair(term, order[0], devices)
    for place in order[1:]:
        own = term.astype(BF)
        other = pair(own, place, devices)
        if beside:
            other, ready = lax.optimization_barrier((other, beside[0]))
            beside = beside[1:]
            done.append(ready)
        term = own.astype(F32) + other.astype(F32)
    return own, other, done + list(beside)


def shards(images, halves, tokens, grad_out, router, slot_scale, w_in, w_out):
    devices = images * halves
    tok_rows, width = tokens.shape[1:]
    experts = router.shape[1]
    plan = (images // experts, halves)
    hidden_dev = w_in.shape[2]
    long = width + LANES
    router_t = router.T
    scale_row = slot_scale.reshape(1, experts)
    inputs = (tokens, grad_out, router_t, scale_row)
    sent, logit, inv_x = call(
        functools.partial(front_kernel, plan),
        [((2 * devices, long), BF), ((experts, tok_rows), F32), ((1, tok_rows), F32)],
        *inputs,
        stays=range(4),
        buffers=[pltpu.VMEM(a.shape, a.dtype) for a in inputs] + [pltpu.SemaphoreType.DMA((4,))],
        flops=FRONT,
    )
    got = exchange(sent, devices)
    back, rows, grad_rows, hidden, dact = call(
        functools.partial(expert_kernel, images, halves),
        [((2 * devices, long), BF), ((images, width), BF), ((images, width), BF),
         ((images, hidden_dev), BF), ((images, hidden_dev), BF)],
        got, w_in, w_out,
        flops=10**9,
    )
    back = exchange(back, devices)
    grad_w_in = weight_grad(rows, dact)
    grad_w_out = weight_grad(hidden, grad_rows)
    sums, ys, coef, mix, signal = call(
        functools.partial(middle_kernel, plan),
        [((experts, long), F32), ((experts, width), BF), ((2 * experts, tok_rows), BF),
         ((2 * experts, width), BF), ((1, tok_rows), F32)],
        back, tokens, grad_out, logit, inv_x, router_t, scale_row,
    )
    combined, grad_tokens = call(
        tail_kernel,
        [(tokens.shape, BF), (tokens.shape, BF)],
        tokens, logit, ys, coef, mix, signal,
    )
    own, other, (grad_w_in, grad_w_out, (combined, grad_tokens)) = sum_everywhere(
        sums, devices, [grad_w_in, grad_w_out, (combined, grad_tokens)]
    )
    grad_router, grad_scale = call(
        last_kernel, [((experts, width), F32), ((1, experts), F32)], own, other
    )
    return (combined, grad_tokens, grad_router.T, grad_scale[0], grad_w_in, grad_w_out)


def solution(mesh):
    images, halves = mesh.shape["img"], mesh.shape["tok"]

    def body(*args):
        return shards(images, halves, *args)

    return jax.shard_map(
        body,
        mesh=mesh,
        in_specs=(
            P("img", "tok", None),
            P("img", "tok", None),
            P(),
            P(),
            P("img", None, "tok"),
            P("img", "tok", None),
        ),
        out_specs=(
            P("img", "tok", None),
            P("img", "tok", None),
            P(),
            P(),
            P("img", None, "tok"),
            P("img", "tok", None),
        ),
        check_vma=False,
    )
```

```python
import functools

import jax
import jax.numpy as jnp
from jax import lax
from jax.experimental import pallas as pl
from jax.experimental.pallas import tpu as pltpu
from jax.sharding import PartitionSpec as P

EPSILON = 1e-06
ROOT_HALF = 0.7071067811865476
DENSITY = 0.3989422804014327
BF = jnp.bfloat16
F32 = jnp.float32
BOTH = ("img", "tok")
LANES = 128
FRONT = 4 * 10**9


def dot(left, right, dims):
    return lax.dot_general(left, right, (dims, ((), ())), preferred_element_type=F32)


def log2(size):
    assert size & (size - 1) == 0
    return size.bit_length() - 1


def iota(shape, axis):
    return lax.broadcasted_iota(jnp.int32, shape, axis)


def digits(row, sizes):
    out = []
    for size in reversed(sizes):
        out.append(row & (size - 1))
        row = row >> log2(size)
    return out[::-1]


def selection(shape, row_key, column_key):
    hit = row_key(iota(shape, 0)) == column_key(iota(shape, 1))
    return jnp.where(hit, 1.0, 0.0).astype(BF)


def pick(left_key, left_size, right, right_key):
    return dot(selection((left_size, right.shape[0]), left_key, right_key), right, ((1,), (0,)))


def store_blocks(ref, rows):
    ref[...] = rows.astype(BF).reshape(ref.shape)


def load_blocks(ref):
    return ref[...].reshape(2 * ref.shape[0], ref.shape[2])


def itself(row):
    return row


def as_column(row):
    size = row.shape[1]
    eye = iota((size, size), 0) == iota((size, size), 1)
    return jnp.sum(jnp.where(eye, row, 0.0), 1, keepdims=True)


def row_of(column):
    return jnp.transpose(jnp.broadcast_to(column, (column.shape[0], LANES)))[:1]


def stack_rows(first, second, extras):
    lane = iota((first.shape[0], LANES), 1)
    high = jnp.zeros(lane.shape, F32)
    low = jnp.zeros(lane.shape, F32)
    for place, value in enumerate(extras):
        top = value.astype(BF).astype(F32)
        high = jnp.where(lane == place, top, high)
        low = jnp.where(lane == place, value - top, low)
    return jnp.concatenate(
        [jnp.concatenate([first, high], 1), jnp.concatenate([second, low], 1)], 0
    ).astype(BF)


def slot_column(router_ref, scale_ref):
    router_f = router_ref[...].astype(F32)
    inv_p = lax.rsqrt(jnp.sum(router_f * router_f, 1, keepdims=True) + EPSILON)
    scale = as_column(scale_ref[...])
    return router_f, inv_p, scale


def softmax(logit):
    expo = jnp.exp(logit)
    return expo, expo / jnp.sum(expo, 0, keepdims=True)


def fetch(sources, targets, sems):
    copies = [
        pltpu.make_async_copy(source, target, sems.at[place])
        for place, (source, target) in enumerate(zip(sources, targets))
    ]
    for copy in copies:
        copy.start()
    return copies


def expert_rows(plan, experts):
    copies, halves = plan

    def key(row):
        _, place, _, kind = digits(row, (copies, experts, halves, 2))
        return kind * experts + place

    return key


def image_rows(images, halves):
    def key(row):
        place, _, kind = digits(row, (images, halves, 2))
        return kind * images + place

    return key


def front_kernel(
    plan, tok_hbm, grad_hbm, router_hbm, scale_hbm, sent_ref, logit_ref, inv_ref,
    tok_ref, grad_ref, router_ref, scale_ref, sems,
):
    arrived = fetch(
        [tok_hbm, router_hbm, scale_hbm, grad_hbm], [tok_ref, router_ref, scale_ref, grad_ref], sems
    )
    for copy in arrived[:3]:
        copy.wait()
    tok = tok_ref[0]
    tok_f = tok.astype(F32)
    inv_x = row_of(lax.rsqrt(jnp.sum(tok_f * tok_f, 1, keepdims=True) + EPSILON))
    _, inv_p, scale = slot_column(router_ref, scale_ref)
    raw = dot(router_ref[...], tok, ((1,), (1,)))
    logit = raw * inv_x * (inv_p * scale)
    expo, comb = softmax(logit)
    numer = dot(expo.astype(BF), tok, ((1,), (0,)))
    arrived[3].wait()
    dys = dot(comb.astype(BF), grad_ref[0], ((1,), (0,)))
    rows = stack_rows(numer, dys, [jnp.sum(expo, 1, keepdims=True)])
    store_blocks(sent_ref, pick(expert_rows(plan, router_ref.shape[0]), 2 * sent_ref.shape[0], rows, itself))
    logit_ref[...] = logit
    inv_ref[...] = inv_x


def expert_kernel(
    images, halves, got_ref, one_ref, two_ref, back_ref, rows_ref, grad_rows_ref, hidden_ref, dact_ref
):
    width = one_ref.shape[1]
    key = image_rows(images, halves)
    sums = pick(itself, 2 * images, load_blocks(got_ref), key)
    den = sums[:images, width : width + 1] + sums[images:, width : width + 1]
    rows = (sums[:images, :width] / den).astype(BF)
    grad_rows = sums[images:, :width].astype(BF)
    act = dot(rows, one_ref[0], ((1,), (0,)))
    grad_h = dot(grad_rows, two_ref[0], ((1,), (1,)))
    phi = 0.5 * (1.0 + lax.erf(act * ROOT_HALF))
    hidden = (act * phi).astype(BF)
    dact = (grad_h * (phi + act * jnp.exp(-0.5 * act * act) * DENSITY)).astype(BF)
    out_part = dot(hidden, two_ref[0], ((1,), (0,)))
    in_part = dot(dact, one_ref[0], ((1,), (1,)))
    corr = jnp.sum(dact.astype(F32) * act, 1, keepdims=True)
    packed = stack_rows(out_part, in_part, [den, corr])
    store_blocks(back_ref, pick(key, 2 * back_ref.shape[0], packed, itself))
    rows_ref[...] = rows
    grad_rows_ref[...] = grad_rows
    hidden_ref[...] = hidden
    dact_ref[...] = dact


def outer_kernel(size, left_ref, right_ref, out_hbm, out_ref, sems):
    copies = []
    for place in range(left_ref.shape[1] // size):
        part = slice(place * size, (place + 1) * size)
        out_ref[0, part] = dot(left_ref[:, part], right_ref[...], ((0,), (0,))).astype(BF)
        copy = pltpu.make_async_copy(
            out_ref.at[:, pl.ds(place * size, size)], out_hbm.at[:, pl.ds(place * size, size)],
            sems.at[place],
        )
        copy.start()
        copies.append(copy)
    for copy in copies:
        copy.wait()


def middle_kernel(
    plan, back_ref, tok_ref, grad_ref, logit_ref, inv_ref, router_ref, scale_ref,
    sums_ref, outs_ref, coef_ref, mix_ref, signal_ref,
):
    experts, width = router_ref.shape
    sums = pick(itself, 2 * experts, load_blocks(back_ref), expert_rows(plan, router_ref.shape[0]))
    extras = sums[:experts, width:] + sums[experts:, width:]
    den = extras[:, :1] * (1.0 / (plan[0] * plan[1]))
    corr = extras[:, 1:2]
    ys = sums[:experts, :width].astype(BF)
    dxs = sums[experts:, :width].astype(BF)
    router_f, inv_p, scale = slot_column(router_ref, scale_ref)
    tok = tok_ref[0]
    logit = logit_ref[...]
    inv_x = inv_ref[...]
    expo, comb = softmax(logit)
    dcomb = dot(ys, grad_ref[0], ((1,), (1,)))
    ddisp = dot(dxs, tok, ((1,), (1,)))
    dlc = comb * (dcomb - jnp.sum(comb * dcomb, 0, keepdims=True))
    grad_l = expo / den * (ddisp - corr) + dlc
    product = grad_l * logit
    grad_q = (grad_l * inv_x * (inv_p * scale)).astype(BF)
    outer = dot(grad_q, tok, ((1,), (0,)))
    total = jnp.sum(product, 1, keepdims=True)
    local = outer - inv_p * inv_p * total * router_f
    lane = iota((experts, LANES), 1)
    sums_ref[...] = jnp.concatenate([local, jnp.where(lane == 0, total / scale, 0.0)], 1)
    outs_ref[...] = ys
    coef_ref[...] = jnp.concatenate([expo, grad_q.astype(F32)], 0).astype(BF)
    mix_ref[...] = jnp.concatenate([dxs.astype(F32) / den, router_f], 0).astype(BF)
    signal_ref[...] = inv_x * inv_x * jnp.sum(product, 0, keepdims=True)


def tail_kernel(tok_ref, logit_ref, outs_ref, coef_ref, mix_ref, signal_ref, combined_ref, grads_ref):
    _, comb = softmax(logit_ref[...])
    combined_ref[0] = dot(comb.astype(BF), outs_ref[...], ((0,), (0,))).astype(BF)
    signal = signal_ref[...]
    column = jnp.transpose(jnp.broadcast_to(signal, (LANES, signal.shape[1])))[:, :1]
    grads = dot(coef_ref[...], mix_ref[...], ((0,), (0,)))
    grads_ref[0] = (grads - column * tok_ref[0].astype(F32)).astype(BF)


def last_kernel(own_ref, other_ref, *refs):
    *more, router_ref, scale_ref = refs
    sums = own_ref[...].astype(F32) + other_ref[...].astype(F32)
    if more:
        sums = sums + (more[0][...].astype(F32) + more[1][...].astype(F32))
    experts, width = router_ref.shape
    router_ref[...] = sums[:, :width]
    eye = iota((experts, experts), 0) == iota((experts, experts), 1)
    scale_ref[...] = jnp.sum(jnp.where(eye, sums[:, width : width + 1], 0.0), 0, keepdims=True)


def call(kernel, outs, *args, stays=(), buffers=(), flops=10**7, room=24 * 2**20, home=pltpu.VMEM):
    specs = [pl.BlockSpec(memory_space=pltpu.VMEM)] * len(args)
    args = list(args)
    for place in stays:
        specs[place] = pl.BlockSpec(memory_space=pltpu.HBM)
        args[place] = pltpu.with_memory_space_constraint(args[place], pltpu.HBM)
    return pl.pallas_call(
        kernel,
        out_shape=[jax.ShapeDtypeStruct(shape, dtype) for shape, dtype in outs],
        in_specs=specs,
        out_specs=[pl.BlockSpec(memory_space=home)] * len(outs),
        scratch_shapes=buffers,
        compiler_params=pltpu.CompilerParams(vmem_limit_bytes=room),
        cost_estimate=pl.CostEstimate(
            flops=flops, bytes_accessed=sum(a.size * a.dtype.itemsize for a in args), transcendentals=0
        ),
    )(*args)


def weight_grad(left, right):
    size = 256
    shape = (1, left.shape[1], right.shape[1])
    (out,) = call(
        functools.partial(outer_kernel, size), [(shape, BF)], left, right,
        buffers=[pltpu.VMEM(shape, BF), pltpu.SemaphoreType.DMA((shape[1] // size,))],
        flops=10**9, home=pltpu.HBM,
    )
    return out


def exchange(block):
    return lax.all_to_all(block, BOTH, split_axis=0, concat_axis=0, tiled=True)


def pair(term, mask, devices):
    return lax.ppermute(term, BOTH, [(d, d ^ mask) for d in range(devices)])


def sum_everywhere(term, devices, beside):
    term = term + pair(term, 2, devices)
    masks = [1] + [1 << place for place in range(2, log2(devices))]
    rounds = [masks[place : place + 2] for place in range(0, len(masks), 2)]
    done = []
    for group in rounds:
        if group is not rounds[0]:
            term = (terms[0].astype(F32) + terms[1].astype(F32)) + (
                terms[2].astype(F32) + terms[3].astype(F32)
            )
        own = term.astype(BF)
        terms = [own, pair(own, group[0], devices)]
        if len(group) == 2:
            terms += [pair(own, group[1], devices), pair(own, group[0] ^ group[1], devices)]
        if beside:
            terms[1], ready = lax.optimization_barrier((terms[1], beside[0]))
            beside = beside[1:]
            done.append(ready)
    return terms, done + list(beside)


def shards(images, halves, tokens, grad_out, router, slot_scale, w_in, w_out):
    devices = images * halves
    tok_rows, width = tokens.shape[1:]
    experts = router.shape[1]
    plan = (images // experts, halves)
    hidden_dev = w_in.shape[2]
    long = width + LANES
    router_t = router.T
    scale_row = slot_scale.reshape(1, experts)
    inputs = (tokens, grad_out, router_t, scale_row)
    sent, logit, inv_x = call(
        functools.partial(front_kernel, plan),
        [((devices, 2, long), BF), ((experts, tok_rows), F32), ((1, tok_rows), F32)],
        *inputs,
        stays=range(4),
        buffers=[pltpu.VMEM(a.shape, a.dtype) for a in inputs] + [pltpu.SemaphoreType.DMA((4,))],
        flops=FRONT,
    )
    got = exchange(sent)
    back, rows, grad_rows, hidden, dact = call(
        functools.partial(expert_kernel, images, halves),
        [((devices, 2, long), BF), ((images, width), BF), ((images, width), BF),
         ((images, hidden_dev), BF), ((images, hidden_dev), BF)],
        got, w_in, w_out,
        flops=10**9,
    )
    back = exchange(back)
    grad_w_in = weight_grad(rows, dact)
    grad_w_out = weight_grad(hidden, grad_rows)
    sums, ys, coef, mix, signal = call(
        functools.partial(middle_kernel, plan),
        [((experts, long), F32), ((experts, width), BF), ((2 * experts, tok_rows), BF),
         ((2 * experts, width), BF), ((1, tok_rows), F32)],
        back, tokens, grad_out, logit, inv_x, router_t, scale_row,
    )
    combined, grad_tokens = call(
        tail_kernel,
        [(tokens.shape, BF), (tokens.shape, BF)],
        tokens, logit, ys, coef, mix, signal,
    )
    terms, (grad_w_in, (grad_w_out, combined, grad_tokens)) = sum_everywhere(
        sums, devices, [grad_w_in, (grad_w_out, combined, grad_tokens)]
    )
    grad_router, grad_scale = call(
        last_kernel, [((experts, width), F32), ((1, experts), F32)], *terms
    )
    return (combined, grad_tokens, grad_router.T, grad_scale[0], grad_w_in, grad_w_out)


def solution(mesh):
    images, halves = mesh.shape["img"], mesh.shape["tok"]

    def body(*args):
        return shards(images, halves, *args)

    return jax.shard_map(
        body,
        mesh=mesh,
        in_specs=(
            P("img", "tok", None),
            P("img", "tok", None),
            P(),
            P(),
            P("img", None, "tok"),
            P("img", "tok", None),
        ),
        out_specs=(
            P("img", "tok", None),
            P("img", "tok", None),
            P(),
            P(),
            P("img", None, "tok"),
            P("img", "tok", None),
        ),
        check_vma=False,
    )
```

```python
import functools

import jax
import jax.numpy as jnp
from jax import lax
from jax.experimental import pallas as pl
from jax.experimental.pallas import tpu as pltpu
from jax.sharding import PartitionSpec as P

EPSILON = 1e-06
ROOT_HALF = 0.7071067811865476
DENSITY = 0.3989422804014327
BF = jnp.bfloat16
F32 = jnp.float32
BOTH = ("img", "tok")
LANES = 128
FRONT = 2 * 10**10


def dot(left, right, dims):
    return lax.dot_general(left, right, (dims, ((), ())), preferred_element_type=F32)


def log2(size):
    assert size & (size - 1) == 0
    return size.bit_length() - 1


def iota(shape, axis):
    return lax.broadcasted_iota(jnp.int32, shape, axis)


def digits(row, sizes):
    out = []
    for size in reversed(sizes):
        out.append(row & (size - 1))
        row = row >> log2(size)
    return out[::-1]


def selection(shape, row_key, column_key):
    hit = row_key(iota(shape, 0)) == column_key(iota(shape, 1))
    return jnp.where(hit, 1.0, 0.0).astype(BF)


def pick(left_key, left_size, right, right_key):
    return dot(selection((left_size, right.shape[0]), left_key, right_key), right, ((1,), (0,)))


def store_blocks(ref, rows):
    ref[...] = rows.astype(BF).reshape(ref.shape)


def load_blocks(ref):
    return ref[...].reshape(2 * ref.shape[0], ref.shape[2])


def itself(row):
    return row


def as_column(row):
    size = row.shape[1]
    eye = iota((size, size), 0) == iota((size, size), 1)
    return jnp.sum(jnp.where(eye, row, 0.0), 1, keepdims=True)


def row_of(column):
    return jnp.transpose(jnp.broadcast_to(column, (column.shape[0], LANES)))[:1]


def stack_rows(first, second, extras):
    lane = iota((first.shape[0], LANES), 1)
    high = jnp.zeros(lane.shape, F32)
    low = jnp.zeros(lane.shape, F32)
    for place, value in enumerate(extras):
        top = value.astype(BF).astype(F32)
        high = jnp.where(lane == place, top, high)
        low = jnp.where(lane == place, value - top, low)
    return jnp.concatenate(
        [jnp.concatenate([first, high], 1), jnp.concatenate([second, low], 1)], 0
    ).astype(BF)


def slot_column(router_ref, scale_ref):
    router_f = router_ref[...].astype(F32)
    inv_p = lax.rsqrt(jnp.sum(router_f * router_f, 1, keepdims=True) + EPSILON)
    scale = as_column(scale_ref[...])
    return router_f, inv_p, scale


def softmax(logit):
    expo = jnp.exp(logit)
    return expo, expo / jnp.sum(expo, 0, keepdims=True)


def fetch(sources, targets, sems):
    copies = [
        pltpu.make_async_copy(source, target, sems.at[place])
        for place, (source, target) in enumerate(zip(sources, targets))
    ]
    for copy in copies:
        copy.start()
    return copies


def expert_rows(plan, experts):
    copies, halves = plan

    def key(row):
        _, place, _, kind = digits(row, (copies, experts, halves, 2))
        return kind * experts + place

    return key


def image_rows(images, halves):
    def key(row):
        place, _, kind = digits(row, (images, halves, 2))
        return kind * images + place

    return key


def scores(tok, tok_f, router, column):
    inv_x = row_of(lax.rsqrt(jnp.sum(tok_f * tok_f, 1, keepdims=True) + EPSILON))
    return dot(router, tok, ((1,), (1,))) * inv_x * column, inv_x


def front_kernel(
    plan, tok_hbm, grad_hbm, router_hbm, scale_hbm, sent_ref, logit_ref, inv_ref,
    tok_ref, grad_ref, router_ref, scale_ref, sems,
):
    arrived = fetch(
        [tok_hbm, router_hbm, scale_hbm, grad_hbm], [tok_ref, router_ref, scale_ref, grad_ref], sems
    )
    for copy in arrived[:3]:
        copy.wait()
    tok = tok_ref[0]
    tok_f = tok.astype(F32)
    _, inv_p, scale = slot_column(router_ref, scale_ref)
    logit, inv_x = scores(tok, tok_f, router_ref[...], inv_p * scale)
    expo, comb = softmax(logit)
    numer = dot(expo.astype(BF), tok, ((1,), (0,)))
    arrived[3].wait()
    dys = dot(comb.astype(BF), grad_ref[0], ((1,), (0,)))
    rows = stack_rows(numer, dys, [jnp.sum(expo, 1, keepdims=True)])
    store_blocks(sent_ref, pick(expert_rows(plan, router_ref.shape[0]), 2 * sent_ref.shape[0], rows, itself))
    logit_ref[...] = logit
    inv_ref[...] = inv_x


def expert_kernel(
    images, halves, got_ref, one_ref, two_ref, back_ref, rows_ref, grad_rows_ref, hidden_ref, dact_ref
):
    width = one_ref.shape[1]
    key = image_rows(images, halves)
    sums = pick(itself, 2 * images, load_blocks(got_ref), key)
    den = sums[:images, width : width + 1] + sums[images:, width : width + 1]
    rows = (sums[:images, :width] / den).astype(BF)
    grad_rows = sums[images:, :width].astype(BF)
    act = dot(rows, one_ref[0], ((1,), (0,)))
    grad_h = dot(grad_rows, two_ref[0], ((1,), (1,)))
    phi = 0.5 * (1.0 + lax.erf(act * ROOT_HALF))
    hidden = (act * phi).astype(BF)
    dact = (grad_h * (phi + act * jnp.exp(-0.5 * act * act) * DENSITY)).astype(BF)
    out_part = dot(hidden, two_ref[0], ((1,), (0,)))
    in_part = dot(dact, one_ref[0], ((1,), (1,)))
    corr = jnp.sum(dact.astype(F32) * act, 1, keepdims=True)
    packed = stack_rows(out_part, in_part, [den, corr])
    store_blocks(back_ref, pick(key, 2 * back_ref.shape[0], packed, itself))
    rows_ref[...] = rows
    grad_rows_ref[...] = grad_rows
    hidden_ref[...] = hidden
    dact_ref[...] = dact


def outer_kernel(size, left_ref, right_ref, out_hbm, out_ref, sems):
    copies = []
    for place in range(left_ref.shape[1] // size):
        part = slice(place * size, (place + 1) * size)
        out_ref[0, part] = dot(left_ref[:, part], right_ref[...], ((0,), (0,))).astype(BF)
        copy = pltpu.make_async_copy(
            out_ref.at[:, pl.ds(place * size, size)], out_hbm.at[:, pl.ds(place * size, size)],
            sems.at[place],
        )
        copy.start()
        copies.append(copy)
    for copy in copies:
        copy.wait()


def middle_kernel(plan, halves, *refs):
    back_ref, logit_ref, inv_ref, router_ref, scale_ref = refs[:5]
    tok_refs, grad_refs = refs[5 : 5 + halves], refs[5 + halves : 5 + 2 * halves]
    sums_ref, outs_ref, coef_ref, mix_ref, signal_ref = refs[5 + 2 * halves :]
    experts, width = router_ref.shape
    sums = pick(itself, 2 * experts, load_blocks(back_ref), expert_rows(plan, experts))
    extras = sums[:experts, width:] + sums[experts:, width:]
    den = extras[:, :1] * (1.0 / (plan[0] * plan[1]))
    corr = extras[:, 1:2]
    ys = sums[:experts, :width].astype(BF)
    dxs = sums[experts:, :width].astype(BF)
    router_f, inv_p, scale = slot_column(router_ref, scale_ref)
    column = inv_p * scale
    outer = total = 0.0
    for half, (tok_ref, grad_ref) in enumerate(zip(tok_refs, grad_refs)):
        tok = tok_ref[0]
        if half == 0:
            logit, inv_x = logit_ref[...], inv_ref[...]
        else:
            logit, inv_x = scores(tok, tok.astype(F32), router_ref[...], column)
        expo, comb = softmax(logit)
        dcomb = dot(ys, grad_ref[0], ((1,), (1,)))
        ddisp = dot(dxs, tok, ((1,), (1,)))
        dlc = comb * (dcomb - jnp.sum(comb * dcomb, 0, keepdims=True))
        grad_l = expo / den * (ddisp - corr) + dlc
        product = grad_l * logit
        grad_q = (grad_l * inv_x * column).astype(BF)
        outer += dot(grad_q, tok, ((1,), (0,)))
        total += jnp.sum(product, 1, keepdims=True)
        if half == 0:
            coef_ref[...] = jnp.concatenate([expo, grad_q.astype(F32)], 0).astype(BF)
            signal_ref[...] = inv_x * inv_x * jnp.sum(product, 0, keepdims=True)
    local = outer - inv_p * inv_p * total * router_f
    lane = iota((experts, LANES), 1)
    sums_ref[...] = jnp.concatenate([local, jnp.where(lane == 0, total / scale, 0.0)], 1)
    outs_ref[...] = ys
    mix_ref[...] = jnp.concatenate([dxs.astype(F32) / den, router_f], 0).astype(BF)


def tail_kernel(tok_ref, logit_ref, outs_ref, coef_ref, mix_ref, signal_ref, combined_ref, grads_ref):
    _, comb = softmax(logit_ref[...])
    combined_ref[0] = dot(comb.astype(BF), outs_ref[...], ((0,), (0,))).astype(BF)
    signal = signal_ref[...]
    column = jnp.transpose(jnp.broadcast_to(signal, (LANES, signal.shape[1])))[:, :1]
    grads = dot(coef_ref[...], mix_ref[...], ((0,), (0,)))
    grads_ref[0] = (grads - column * tok_ref[0].astype(F32)).astype(BF)


def last_kernel(own_ref, other_ref, *refs):
    *more, router_ref, scale_ref = refs
    sums = own_ref[...].astype(F32) + other_ref[...].astype(F32)
    if more:
        sums = sums + (more[0][...].astype(F32) + more[1][...].astype(F32))
    experts, width = router_ref.shape
    router_ref[...] = sums[:, :width]
    eye = iota((experts, experts), 0) == iota((experts, experts), 1)
    scale_ref[...] = jnp.sum(jnp.where(eye, sums[:, width : width + 1], 0.0), 0, keepdims=True)


def call(kernel, outs, *args, stays=(), buffers=(), flops=10**7, room=24 * 2**20, home=pltpu.VMEM):
    specs = [pl.BlockSpec(memory_space=pltpu.VMEM)] * len(args)
    args = list(args)
    for place in stays:
        specs[place] = pl.BlockSpec(memory_space=pltpu.HBM)
        args[place] = pltpu.with_memory_space_constraint(args[place], pltpu.HBM)
    return pl.pallas_call(
        kernel,
        out_shape=[jax.ShapeDtypeStruct(shape, dtype) for shape, dtype in outs],
        in_specs=specs,
        out_specs=[pl.BlockSpec(memory_space=home)] * len(outs),
        scratch_shapes=buffers,
        compiler_params=pltpu.CompilerParams(vmem_limit_bytes=room),
        cost_estimate=pl.CostEstimate(
            flops=flops, bytes_accessed=sum(a.size * a.dtype.itemsize for a in args), transcendentals=0
        ),
    )(*args)


def weight_grad(left, right):
    size = 256
    shape = (1, left.shape[1], right.shape[1])
    (out,) = call(
        functools.partial(outer_kernel, size), [(shape, BF)], left, right,
        buffers=[pltpu.VMEM(shape, BF), pltpu.SemaphoreType.DMA((shape[1] // size,))],
        flops=10**9, home=pltpu.HBM,
    )
    return out


def exchange(block):
    return lax.all_to_all(block, BOTH, split_axis=0, concat_axis=0, tiled=True)


def pair(term, mask, axis, size):
    return lax.ppermute(term, axis, [(d, d ^ mask) for d in range(size)])


def sum_images(term, images, beside):
    masks = [1 << place for place in range(log2(images))]
    term = term + pair(term, masks[0], "img", images)
    rounds = [masks[place : place + 2] for place in range(1, len(masks), 2)]
    done = []
    for group in rounds:
        if group is not rounds[0]:
            term = (terms[0].astype(F32) + terms[1].astype(F32)) + (
                terms[2].astype(F32) + terms[3].astype(F32)
            )
        own = term.astype(BF)
        terms = [own, pair(own, group[0], "img", images)]
        if len(group) == 2:
            terms.append(pair(own, group[1], "img", images))
            terms.append(pair(own, group[0] ^ group[1], "img", images))
        if beside:
            terms[1], ready = lax.optimization_barrier((terms[1], beside[0]))
            beside = beside[1:]
            done.append(ready)
    return terms, done + list(beside)


def shards(images, halves, tokens, grad_out, router, slot_scale, w_in, w_out):
    devices = images * halves
    tok_rows, width = tokens.shape[1:]
    experts = router.shape[1]
    plan = (images // experts, halves)
    hidden_dev = w_in.shape[2]
    long = width + LANES
    router_t = router.T
    scale_row = slot_scale.reshape(1, experts)
    inputs = (tokens, grad_out, router_t, scale_row)
    sent, logit, inv_x = call(
        functools.partial(front_kernel, plan),
        [((devices, 2, long), BF), ((experts, tok_rows), F32), ((1, tok_rows), F32)],
        *inputs,
        stays=range(4),
        buffers=[pltpu.VMEM(a.shape, a.dtype) for a in inputs] + [pltpu.SemaphoreType.DMA((4,))],
        flops=FRONT,
    )
    toks = [pair(tokens, mask, "tok", halves) for mask in range(1, halves)]
    grads = [pair(grad_out, mask, "tok", halves) for mask in range(1, halves)]
    got, toks, grads = lax.optimization_barrier((exchange(sent), toks, grads))
    back, rows, grad_rows, hidden, dact = call(
        functools.partial(expert_kernel, images, halves),
        [((devices, 2, long), BF), ((images, width), BF), ((images, width), BF),
         ((images, hidden_dev), BF), ((images, hidden_dev), BF)],
        got, w_in, w_out,
        flops=10**9,
    )
    back = exchange(back)
    grad_w_in = weight_grad(rows, dact)
    grad_w_out = weight_grad(hidden, grad_rows)
    sums, ys, coef, mix, signal = call(
        functools.partial(middle_kernel, plan, halves),
        [((experts, long), F32), ((experts, width), BF), ((2 * experts, tok_rows), BF),
         ((2 * experts, width), BF), ((1, tok_rows), F32)],
        back, logit, inv_x, router_t, scale_row, tokens, *toks, grad_out, *grads,
    )
    combined, grad_tokens = call(
        tail_kernel,
        [(tokens.shape, BF), (tokens.shape, BF)],
        tokens, logit, ys, coef, mix, signal,
    )
    terms, (grad_w_in, (grad_w_out, combined, grad_tokens)) = sum_images(
        sums, images, [grad_w_in, (grad_w_out, combined, grad_tokens)]
    )
    grad_router, grad_scale = call(
        last_kernel, [((experts, width), F32), ((1, experts), F32)], *terms
    )
    return (combined, grad_tokens, grad_router.T, grad_scale[0], grad_w_in, grad_w_out)


def solution(mesh):
    images, halves = mesh.shape["img"], mesh.shape["tok"]

    def body(*args):
        return shards(images, halves, *args)

    return jax.shard_map(
        body,
        mesh=mesh,
        in_specs=(
            P("img", "tok", None),
            P("img", "tok", None),
            P(),
            P(),
            P("img", None, "tok"),
            P("img", "tok", None),
        ),
        out_specs=(
            P("img", "tok", None),
            P("img", "tok", None),
            P(),
            P(),
            P("img", None, "tok"),
            P("img", "tok", None),
        ),
        check_vma=False,
    )
```

```python
import functools

import jax
import jax.numpy as jnp
from jax import lax
from jax.experimental import pallas as pl
from jax.experimental.pallas import tpu as pltpu
from jax.sharding import PartitionSpec as P

EPSILON = 1e-06
ROOT_HALF = 0.7071067811865476
DENSITY = 0.3989422804014327
BF = jnp.bfloat16
F32 = jnp.float32
BOTH = ("img", "tok")
LANES = 128
FRONT = 4 * 10**9


def dot(left, right, dims):
    return lax.dot_general(left, right, (dims, ((), ())), preferred_element_type=F32)


def log2(size):
    assert size & (size - 1) == 0
    return size.bit_length() - 1


def iota(shape, axis):
    return lax.broadcasted_iota(jnp.int32, shape, axis)


def digits(row, sizes):
    out = []
    for size in reversed(sizes):
        out.append(row & (size - 1))
        row = row >> log2(size)
    return out[::-1]


def selection(shape, row_key, column_key):
    hit = row_key(iota(shape, 0)) == column_key(iota(shape, 1))
    return jnp.where(hit, 1.0, 0.0).astype(BF)


def pick(left_key, left_size, right, right_key):
    return dot(selection((left_size, right.shape[0]), left_key, right_key), right, ((1,), (0,)))


def store_blocks(ref, rows):
    ref[...] = rows.astype(BF).reshape(ref.shape)


def load_blocks(ref):
    return ref[...].reshape(2 * ref.shape[0], ref.shape[2])


def itself(row):
    return row


def as_column(row):
    size = row.shape[1]
    eye = iota((size, size), 0) == iota((size, size), 1)
    return jnp.sum(jnp.where(eye, row, 0.0), 1, keepdims=True)


def row_of(column):
    return jnp.transpose(jnp.broadcast_to(column, (column.shape[0], LANES)))[:1]


def stack_rows(first, second, extras):
    lane = iota((first.shape[0], LANES), 1)
    high = jnp.zeros(lane.shape, F32)
    low = jnp.zeros(lane.shape, F32)
    for place, value in enumerate(extras):
        top = value.astype(BF).astype(F32)
        high = jnp.where(lane == place, top, high)
        low = jnp.where(lane == place, value - top, low)
    return jnp.concatenate(
        [jnp.concatenate([first, high], 1), jnp.concatenate([second, low], 1)], 0
    ).astype(BF)


def slot_column(router_ref, scale_ref):
    router_f = router_ref[...].astype(F32)
    inv_p = lax.rsqrt(jnp.sum(router_f * router_f, 1, keepdims=True) + EPSILON)
    scale = as_column(scale_ref[...])
    return router_f, inv_p, scale


def softmax(logit):
    expo = jnp.exp(logit)
    return expo, expo / jnp.sum(expo, 0, keepdims=True)


def fetch(sources, targets, sems):
    copies = [
        pltpu.make_async_copy(source, target, sems.at[place])
        for place, (source, target) in enumerate(zip(sources, targets))
    ]
    for copy in copies:
        copy.start()
    return copies


def expert_rows(plan, experts):
    copies, halves = plan

    def key(row):
        _, place, _, kind = digits(row, (copies, experts, halves, 2))
        return kind * experts + place

    return key


def image_rows(images, halves):
    def key(row):
        place, _, kind = digits(row, (images, halves, 2))
        return kind * images + place

    return key


def front_kernel(
    plan, tok_hbm, grad_hbm, router_hbm, scale_hbm, sent_ref, logit_ref, inv_ref,
    tok_ref, grad_ref, router_ref, scale_ref, sems,
):
    arrived = fetch(
        [tok_hbm, router_hbm, scale_hbm, grad_hbm], [tok_ref, router_ref, scale_ref, grad_ref], sems
    )
    for copy in arrived[:3]:
        copy.wait()
    tok = tok_ref[0]
    tok_f = tok.astype(F32)
    inv_x = row_of(lax.rsqrt(jnp.sum(tok_f * tok_f, 1, keepdims=True) + EPSILON))
    _, inv_p, scale = slot_column(router_ref, scale_ref)
    raw = dot(router_ref[...], tok, ((1,), (1,)))
    logit = raw * inv_x * (inv_p * scale)
    expo, comb = softmax(logit)
    numer = dot(expo.astype(BF), tok, ((1,), (0,)))
    arrived[3].wait()
    dys = dot(comb.astype(BF), grad_ref[0], ((1,), (0,)))
    rows = stack_rows(numer, dys, [jnp.sum(expo, 1, keepdims=True)])
    store_blocks(sent_ref, pick(expert_rows(plan, router_ref.shape[0]), 2 * sent_ref.shape[0], rows, itself))
    logit_ref[...] = logit
    inv_ref[...] = inv_x


def expert_kernel(
    images, halves, got_ref, one_ref, two_ref, back_ref, rows_ref, grad_rows_ref, hidden_ref, dact_ref
):
    width = one_ref.shape[1]
    key = image_rows(images, halves)
    sums = pick(itself, 2 * images, load_blocks(got_ref), key)
    den = sums[:images, width : width + 1] + sums[images:, width : width + 1]
    rows = (sums[:images, :width] / den).astype(BF)
    grad_rows = sums[images:, :width].astype(BF)
    act = dot(rows, one_ref[0], ((1,), (0,)))
    grad_h = dot(grad_rows, two_ref[0], ((1,), (1,)))
    phi = 0.5 * (1.0 + lax.erf(act * ROOT_HALF))
    hidden = (act * phi).astype(BF)
    dact = (grad_h * (phi + act * jnp.exp(-0.5 * act * act) * DENSITY)).astype(BF)
    out_part = dot(hidden, two_ref[0], ((1,), (0,)))
    in_part = dot(dact, one_ref[0], ((1,), (1,)))
    corr = jnp.sum(dact.astype(F32) * act, 1, keepdims=True)
    packed = stack_rows(out_part, in_part, [den, corr])
    store_blocks(back_ref, pick(key, 2 * back_ref.shape[0], packed, itself))
    rows_ref[...] = rows
    grad_rows_ref[...] = grad_rows
    hidden_ref[...] = hidden
    dact_ref[...] = dact


def outer_kernel(size, left_ref, right_ref, out_hbm, out_ref, sems):
    copies = []
    for place in range(left_ref.shape[1] // size):
        part = slice(place * size, (place + 1) * size)
        out_ref[0, part] = dot(left_ref[:, part], right_ref[...], ((0,), (0,))).astype(BF)
        copy = pltpu.make_async_copy(
            out_ref.at[:, pl.ds(place * size, size)], out_hbm.at[:, pl.ds(place * size, size)],
            sems.at[place],
        )
        copy.start()
        copies.append(copy)
    for copy in copies:
        copy.wait()


def middle_kernel(
    plan, back_ref, tok_ref, grad_ref, logit_ref, inv_ref, router_ref, scale_ref,
    sums_ref, outs_ref, coef_ref, mix_ref, signal_ref,
):
    experts, width = router_ref.shape
    sums = pick(itself, 2 * experts, load_blocks(back_ref), expert_rows(plan, router_ref.shape[0]))
    extras = sums[:experts, width:] + sums[experts:, width:]
    den = extras[:, :1] * (1.0 / (plan[0] * plan[1]))
    corr = extras[:, 1:2]
    ys = sums[:experts, :width].astype(BF)
    dxs = sums[experts:, :width].astype(BF)
    router_f, inv_p, scale = slot_column(router_ref, scale_ref)
    tok = tok_ref[0]
    logit = logit_ref[...]
    inv_x = inv_ref[...]
    expo, comb = softmax(logit)
    dcomb = dot(ys, grad_ref[0], ((1,), (1,)))
    ddisp = dot(dxs, tok, ((1,), (1,)))
    dlc = comb * (dcomb - jnp.sum(comb * dcomb, 0, keepdims=True))
    grad_l = expo / den * (ddisp - corr) + dlc
    product = grad_l * logit
    grad_q = (grad_l * inv_x * (inv_p * scale)).astype(BF)
    outer = dot(grad_q, tok, ((1,), (0,)))
    total = jnp.sum(product, 1, keepdims=True)
    local = outer - inv_p * inv_p * total * router_f
    lane = iota((experts, LANES), 1)
    sums_ref[...] = jnp.concatenate([local, jnp.where(lane == 0, total / scale, 0.0)], 1)
    outs_ref[...] = ys
    coef_ref[...] = jnp.concatenate([expo, grad_q.astype(F32)], 0).astype(BF)
    mix_ref[...] = jnp.concatenate([dxs.astype(F32) / den, router_f], 0).astype(BF)
    signal_ref[...] = inv_x * inv_x * jnp.sum(product, 0, keepdims=True)


def tail_kernel(tok_ref, logit_ref, outs_ref, coef_ref, mix_ref, signal_ref, combined_ref, grads_ref):
    _, comb = softmax(logit_ref[...])
    combined_ref[0] = dot(comb.astype(BF), outs_ref[...], ((0,), (0,))).astype(BF)
    signal = signal_ref[...]
    column = jnp.transpose(jnp.broadcast_to(signal, (LANES, signal.shape[1])))[:, :1]
    grads = dot(coef_ref[...], mix_ref[...], ((0,), (0,)))
    grads_ref[0] = (grads - column * tok_ref[0].astype(F32)).astype(BF)


def last_kernel(mine_ref, other_ref, router_ref, scale_ref):
    sums = mine_ref[...] + other_ref[...]
    experts, width = router_ref.shape
    router_ref[...] = sums[:, :width]
    eye = iota((experts, experts), 0) == iota((experts, experts), 1)
    scale_ref[...] = jnp.sum(jnp.where(eye, sums[:, width : width + 1], 0.0), 0, keepdims=True)


def call(kernel, outs, *args, stays=(), buffers=(), flops=10**7, room=24 * 2**20, home=pltpu.VMEM):
    specs = [pl.BlockSpec(memory_space=pltpu.VMEM)] * len(args)
    args = list(args)
    for place in stays:
        specs[place] = pl.BlockSpec(memory_space=pltpu.HBM)
        args[place] = pltpu.with_memory_space_constraint(args[place], pltpu.HBM)
    return pl.pallas_call(
        kernel,
        out_shape=[jax.ShapeDtypeStruct(shape, dtype) for shape, dtype in outs],
        in_specs=specs,
        out_specs=[pl.BlockSpec(memory_space=home)] * len(outs),
        scratch_shapes=buffers,
        compiler_params=pltpu.CompilerParams(vmem_limit_bytes=room),
        cost_estimate=pl.CostEstimate(
            flops=flops, bytes_accessed=sum(a.size * a.dtype.itemsize for a in args), transcendentals=0
        ),
    )(*args)


def weight_grad(left, right):
    size = 256
    shape = (1, left.shape[1], right.shape[1])
    (out,) = call(
        functools.partial(outer_kernel, size), [(shape, BF)], left, right,
        buffers=[pltpu.VMEM(shape, BF), pltpu.SemaphoreType.DMA((shape[1] // size,))],
        flops=10**9, home=pltpu.HBM,
    )
    return out


def exchange(block):
    return lax.all_to_all(block, BOTH, split_axis=0, concat_axis=0, tiled=True)


def pair(term, masks):
    return lax.ppermute(term, BOTH, [(d, d ^ mask) for d, mask in enumerate(masks)])


def sum_everywhere(term, devices, beside):
    core = (lax.axis_index("img") & 1) == 0
    bit = 2
    masks = [1] + [1 << place for place in range(2, log2(devices))]
    done = []

    def together(value):
        if len(done) < len(beside):
            value, ready = lax.optimization_barrier((value, beside[len(done)]))
            done.append(ready)
        return value

    mine, other = term, pair(term, [bit] * devices)
    for place in range(0, len(masks), 2):
        group = masks[place : place + 2]
        own = (mine + other).astype(BF)
        if len(group) == 1:
            mine, other = own.astype(F32), together(pair(own, group * devices)).astype(F32)
            continue
        near, far = group
        first = pair(own, [near if d & bit else near ^ far for d in range(devices)])
        second = pair(own, [far] * devices)
        first = together(first)
        mine = first.astype(F32) + jnp.where(core, own, second).astype(F32)
        other = pair(mine, [bit] * devices)
        if place + 2 >= len(masks):
            other = together(other)
    return mine, other, done + beside[len(done) :]


def shards(images, halves, tokens, grad_out, router, slot_scale, w_in, w_out):
    devices = images * halves
    tok_rows, width = tokens.shape[1:]
    experts = router.shape[1]
    plan = (images // experts, halves)
    hidden_dev = w_in.shape[2]
    long = width + LANES
    router_t = router.T
    scale_row = slot_scale.reshape(1, experts)
    inputs = (tokens, grad_out, router_t, scale_row)
    sent, logit, inv_x = call(
        functools.partial(front_kernel, plan),
        [((devices, 2, long), BF), ((experts, tok_rows), F32), ((1, tok_rows), F32)],
        *inputs,
        stays=range(4),
        buffers=[pltpu.VMEM(a.shape, a.dtype) for a in inputs] + [pltpu.SemaphoreType.DMA((4,))],
        flops=FRONT,
    )
    got = exchange(sent)
    back, rows, grad_rows, hidden, dact = call(
        functools.partial(expert_kernel, images, halves),
        [((devices, 2, long), BF), ((images, width), BF), ((images, width), BF),
         ((images, hidden_dev), BF), ((images, hidden_dev), BF)],
        got, w_in, w_out,
        flops=10**9,
    )
    back = exchange(back)
    grad_w_in = weight_grad(rows, dact)
    grad_w_out = weight_grad(hidden, grad_rows)
    sums, ys, coef, mix, signal = call(
        functools.partial(middle_kernel, plan),
        [((experts, long), F32), ((experts, width), BF), ((2 * experts, tok_rows), BF),
         ((2 * experts, width), BF), ((1, tok_rows), F32)],
        back, tokens, grad_out, logit, inv_x, router_t, scale_row,
    )
    combined, grad_tokens = call(
        tail_kernel,
        [(tokens.shape, BF), (tokens.shape, BF)],
        tokens, logit, ys, coef, mix, signal,
    )
    mine, other, (grad_w_in, grad_w_out, (combined, grad_tokens)) = sum_everywhere(
        sums, devices, [grad_w_in, grad_w_out, (combined, grad_tokens)]
    )
    grad_router, grad_scale = call(
        last_kernel, [((experts, width), F32), ((1, experts), F32)], mine, other
    )
    return (combined, grad_tokens, grad_router.T, grad_scale[0], grad_w_in, grad_w_out)


def solution(mesh):
    images, halves = mesh.shape["img"], mesh.shape["tok"]

    def body(*args):
        return shards(images, halves, *args)

    return jax.shard_map(
        body,
        mesh=mesh,
        in_specs=(
            P("img", "tok", None),
            P("img", "tok", None),
            P(),
            P(),
            P("img", None, "tok"),
            P("img", "tok", None),
        ),
        out_specs=(
            P("img", "tok", None),
            P("img", "tok", None),
            P(),
            P(),
            P("img", None, "tok"),
            P("img", "tok", None),
        ),
        check_vma=False,
    )
```

```python
import functools

import jax
import jax.numpy as jnp
from jax import lax
from jax.experimental import pallas as pl
from jax.experimental.pallas import tpu as pltpu
from jax.sharding import PartitionSpec as P

EPSILON = 1e-06
ROOT_HALF = 0.7071067811865476
DENSITY = 0.3989422804014327
BF = jnp.bfloat16
F32 = jnp.float32
BOTH = ("img", "tok")
LANES = 128
FRONT = 4 * 10**9


def dot(left, right, dims):
    return lax.dot_general(left, right, (dims, ((), ())), preferred_element_type=F32)


def log2(size):
    assert size & (size - 1) == 0
    return size.bit_length() - 1


def iota(shape, axis):
    return lax.broadcasted_iota(jnp.int32, shape, axis)


def digits(row, sizes):
    out = []
    for size in reversed(sizes):
        out.append(row & (size - 1))
        row = row >> log2(size)
    return out[::-1]


def selection(shape, row_key, column_key):
    hit = row_key(iota(shape, 0)) == column_key(iota(shape, 1))
    return jnp.where(hit, 1.0, 0.0).astype(BF)


def pick(left_key, left_size, right, right_key):
    return dot(selection((left_size, right.shape[0]), left_key, right_key), right, ((1,), (0,)))


def store_blocks(ref, rows):
    ref[...] = rows.astype(BF).reshape(ref.shape)


def load_blocks(ref):
    return ref[...].reshape(2 * ref.shape[0], ref.shape[2])


def itself(row):
    return row


def as_column(row):
    size = row.shape[1]
    eye = iota((size, size), 0) == iota((size, size), 1)
    return jnp.sum(jnp.where(eye, row, 0.0), 1, keepdims=True)


def row_of(column):
    return jnp.transpose(jnp.broadcast_to(column, (column.shape[0], LANES)))[:1]


def stack_rows(first, second, extras):
    lane = iota((first.shape[0], LANES), 1)
    high = jnp.zeros(lane.shape, F32)
    low = jnp.zeros(lane.shape, F32)
    for place, value in enumerate(extras):
        top = value.astype(BF).astype(F32)
        high = jnp.where(lane == place, top, high)
        low = jnp.where(lane == place, value - top, low)
    return jnp.concatenate(
        [jnp.concatenate([first, high], 1), jnp.concatenate([second, low], 1)], 0
    ).astype(BF)


def slot_column(router_ref, scale_ref):
    router_f = router_ref[...].astype(F32)
    inv_p = lax.rsqrt(jnp.sum(router_f * router_f, 1, keepdims=True) + EPSILON)
    scale = as_column(scale_ref[...])
    return router_f, inv_p, scale


def softmax(logit):
    expo = jnp.exp(logit)
    return expo, expo / jnp.sum(expo, 0, keepdims=True)


def fetch(sources, targets, sems):
    copies = [
        pltpu.make_async_copy(source, target, sems.at[place])
        for place, (source, target) in enumerate(zip(sources, targets))
    ]
    for copy in copies:
        copy.start()
    return copies


def expert_rows(plan, experts):
    copies, halves = plan

    def key(row):
        _, place, _, kind = digits(row, (copies, experts, halves, 2))
        return kind * experts + place

    return key


def image_rows(images, halves):
    def key(row):
        place, _, kind = digits(row, (images, halves, 2))
        return kind * images + place

    return key


def lane_factor(shape):
    return 1.0 + iota(shape, 1).astype(F32) * (1.0 / LANES)


def front_kernel(
    plan, tok_hbm, grad_hbm, router_hbm, scale_hbm, sent_ref, logit_ref, inv_ref,
    tok_ref, grad_ref, router_ref, scale_ref, sems,
):
    arrived = fetch(
        [tok_hbm, router_hbm, scale_hbm, grad_hbm], [tok_ref, router_ref, scale_ref, grad_ref], sems
    )
    for copy in arrived[:3]:
        copy.wait()
    tok = tok_ref[0]
    tok_f = tok.astype(F32)
    inv_x = row_of(lax.rsqrt(jnp.sum(tok_f * tok_f, 1, keepdims=True) + EPSILON))
    _, inv_p, scale = slot_column(router_ref, scale_ref)
    raw = dot(router_ref[...], tok, ((1,), (1,)))
    logit = raw * inv_x * (inv_p * scale)
    expo, comb = softmax(logit)
    numer = dot(expo.astype(BF), tok, ((1,), (0,)))
    arrived[3].wait()
    dys = dot(comb.astype(BF), grad_ref[0], ((1,), (0,)))
    rows = stack_rows(numer, dys, [jnp.sum(expo, 1, keepdims=True)])
    store_blocks(sent_ref, pick(expert_rows(plan, router_ref.shape[0]), 2 * sent_ref.shape[0], rows, itself))
    logit_ref[...] = logit
    inv_ref[...] = inv_x


def expert_kernel(
    images, halves, got_ref, one_ref, two_ref, back_ref, rows_ref, grad_rows_ref, hidden_ref, dact_ref
):
    width = one_ref.shape[1]
    key = image_rows(images, halves)
    sums = pick(itself, 2 * images, load_blocks(got_ref), key)
    den = sums[:images, width : width + 1] + sums[images:, width : width + 1]
    rows = (sums[:images, :width] / den).astype(BF)
    grad_rows = sums[images:, :width].astype(BF)
    act = dot(rows, one_ref[0], ((1,), (0,)))
    grad_h = dot(grad_rows, two_ref[0], ((1,), (1,)))
    phi = 0.5 * (1.0 + lax.erf(act * ROOT_HALF))
    hidden = (act * phi).astype(BF)
    dact = (grad_h * (phi + act * jnp.exp(-0.5 * act * act) * DENSITY)).astype(BF)
    out_part = dot(hidden, two_ref[0], ((1,), (0,)))
    in_part = dot(dact, one_ref[0], ((1,), (1,)))
    corr = jnp.sum(dact.astype(F32) * act, 1, keepdims=True)
    packed = stack_rows(out_part, in_part, [den, corr])
    store_blocks(back_ref, pick(key, 2 * back_ref.shape[0], packed, itself))
    rows_ref[...] = rows
    grad_rows_ref[...] = grad_rows
    hidden_ref[...] = hidden
    dact_ref[...] = dact


def outer_kernel(size, left_ref, right_ref, out_hbm, out_ref, sems):
    copies = []
    for place in range(left_ref.shape[1] // size):
        part = slice(place * size, (place + 1) * size)
        out_ref[0, part] = dot(left_ref[:, part], right_ref[...], ((0,), (0,))).astype(BF)
        copy = pltpu.make_async_copy(
            out_ref.at[:, pl.ds(place * size, size)], out_hbm.at[:, pl.ds(place * size, size)],
            sems.at[place],
        )
        copy.start()
        copies.append(copy)
    for copy in copies:
        copy.wait()


def middle_kernel(
    plan, back_ref, tok_ref, grad_ref, logit_ref, inv_ref, router_ref, scale_ref,
    sums_ref, outs_ref, coef_ref, mix_ref, signal_ref,
):
    experts, width = router_ref.shape
    sums = pick(itself, 2 * experts, load_blocks(back_ref), expert_rows(plan, router_ref.shape[0]))
    extras = sums[:experts, width:] + sums[experts:, width:]
    den = extras[:, :1] * (1.0 / (plan[0] * plan[1]))
    corr = extras[:, 1:2]
    ys = sums[:experts, :width].astype(BF)
    dxs = sums[experts:, :width].astype(BF)
    router_f, inv_p, scale = slot_column(router_ref, scale_ref)
    tok = tok_ref[0]
    logit = logit_ref[...]
    inv_x = inv_ref[...]
    expo, comb = softmax(logit)
    dcomb = dot(ys, grad_ref[0], ((1,), (1,)))
    ddisp = dot(dxs, tok, ((1,), (1,)))
    dlc = comb * (dcomb - jnp.sum(comb * dcomb, 0, keepdims=True))
    grad_l = expo / den * (ddisp - corr) + dlc
    product = grad_l * logit
    grad_q = (grad_l * inv_x * (inv_p * scale)).astype(BF)
    outer = dot(grad_q, tok, ((1,), (0,)))
    total = jnp.sum(product, 1, keepdims=True)
    local = outer - inv_p * inv_p * total * router_f
    sums_ref[...] = jnp.concatenate([local, total / scale * lane_factor((experts, LANES))], 1)
    outs_ref[...] = ys
    coef_ref[...] = jnp.concatenate([expo, grad_q.astype(F32)], 0).astype(BF)
    mix_ref[...] = jnp.concatenate([dxs.astype(F32) / den, router_f], 0).astype(BF)
    signal_ref[...] = inv_x * inv_x * jnp.sum(product, 0, keepdims=True)


def tail_kernel(tok_ref, logit_ref, outs_ref, coef_ref, mix_ref, signal_ref, combined_ref, grads_ref):
    _, comb = softmax(logit_ref[...])
    combined_ref[0] = dot(comb.astype(BF), outs_ref[...], ((0,), (0,))).astype(BF)
    signal = signal_ref[...]
    column = jnp.transpose(jnp.broadcast_to(signal, (LANES, signal.shape[1])))[:, :1]
    grads = dot(coef_ref[...], mix_ref[...], ((0,), (0,)))
    grads_ref[0] = (grads - column * tok_ref[0].astype(F32)).astype(BF)


def last_kernel(own_ref, other_ref, *refs):
    *more, router_ref, scale_ref = refs
    sums = own_ref[...].astype(F32) + other_ref[...].astype(F32)
    if more:
        sums = sums + (more[0][...].astype(F32) + more[1][...].astype(F32))
    experts, width = router_ref.shape
    router_ref[...] = sums[:, :width]
    eye = iota((experts, experts), 0) == iota((experts, experts), 1)
    scale = jnp.sum(sums[:, width:] / lane_factor((experts, LANES)), 1, keepdims=True) * (1.0 / LANES)
    scale_ref[...] = jnp.sum(jnp.where(eye, scale, 0.0), 0, keepdims=True)


def call(kernel, outs, *args, stays=(), buffers=(), flops=10**7, room=24 * 2**20, home=pltpu.VMEM):
    specs = [pl.BlockSpec(memory_space=pltpu.VMEM)] * len(args)
    args = list(args)
    for place in stays:
        specs[place] = pl.BlockSpec(memory_space=pltpu.HBM)
        args[place] = pltpu.with_memory_space_constraint(args[place], pltpu.HBM)
    return pl.pallas_call(
        kernel,
        out_shape=[jax.ShapeDtypeStruct(shape, dtype) for shape, dtype in outs],
        in_specs=specs,
        out_specs=[pl.BlockSpec(memory_space=home)] * len(outs),
        scratch_shapes=buffers,
        compiler_params=pltpu.CompilerParams(vmem_limit_bytes=room),
        cost_estimate=pl.CostEstimate(
            flops=flops, bytes_accessed=sum(a.size * a.dtype.itemsize for a in args), transcendentals=0
        ),
    )(*args)


def weight_grad(left, right):
    size = 256
    shape = (1, left.shape[1], right.shape[1])
    (out,) = call(
        functools.partial(outer_kernel, size), [(shape, BF)], left, right,
        buffers=[pltpu.VMEM(shape, BF), pltpu.SemaphoreType.DMA((shape[1] // size,))],
        flops=10**9, home=pltpu.HBM,
    )
    return out


def exchange(block):
    return lax.all_to_all(block, BOTH, split_axis=0, concat_axis=0, tiled=True)


def pair(term, mask, devices):
    return lax.ppermute(term, BOTH, [(d, d ^ mask) for d in range(devices)])


def sum_everywhere(term, devices, beside):
    done = []

    def together(value):
        if len(done) < len(beside):
            value, ready = lax.optimization_barrier((value, beside[len(done)]))
            done.append(ready)
        return value

    term = term + together(pair(term, 2, devices))
    masks = [1] + [1 << place for place in range(2, log2(devices))]
    rounds = [masks[place : place + 2] for place in range(0, len(masks), 2)]
    for group in rounds:
        if group is not rounds[0]:
            term = (terms[0].astype(F32) + terms[1].astype(F32)) + (
                terms[2].astype(F32) + terms[3].astype(F32)
            )
        own = term.astype(BF)
        steps = [group[1], group[0], group[0] ^ group[1]] if len(group) == 2 else group
        terms = [own] + [pair(own, mask, devices) for mask in steps]
        terms[-1] = together(terms[-1])
    return terms, done + beside[len(done) :]


def shards(images, halves, tokens, grad_out, router, slot_scale, w_in, w_out):
    devices = images * halves
    tok_rows, width = tokens.shape[1:]
    experts = router.shape[1]
    plan = (images // experts, halves)
    hidden_dev = w_in.shape[2]
    long = width + LANES
    router_t = router.T
    scale_row = slot_scale.reshape(1, experts)
    inputs = (tokens, grad_out, router_t, scale_row)
    sent, logit, inv_x = call(
        functools.partial(front_kernel, plan),
        [((devices, 2, long), BF), ((experts, tok_rows), F32), ((1, tok_rows), F32)],
        *inputs,
        stays=range(4),
        buffers=[pltpu.VMEM(a.shape, a.dtype) for a in inputs] + [pltpu.SemaphoreType.DMA((4,))],
        flops=FRONT,
    )
    got = exchange(sent)
    back, rows, grad_rows, hidden, dact = call(
        functools.partial(expert_kernel, images, halves),
        [((devices, 2, long), BF), ((images, width), BF), ((images, width), BF),
         ((images, hidden_dev), BF), ((images, hidden_dev), BF)],
        got, w_in, w_out,
        flops=10**9,
    )
    back = exchange(back)
    grad_w_in = weight_grad(rows, dact)
    grad_w_out = weight_grad(hidden, grad_rows)
    sums, ys, coef, mix, signal = call(
        functools.partial(middle_kernel, plan),
        [((experts, long), F32), ((experts, width), BF), ((2 * experts, tok_rows), BF),
         ((2 * experts, width), BF), ((1, tok_rows), F32)],
        back, tokens, grad_out, logit, inv_x, router_t, scale_row,
    )
    combined, grad_tokens = call(
        tail_kernel,
        [(tokens.shape, BF), (tokens.shape, BF)],
        tokens, logit, ys, coef, mix, signal,
    )
    terms, ((combined, grad_tokens), grad_w_in, grad_w_out) = sum_everywhere(
        sums, devices, [(combined, grad_tokens), grad_w_in, grad_w_out]
    )
    grad_router, grad_scale = call(
        last_kernel, [((experts, width), F32), ((1, experts), F32)], *terms
    )
    return (combined, grad_tokens, grad_router.T, grad_scale[0], grad_w_in, grad_w_out)


def solution(mesh):
    images, halves = mesh.shape["img"], mesh.shape["tok"]

    def body(*args):
        return shards(images, halves, *args)

    return jax.shard_map(
        body,
        mesh=mesh,
        in_specs=(
            P("img", "tok", None),
            P("img", "tok", None),
            P(),
            P(),
            P("img", None, "tok"),
            P("img", "tok", None),
        ),
        out_specs=(
            P("img", "tok", None),
            P("img", "tok", None),
            P(),
            P(),
            P("img", None, "tok"),
            P("img", "tok", None),
        ),
        check_vma=False,
    )
```

```python
import functools

import jax
import jax.numpy as jnp
from jax import lax
from jax.experimental import pallas as pl
from jax.experimental.pallas import tpu as pltpu
from jax.sharding import PartitionSpec as P

EPSILON = 1e-06
ROOT_HALF = 0.7071067811865476
DENSITY = 0.3989422804014327
BF = jnp.bfloat16
F32 = jnp.float32
BOTH = ("img", "tok")
LANES = 128
FRONT = 4 * 10**9
PIECES = 4


def dot(left, right, dims):
    return lax.dot_general(left, right, (dims, ((), ())), preferred_element_type=F32)


def log2(size):
    assert size & (size - 1) == 0
    return size.bit_length() - 1


def iota(shape, axis):
    return lax.broadcasted_iota(jnp.int32, shape, axis)


def digits(row, sizes):
    out = []
    for size in reversed(sizes):
        out.append(row & (size - 1))
        row = row >> log2(size)
    return out[::-1]


def selection(shape, row_key, column_key):
    hit = row_key(iota(shape, 0)) == column_key(iota(shape, 1))
    return jnp.where(hit, 1.0, 0.0).astype(BF)


def pick(left_key, left_size, right, right_key):
    return dot(selection((left_size, right.shape[0]), left_key, right_key), right, ((1,), (0,)))


def store_blocks(ref, rows):
    ref[...] = rows.astype(BF).reshape(ref.shape)


def load_blocks(ref):
    return ref[...].reshape(2 * ref.shape[0], ref.shape[2])


def itself(row):
    return row


def as_column(row):
    size = row.shape[1]
    eye = iota((size, size), 0) == iota((size, size), 1)
    return jnp.sum(jnp.where(eye, row, 0.0), 1, keepdims=True)


def row_of(column):
    return jnp.transpose(jnp.broadcast_to(column, (column.shape[0], LANES)))[:1]


def stack_rows(first, second, extras):
    lane = iota((first.shape[0], LANES), 1)
    high = jnp.zeros(lane.shape, F32)
    low = jnp.zeros(lane.shape, F32)
    for place, value in enumerate(extras):
        top = value.astype(BF).astype(F32)
        high = jnp.where(lane == place, top, high)
        low = jnp.where(lane == place, value - top, low)
    return jnp.concatenate(
        [jnp.concatenate([first, high], 1), jnp.concatenate([second, low], 1)], 0
    ).astype(BF)


def slot_column(router_ref, scale_ref):
    router_f = router_ref[...].astype(F32)
    inv_p = lax.rsqrt(jnp.sum(router_f * router_f, 1, keepdims=True) + EPSILON)
    scale = as_column(scale_ref[...])
    return router_f, inv_p, scale


def softmax(logit):
    expo = jnp.exp(logit)
    return expo, expo / jnp.sum(expo, 0, keepdims=True)


def fetch(sources, targets, sems):
    copies = [
        pltpu.make_async_copy(source, target, sems.at[place])
        for place, (source, target) in enumerate(zip(sources, targets))
    ]
    for copy in copies:
        copy.start()
    return copies


def expert_rows(plan, experts):
    copies, halves = plan

    def key(row):
        _, place, _, kind = digits(row, (copies, experts, halves, 2))
        return kind * experts + place

    return key


def image_rows(images, halves):
    def key(row):
        place, _, kind = digits(row, (images, halves, 2))
        return kind * images + place

    return key


def lane_factor(shape):
    return 1.0 + iota(shape, 1).astype(F32) * (1.0 / LANES)


def front_kernel(
    plan, tok_hbm, grad_hbm, router_hbm, scale_hbm, sent_ref, logit_ref, inv_ref,
    tok_ref, grad_ref, router_ref, scale_ref, sems,
):
    size = tok_ref.shape[1] // PIECES
    pieces = [pl.ds(place * size, size) for place in range(PIECES)]
    arrived = fetch(
        [tok_hbm.at[:, piece] for piece in pieces] + [router_hbm, scale_hbm]
        + [grad_hbm.at[:, piece] for piece in pieces],
        [tok_ref.at[:, piece] for piece in pieces] + [router_ref, scale_ref]
        + [grad_ref.at[:, piece] for piece in pieces],
        sems,
    )
    for copy in arrived[: PIECES + 2]:
        copy.wait()
    tok = tok_ref[0]
    tok_f = tok.astype(F32)
    inv_x = row_of(lax.rsqrt(jnp.sum(tok_f * tok_f, 1, keepdims=True) + EPSILON))
    _, inv_p, scale = slot_column(router_ref, scale_ref)
    raw = dot(router_ref[...], tok, ((1,), (1,)))
    logit = raw * inv_x * (inv_p * scale)
    expo, comb = softmax(logit)
    numer = dot(expo.astype(BF), tok, ((1,), (0,)))
    for copy in arrived[PIECES + 2 :]:
        copy.wait()
    dys = dot(comb.astype(BF), grad_ref[0], ((1,), (0,)))
    rows = stack_rows(numer, dys, [jnp.sum(expo, 1, keepdims=True)])
    store_blocks(sent_ref, pick(expert_rows(plan, router_ref.shape[0]), 2 * sent_ref.shape[0], rows, itself))
    logit_ref[...] = logit
    inv_ref[...] = inv_x


def expert_kernel(
    images, halves, got_ref, one_ref, two_ref, back_ref, rows_ref, grad_rows_ref, hidden_ref, dact_ref
):
    width = one_ref.shape[1]
    key = image_rows(images, halves)
    sums = pick(itself, 2 * images, load_blocks(got_ref), key)
    den = sums[:images, width : width + 1] + sums[images:, width : width + 1]
    rows = (sums[:images, :width] / den).astype(BF)
    grad_rows = sums[images:, :width].astype(BF)
    out_part = in_part = corr = 0.0
    size = one_ref.shape[2] // 2
    for start in (0, size):
        part = slice(start, start + size)
        act = dot(rows, one_ref[0, :, part], ((1,), (0,)))
        grad_h = dot(grad_rows, two_ref[0, part], ((1,), (1,)))
        phi = 0.5 * (1.0 + lax.erf(act * ROOT_HALF))
        hidden = (act * phi).astype(BF)
        dact = (grad_h * (phi + act * jnp.exp(-0.5 * act * act) * DENSITY)).astype(BF)
        out_part += dot(hidden, two_ref[0, part], ((1,), (0,)))
        in_part += dot(dact, one_ref[0, :, part], ((1,), (1,)))
        corr += jnp.sum(dact.astype(F32) * act, 1, keepdims=True)
        hidden_ref[:, part] = hidden
        dact_ref[:, part] = dact
    packed = stack_rows(out_part, in_part, [den, corr])
    store_blocks(back_ref, pick(key, 2 * back_ref.shape[0], packed, itself))
    rows_ref[...] = rows
    grad_rows_ref[...] = grad_rows


def outer_kernel(size, left_ref, right_ref, out_hbm, out_ref, sems):
    copies = []
    for place in range(left_ref.shape[1] // size):
        part = slice(place * size, (place + 1) * size)
        out_ref[0, part] = dot(left_ref[:, part], right_ref[...], ((0,), (0,))).astype(BF)
        copy = pltpu.make_async_copy(
            out_ref.at[:, pl.ds(place * size, size)], out_hbm.at[:, pl.ds(place * size, size)],
            sems.at[place],
        )
        copy.start()
        copies.append(copy)
    for copy in copies:
        copy.wait()


def middle_kernel(
    plan, back_ref, tok_ref, grad_ref, logit_ref, inv_ref, router_ref, scale_ref,
    sums_ref, outs_ref, coef_ref, mix_ref, signal_ref,
):
    experts, width = router_ref.shape
    sums = pick(itself, 2 * experts, load_blocks(back_ref), expert_rows(plan, router_ref.shape[0]))
    extras = sums[:experts, width:] + sums[experts:, width:]
    den = extras[:, :1] * (1.0 / (plan[0] * plan[1]))
    corr = extras[:, 1:2]
    ys = sums[:experts, :width].astype(BF)
    dxs = sums[experts:, :width].astype(BF)
    router_f, inv_p, scale = slot_column(router_ref, scale_ref)
    tok = tok_ref[0]
    logit = logit_ref[...]
    inv_x = inv_ref[...]
    expo, comb = softmax(logit)
    dcomb = dot(ys, grad_ref[0], ((1,), (1,)))
    ddisp = dot(dxs, tok, ((1,), (1,)))
    dlc = comb * (dcomb - jnp.sum(comb * dcomb, 0, keepdims=True))
    grad_l = expo / den * (ddisp - corr) + dlc
    product = grad_l * logit
    grad_q = (grad_l * inv_x * (inv_p * scale)).astype(BF)
    outer = dot(grad_q, tok, ((1,), (0,)))
    total = jnp.sum(product, 1, keepdims=True)
    local = outer - inv_p * inv_p * total * router_f
    sums_ref[...] = jnp.concatenate([local, total / scale * lane_factor((experts, LANES))], 1).astype(BF)
    outs_ref[...] = ys
    coef_ref[...] = jnp.concatenate([expo, grad_q.astype(F32)], 0).astype(BF)
    mix_ref[...] = jnp.concatenate([dxs.astype(F32) / den, router_f], 0).astype(BF)
    signal_ref[...] = inv_x * inv_x * jnp.sum(product, 0, keepdims=True)


def tail_kernel(tok_ref, logit_ref, outs_ref, coef_ref, mix_ref, signal_ref, combined_ref, grads_ref):
    _, comb = softmax(logit_ref[...])
    combined_ref[0] = dot(comb.astype(BF), outs_ref[...], ((0,), (0,))).astype(BF)
    signal = signal_ref[...]
    column = jnp.transpose(jnp.broadcast_to(signal, (LANES, signal.shape[1])))[:, :1]
    grads = dot(coef_ref[...], mix_ref[...], ((0,), (0,)))
    grads_ref[0] = (grads - column * tok_ref[0].astype(F32)).astype(BF)


def last_kernel(own_ref, other_ref, *refs):
    *more, router_ref, scale_ref = refs
    sums = own_ref[...].astype(F32) + other_ref[...].astype(F32)
    if more:
        sums = sums + (more[0][...].astype(F32) + more[1][...].astype(F32))
    experts, width = router_ref.shape
    router_ref[...] = sums[:, :width]
    eye = iota((experts, experts), 0) == iota((experts, experts), 1)
    scale = jnp.sum(sums[:, width:] / lane_factor((experts, LANES)), 1, keepdims=True) * (1.0 / LANES)
    scale_ref[...] = jnp.sum(jnp.where(eye, scale, 0.0), 0, keepdims=True)


def call(kernel, outs, *args, stays=(), buffers=(), flops=10**7, room=24 * 2**20, home=pltpu.VMEM):
    specs = [pl.BlockSpec(memory_space=pltpu.VMEM)] * len(args)
    args = list(args)
    for place in stays:
        specs[place] = pl.BlockSpec(memory_space=pltpu.HBM)
        args[place] = pltpu.with_memory_space_constraint(args[place], pltpu.HBM)
    return pl.pallas_call(
        kernel,
        out_shape=[jax.ShapeDtypeStruct(shape, dtype) for shape, dtype in outs],
        in_specs=specs,
        out_specs=[pl.BlockSpec(memory_space=home)] * len(outs),
        scratch_shapes=buffers,
        compiler_params=pltpu.CompilerParams(vmem_limit_bytes=room),
        cost_estimate=pl.CostEstimate(
            flops=flops, bytes_accessed=sum(a.size * a.dtype.itemsize for a in args), transcendentals=0
        ),
    )(*args)


def weight_grad(left, right):
    size = 256
    shape = (1, left.shape[1], right.shape[1])
    (out,) = call(
        functools.partial(outer_kernel, size), [(shape, BF)], left, right,
        buffers=[pltpu.VMEM(shape, BF), pltpu.SemaphoreType.DMA((shape[1] // size,))],
        flops=10**9, home=pltpu.HBM,
    )
    return out


def exchange(block):
    return lax.all_to_all(block, BOTH, split_axis=0, concat_axis=0, tiled=True)


def pair(term, mask, devices):
    return lax.ppermute(term, BOTH, [(d, d ^ mask) for d in range(devices)])


def sum_everywhere(term, devices, beside):
    done = []

    def together(value):
        if len(done) < len(beside):
            value, ready = lax.optimization_barrier((value, beside[len(done)]))
            done.append(ready)
        return value

    term = term.astype(F32) + together(pair(term, 2, devices)).astype(F32)
    masks = [1] + [1 << place for place in range(2, log2(devices))]
    rounds = [masks[place : place + 2] for place in range(0, len(masks), 2)]
    for group in rounds:
        if group is not rounds[0]:
            term = (terms[0].astype(F32) + terms[1].astype(F32)) + (
                terms[2].astype(F32) + terms[3].astype(F32)
            )
        own = term.astype(BF)
        steps = [group[1], group[0], group[0] ^ group[1]] if len(group) == 2 else group
        terms = [own] + [pair(own, mask, devices) for mask in steps]
        terms[-1] = together(terms[-1])
    return terms, done + beside[len(done) :]


def shards(images, halves, tokens, grad_out, router, slot_scale, w_in, w_out):
    devices = images * halves
    tok_rows, width = tokens.shape[1:]
    experts = router.shape[1]
    plan = (images // experts, halves)
    hidden_dev = w_in.shape[2]
    long = width + LANES
    router_t = router.T
    scale_row = slot_scale.reshape(1, experts)
    inputs = (tokens, grad_out, router_t, scale_row)
    sent, logit, inv_x = call(
        functools.partial(front_kernel, plan),
        [((devices, 2, long), BF), ((experts, tok_rows), F32), ((1, tok_rows), F32)],
        *inputs,
        stays=range(4),
        buffers=[pltpu.VMEM(a.shape, a.dtype) for a in inputs] + [pltpu.SemaphoreType.DMA((2 * PIECES + 2,))],
        flops=FRONT,
    )
    got = exchange(sent)
    back, rows, grad_rows, hidden, dact = call(
        functools.partial(expert_kernel, images, halves),
        [((devices, 2, long), BF), ((images, width), BF), ((images, width), BF),
         ((images, hidden_dev), BF), ((images, hidden_dev), BF)],
        got, w_in, w_out,
        flops=10**9,
    )
    back = exchange(back)
    grad_w_in = weight_grad(rows, dact)
    grad_w_out = weight_grad(hidden, grad_rows)
    sums, ys, coef, mix, signal = call(
        functools.partial(middle_kernel, plan),
        [((experts, long), BF), ((experts, width), BF), ((2 * experts, tok_rows), BF),
         ((2 * experts, width), BF), ((1, tok_rows), F32)],
        back, tokens, grad_out, logit, inv_x, router_t, scale_row,
    )
    combined, grad_tokens = call(
        tail_kernel,
        [(tokens.shape, BF), (tokens.shape, BF)],
        tokens, logit, ys, coef, mix, signal,
    )
    terms, ((combined, grad_tokens), grad_w_in, grad_w_out) = sum_everywhere(
        sums, devices, [(combined, grad_tokens), grad_w_in, grad_w_out]
    )
    grad_router, grad_scale = call(
        last_kernel, [((experts, width), F32), ((1, experts), F32)], *terms
    )
    return (combined, grad_tokens, grad_router.T, grad_scale[0], grad_w_in, grad_w_out)


def solution(mesh):
    images, halves = mesh.shape["img"], mesh.shape["tok"]

    def body(*args):
        return shards(images, halves, *args)

    return jax.shard_map(
        body,
        mesh=mesh,
        in_specs=(
            P("img", "tok", None),
            P("img", "tok", None),
            P(),
            P(),
            P("img", None, "tok"),
            P("img", "tok", None),
        ),
        out_specs=(
            P("img", "tok", None),
            P("img", "tok", None),
            P(),
            P(),
            P("img", None, "tok"),
            P("img", "tok", None),
        ),
        check_vma=False,
    )
```

```python
import functools

import jax
import jax.numpy as jnp
from jax import lax
from jax.experimental import pallas as pl
from jax.experimental.pallas import tpu as pltpu
from jax.sharding import PartitionSpec as P

EPSILON = 1e-06
ROOT_HALF = 0.7071067811865476
DENSITY = 0.3989422804014327
BF = jnp.bfloat16
F32 = jnp.float32
BOTH = ("img", "tok")
LANES = 128
FRONT = 4 * 10**9


def dot(left, right, dims):
    return lax.dot_general(left, right, (dims, ((), ())), preferred_element_type=F32)


def log2(size):
    assert size & (size - 1) == 0
    return size.bit_length() - 1


def iota(shape, axis):
    return lax.broadcasted_iota(jnp.int32, shape, axis)


def digits(row, sizes):
    out = []
    for size in reversed(sizes):
        out.append(row & (size - 1))
        row = row >> log2(size)
    return out[::-1]


def selection(shape, row_key, column_key):
    hit = row_key(iota(shape, 0)) == column_key(iota(shape, 1))
    return jnp.where(hit, 1.0, 0.0).astype(BF)


def pick(left_key, left_size, right, right_key):
    return dot(selection((left_size, right.shape[0]), left_key, right_key), right, ((1,), (0,)))


def store_blocks(ref, rows):
    ref[...] = rows.astype(BF).reshape(ref.shape)


def load_blocks(ref):
    return ref[...].reshape(2 * ref.shape[0], ref.shape[2])


def itself(row):
    return row


def as_column(row):
    size = row.shape[1]
    eye = iota((size, size), 0) == iota((size, size), 1)
    return jnp.sum(jnp.where(eye, row, 0.0), 1, keepdims=True)


def row_of(column):
    return jnp.transpose(jnp.broadcast_to(column, (column.shape[0], LANES)))[:1]


def stack_rows(first, second, extras):
    lane = iota((first.shape[0], LANES), 1)
    high = jnp.zeros(lane.shape, F32)
    low = jnp.zeros(lane.shape, F32)
    for place, value in enumerate(extras):
        top = value.astype(BF).astype(F32)
        high = jnp.where(lane == place, top, high)
        low = jnp.where(lane == place, value - top, low)
    return jnp.concatenate(
        [jnp.concatenate([first, high], 1), jnp.concatenate([second, low], 1)], 0
    ).astype(BF)


def slot_column(router_ref, scale_ref):
    router_f = router_ref[...].astype(F32)
    inv_p = lax.rsqrt(jnp.sum(router_f * router_f, 1, keepdims=True) + EPSILON)
    scale = as_column(scale_ref[...])
    return router_f, inv_p, scale


def softmax(logit):
    expo = jnp.exp(logit)
    return expo, expo / jnp.sum(expo, 0, keepdims=True)


def fetch(sources, targets, sems):
    copies = [
        pltpu.make_async_copy(source, target, sems.at[place])
        for place, (source, target) in enumerate(zip(sources, targets))
    ]
    for copy in copies:
        copy.start()
    return copies


def expert_rows(plan, experts):
    copies, halves = plan

    def key(row):
        _, place, _, kind = digits(row, (copies, experts, halves, 2))
        return kind * experts + place

    return key


def image_rows(images, halves):
    def key(row):
        place, _, kind = digits(row, (images, halves, 2))
        return kind * images + place

    return key


def lane_factor(shape):
    return 1.0 + iota(shape, 1).astype(F32) * (1.0 / LANES)


def front_kernel(
    plan, tok_hbm, grad_hbm, router_hbm, scale_hbm, sent_ref, logit_ref, inv_ref,
    tok_ref, grad_ref, router_ref, scale_ref, sems,
):
    arrived = fetch(
        [tok_hbm, router_hbm, scale_hbm, grad_hbm], [tok_ref, router_ref, scale_ref, grad_ref], sems
    )
    for copy in arrived[:3]:
        copy.wait()
    tok = tok_ref[0]
    tok_f = tok.astype(F32)
    inv_x = row_of(lax.rsqrt(jnp.sum(tok_f * tok_f, 1, keepdims=True) + EPSILON))
    _, inv_p, scale = slot_column(router_ref, scale_ref)
    raw = dot(router_ref[...], tok, ((1,), (1,)))
    logit = raw * inv_x * (inv_p * scale)
    expo, comb = softmax(logit)
    numer = dot(expo.astype(BF), tok, ((1,), (0,)))
    arrived[3].wait()
    dys = dot(comb.astype(BF), grad_ref[0], ((1,), (0,)))
    rows = stack_rows(numer, dys, [jnp.sum(expo, 1, keepdims=True)])
    store_blocks(sent_ref, pick(expert_rows(plan, router_ref.shape[0]), 2 * sent_ref.shape[0], rows, itself))
    logit_ref[...] = logit
    inv_ref[...] = inv_x


def expert_kernel(
    images, halves, got_ref, one_ref, two_ref, back_ref, rows_ref, grad_rows_ref, hidden_ref, dact_ref
):
    width = one_ref.shape[1]
    key = image_rows(images, halves)
    sums = pick(itself, 2 * images, load_blocks(got_ref), key)
    den = sums[:images, width : width + 1] + sums[images:, width : width + 1]
    rows = (sums[:images, :width] / den).astype(BF)
    grad_rows = sums[images:, :width].astype(BF)
    act = jnp.concatenate(
        [dot(rows, one_ref[0, :, n : n + 256], ((1,), (0,))) for n in range(0, one_ref.shape[2], 256)], 1
    )
    grad_h = dot(grad_rows, two_ref[0], ((1,), (1,)))
    phi = 0.5 * (1.0 + lax.erf(act * ROOT_HALF))
    hidden = (act * phi).astype(BF)
    dact = (grad_h * (phi + act * jnp.exp(-0.5 * act * act) * DENSITY)).astype(BF)
    out_part = dot(hidden, two_ref[0], ((1,), (0,)))
    in_part = jnp.concatenate(
        [dot(dact, one_ref[0, n : n + 256], ((1,), (1,))) for n in range(0, width, 256)], 1
    )
    corr = jnp.sum(dact.astype(F32) * act, 1, keepdims=True)
    packed = stack_rows(out_part, in_part, [den, corr])
    store_blocks(back_ref, pick(key, 2 * back_ref.shape[0], packed, itself))
    rows_ref[...] = rows
    grad_rows_ref[...] = grad_rows
    hidden_ref[...] = hidden
    dact_ref[...] = dact


def outer_kernel(size, left_ref, right_ref, out_hbm, out_ref, sems):
    copies = []
    for place in range(left_ref.shape[1] // size):
        part = slice(place * size, (place + 1) * size)
        out_ref[0, part] = dot(left_ref[:, part], right_ref[...], ((0,), (0,))).astype(BF)
        copy = pltpu.make_async_copy(
            out_ref.at[:, pl.ds(place * size, size)], out_hbm.at[:, pl.ds(place * size, size)],
            sems.at[place],
        )
        copy.start()
        copies.append(copy)
    for copy in copies:
        copy.wait()


def middle_kernel(
    plan, back_ref, tok_ref, grad_ref, logit_ref, inv_ref, router_ref, scale_ref,
    sums_ref, outs_ref, coef_ref, mix_ref, signal_ref,
):
    experts, width = router_ref.shape
    sums = pick(itself, 2 * experts, load_blocks(back_ref), expert_rows(plan, router_ref.shape[0]))
    extras = sums[:experts, width:] + sums[experts:, width:]
    den = extras[:, :1] * (1.0 / (plan[0] * plan[1]))
    corr = extras[:, 1:2]
    ys = sums[:experts, :width].astype(BF)
    dxs = sums[experts:, :width].astype(BF)
    router_f, inv_p, scale = slot_column(router_ref, scale_ref)
    tok = tok_ref[0]
    logit = logit_ref[...]
    inv_x = inv_ref[...]
    expo, comb = softmax(logit)
    dcomb = dot(ys, grad_ref[0], ((1,), (1,)))
    ddisp = dot(dxs, tok, ((1,), (1,)))
    dlc = comb * (dcomb - jnp.sum(comb * dcomb, 0, keepdims=True))
    grad_l = expo / den * (ddisp - corr) + dlc
    product = grad_l * logit
    grad_q = (grad_l * inv_x * (inv_p * scale)).astype(BF)
    outer = dot(grad_q, tok, ((1,), (0,)))
    total = jnp.sum(product, 1, keepdims=True)
    local = outer - inv_p * inv_p * total * router_f
    sums_ref[...] = jnp.concatenate([local, total / scale * lane_factor((experts, LANES))], 1)
    outs_ref[...] = ys
    coef_ref[...] = jnp.concatenate([expo, grad_q.astype(F32)], 0).astype(BF)
    mix_ref[...] = jnp.concatenate([dxs.astype(F32) / den, router_f], 0).astype(BF)
    signal_ref[...] = inv_x * inv_x * jnp.sum(product, 0, keepdims=True)


def tail_kernel(tok_ref, logit_ref, outs_ref, coef_ref, mix_ref, signal_ref, combined_ref, grads_ref):
    _, comb = softmax(logit_ref[...])
    combined_ref[0] = dot(comb.astype(BF), outs_ref[...], ((0,), (0,))).astype(BF)
    signal = signal_ref[...]
    column = jnp.transpose(jnp.broadcast_to(signal, (LANES, signal.shape[1])))[:, :1]
    grads = dot(coef_ref[...], mix_ref[...], ((0,), (0,)))
    grads_ref[0] = (grads - column * tok_ref[0].astype(F32)).astype(BF)


def last_kernel(own_ref, other_ref, *refs):
    *more, router_ref, scale_ref = refs
    sums = own_ref[...].astype(F32) + other_ref[...].astype(F32)
    if more:
        sums = sums + (more[0][...].astype(F32) + more[1][...].astype(F32))
    experts, width = router_ref.shape
    router_ref[...] = sums[:, :width]
    eye = iota((experts, experts), 0) == iota((experts, experts), 1)
    scale = jnp.sum(sums[:, width:] / lane_factor((experts, LANES)), 1, keepdims=True) * (1.0 / LANES)
    scale_ref[...] = jnp.sum(jnp.where(eye, scale, 0.0), 0, keepdims=True)


def call(kernel, outs, *args, stays=(), buffers=(), flops=10**7, room=24 * 2**20, home=pltpu.VMEM):
    specs = [pl.BlockSpec(memory_space=pltpu.VMEM)] * len(args)
    args = list(args)
    for place in stays:
        specs[place] = pl.BlockSpec(memory_space=pltpu.HBM)
        args[place] = pltpu.with_memory_space_constraint(args[place], pltpu.HBM)
    return pl.pallas_call(
        kernel,
        out_shape=[jax.ShapeDtypeStruct(shape, dtype) for shape, dtype in outs],
        in_specs=specs,
        out_specs=[pl.BlockSpec(memory_space=home)] * len(outs),
        scratch_shapes=buffers,
        compiler_params=pltpu.CompilerParams(vmem_limit_bytes=room),
        cost_estimate=pl.CostEstimate(
            flops=flops, bytes_accessed=sum(a.size * a.dtype.itemsize for a in args), transcendentals=0
        ),
    )(*args)


def weight_grad(left, right):
    size = 256
    shape = (1, left.shape[1], right.shape[1])
    (out,) = call(
        functools.partial(outer_kernel, size), [(shape, BF)], left, right,
        buffers=[pltpu.VMEM(shape, BF), pltpu.SemaphoreType.DMA((shape[1] // size,))],
        flops=10**9, home=pltpu.HBM,
    )
    return out


def exchange(block):
    return lax.all_to_all(block, BOTH, split_axis=0, concat_axis=0, tiled=True)


def pair(term, mask, devices):
    return lax.ppermute(term, BOTH, [(d, d ^ mask) for d in range(devices)])


def sum_everywhere(term, devices, beside):
    done = []

    def together(value):
        if len(done) < len(beside):
            value, ready = lax.optimization_barrier((value, beside[len(done)]))
            done.append(ready)
        return value

    term = term + together(pair(term, 2, devices))
    masks = [1] + [1 << place for place in range(2, log2(devices))]
    rounds = [masks[place : place + 2] for place in range(0, len(masks), 2)]
    for group in rounds:
        if group is not rounds[0]:
            term = (terms[0].astype(F32) + terms[1].astype(F32)) + (
                terms[2].astype(F32) + terms[3].astype(F32)
            )
        own = term.astype(BF)
        steps = [group[1], group[0], group[0] ^ group[1]] if len(group) == 2 else group
        terms = [own] + [pair(own, mask, devices) for mask in steps]
        terms[-1] = together(terms[-1])
    return terms, done + beside[len(done) :]


def shards(images, halves, tokens, grad_out, router, slot_scale, w_in, w_out):
    devices = images * halves
    tok_rows, width = tokens.shape[1:]
    experts = router.shape[1]
    plan = (images // experts, halves)
    hidden_dev = w_in.shape[2]
    long = width + LANES
    router_t = router.T
    scale_row = slot_scale.reshape(1, experts)
    inputs = (tokens, grad_out, router_t, scale_row)
    sent, logit, inv_x = call(
        functools.partial(front_kernel, plan),
        [((devices, 2, long), BF), ((experts, tok_rows), F32), ((1, tok_rows), F32)],
        *inputs,
        stays=range(4),
        buffers=[pltpu.VMEM(a.shape, a.dtype) for a in inputs] + [pltpu.SemaphoreType.DMA((4,))],
        flops=FRONT,
    )
    got = exchange(sent)
    back, rows, grad_rows, hidden, dact = call(
        functools.partial(expert_kernel, images, halves),
        [((devices, 2, long), BF), ((images, width), BF), ((images, width), BF),
         ((images, hidden_dev), BF), ((images, hidden_dev), BF)],
        got, w_in, w_out,
        flops=10**9,
    )
    back = exchange(back)
    grad_w_in = weight_grad(rows, dact)
    grad_w_out = weight_grad(hidden, grad_rows)
    sums, ys, coef, mix, signal = call(
        functools.partial(middle_kernel, plan),
        [((experts, long), F32), ((experts, width), BF), ((2 * experts, tok_rows), BF),
         ((2 * experts, width), BF), ((1, tok_rows), F32)],
        back, tokens, grad_out, logit, inv_x, router_t, scale_row,
    )
    combined, grad_tokens = call(
        tail_kernel,
        [(tokens.shape, BF), (tokens.shape, BF)],
        tokens, logit, ys, coef, mix, signal,
    )
    terms, ((combined, grad_tokens), grad_w_in, grad_w_out) = sum_everywhere(
        sums, devices, [(combined, grad_tokens), grad_w_in, grad_w_out]
    )
    grad_router, grad_scale = call(
        last_kernel, [((experts, width), F32), ((1, experts), F32)], *terms
    )
    return (combined, grad_tokens, grad_router.T, grad_scale[0], grad_w_in, grad_w_out)


def solution(mesh):
    images, halves = mesh.shape["img"], mesh.shape["tok"]

    def body(*args):
        return shards(images, halves, *args)

    return jax.shard_map(
        body,
        mesh=mesh,
        in_specs=(
            P("img", "tok", None),
            P("img", "tok", None),
            P(),
            P(),
            P("img", None, "tok"),
            P("img", "tok", None),
        ),
        out_specs=(
            P("img", "tok", None),
            P("img", "tok", None),
            P(),
            P(),
            P("img", None, "tok"),
            P("img", "tok", None),
        ),
        check_vma=False,
    )
```

```python
import functools

import jax
import jax.numpy as jnp
from jax import lax
from jax.experimental import pallas as pl
from jax.experimental.pallas import tpu as pltpu
from jax.sharding import PartitionSpec as P

EPSILON = 1e-06
ROOT_HALF = 0.7071067811865476
DENSITY = 0.3989422804014327
BF = jnp.bfloat16
F32 = jnp.float32
BOTH = ("img", "tok")
LANES = 128
FRONT = 4 * 10**9


def dot(left, right, dims):
    return lax.dot_general(left, right, (dims, ((), ())), preferred_element_type=F32)


def log2(size):
    assert size & (size - 1) == 0
    return size.bit_length() - 1


def iota(shape, axis):
    return lax.broadcasted_iota(jnp.int32, shape, axis)


def digits(row, sizes):
    out = []
    for size in reversed(sizes):
        out.append(row & (size - 1))
        row = row >> log2(size)
    return out[::-1]


def selection(shape, row_key, column_key):
    hit = row_key(iota(shape, 0)) == column_key(iota(shape, 1))
    return jnp.where(hit, 1.0, 0.0).astype(BF)


def pick(left_key, left_size, right, right_key):
    return dot(selection((left_size, right.shape[0]), left_key, right_key), right, ((1,), (0,)))


def store_blocks(ref, rows):
    ref[...] = rows.astype(BF).reshape(ref.shape)


def load_blocks(ref):
    return ref[...].reshape(2 * ref.shape[0], ref.shape[2])


def itself(row):
    return row


def as_column(row):
    size = row.shape[1]
    eye = iota((size, size), 0) == iota((size, size), 1)
    return jnp.sum(jnp.where(eye, row, 0.0), 1, keepdims=True)


def row_of(column):
    return jnp.transpose(jnp.broadcast_to(column, (column.shape[0], LANES)))[:1]


def stack_rows(first, second, extras):
    lane = iota((first.shape[0], LANES), 1)
    high = jnp.zeros(lane.shape, F32)
    low = jnp.zeros(lane.shape, F32)
    for place, value in enumerate(extras):
        top = value.astype(BF).astype(F32)
        high = jnp.where(lane == place, top, high)
        low = jnp.where(lane == place, value - top, low)
    return jnp.concatenate(
        [jnp.concatenate([first, high], 1), jnp.concatenate([second, low], 1)], 0
    ).astype(BF)


def slot_column(router_ref, scale_ref):
    router_f = router_ref[...].astype(F32)
    inv_p = lax.rsqrt(jnp.sum(router_f * router_f, 1, keepdims=True) + EPSILON)
    scale = as_column(scale_ref[...])
    return router_f, inv_p, scale


def softmax(logit):
    expo = jnp.exp(logit)
    return expo, expo / jnp.sum(expo, 0, keepdims=True)


def fetch(sources, targets, sems):
    copies = [
        pltpu.make_async_copy(source, target, sems.at[place])
        for place, (source, target) in enumerate(zip(sources, targets))
    ]
    for copy in copies:
        copy.start()
    return copies


def expert_rows(plan, experts):
    copies, halves = plan

    def key(row):
        _, place, _, kind = digits(row, (copies, experts, halves, 2))
        return kind * experts + place

    return key


def half_first(key, inner, halves):
    def moved(row):
        half, place, kind = digits(row, (halves, inner, 2))
        return key((place * halves + half) * 2 + kind)

    return moved


def image_rows(images, halves):
    def key(row):
        place, _, kind = digits(row, (images, halves, 2))
        return kind * images + place

    return key


def lane_factor(shape):
    return 1.0 + iota(shape, 1).astype(F32) * (1.0 / LANES)


def front_kernel(
    plan, tok_hbm, grad_hbm, router_hbm, scale_hbm, sent_ref, logit_ref, inv_ref,
    tok_ref, grad_ref, router_ref, scale_ref, sems,
):
    arrived = fetch(
        [tok_hbm, router_hbm, scale_hbm, grad_hbm], [tok_ref, router_ref, scale_ref, grad_ref], sems
    )
    for copy in arrived[:3]:
        copy.wait()
    tok = tok_ref[0]
    tok_f = tok.astype(F32)
    inv_x = row_of(lax.rsqrt(jnp.sum(tok_f * tok_f, 1, keepdims=True) + EPSILON))
    _, inv_p, scale = slot_column(router_ref, scale_ref)
    raw = dot(router_ref[...], tok, ((1,), (1,)))
    logit = raw * inv_x * (inv_p * scale)
    expo, comb = softmax(logit)
    numer = dot(expo.astype(BF), tok, ((1,), (0,)))
    arrived[3].wait()
    dys = dot(comb.astype(BF), grad_ref[0], ((1,), (0,)))
    rows = stack_rows(numer, dys, [jnp.sum(expo, 1, keepdims=True)])
    experts = router_ref.shape[0]
    key = half_first(expert_rows(plan, experts), plan[0] * experts, plan[1])
    store_blocks(sent_ref, pick(key, 2 * sent_ref.shape[0], rows, itself))
    logit_ref[...] = logit
    inv_ref[...] = inv_x


def expert_kernel(
    images, halves, got_ref, one_ref, two_ref, back_ref, rows_ref, grad_rows_ref, hidden_ref, dact_ref
):
    width = one_ref.shape[1]
    key = image_rows(images, halves)
    sums = pick(itself, 2 * images, load_blocks(got_ref), half_first(key, images, halves))
    den = sums[:images, width : width + 1] + sums[images:, width : width + 1]
    rows = (sums[:images, :width] / den).astype(BF)
    grad_rows = sums[images:, :width].astype(BF)
    act = dot(rows, one_ref[0], ((1,), (0,)))
    grad_h = dot(grad_rows, two_ref[0], ((1,), (1,)))
    phi = 0.5 * (1.0 + lax.erf(act * ROOT_HALF))
    hidden = (act * phi).astype(BF)
    dact = (grad_h * (phi + act * jnp.exp(-0.5 * act * act) * DENSITY)).astype(BF)
    out_part = dot(hidden, two_ref[0], ((1,), (0,)))
    in_part = dot(dact, one_ref[0], ((1,), (1,)))
    corr = jnp.sum(dact.astype(F32) * act, 1, keepdims=True)
    packed = stack_rows(out_part, in_part, [den, corr])
    store_blocks(back_ref, pick(key, 2 * back_ref.shape[0], packed, itself))
    rows_ref[...] = rows
    grad_rows_ref[...] = grad_rows
    hidden_ref[...] = hidden
    dact_ref[...] = dact


def outer_kernel(size, left_ref, right_ref, out_hbm, out_ref, sems):
    copies = []
    for place in range(left_ref.shape[1] // size):
        part = slice(place * size, (place + 1) * size)
        out_ref[0, part] = dot(left_ref[:, part], right_ref[...], ((0,), (0,))).astype(BF)
        copy = pltpu.make_async_copy(
            out_ref.at[:, pl.ds(place * size, size)], out_hbm.at[:, pl.ds(place * size, size)],
            sems.at[place],
        )
        copy.start()
        copies.append(copy)
    for copy in copies:
        copy.wait()


def middle_kernel(
    plan, back_ref, tok_ref, grad_ref, logit_ref, inv_ref, router_ref, scale_ref,
    sums_ref, outs_ref, coef_ref, mix_ref, signal_ref,
):
    experts, width = router_ref.shape
    sums = pick(itself, 2 * experts, load_blocks(back_ref), expert_rows(plan, router_ref.shape[0]))
    extras = sums[:experts, width:] + sums[experts:, width:]
    den = extras[:, :1] * (1.0 / (plan[0] * plan[1]))
    corr = extras[:, 1:2]
    ys = sums[:experts, :width].astype(BF)
    dxs = sums[experts:, :width].astype(BF)
    router_f, inv_p, scale = slot_column(router_ref, scale_ref)
    tok = tok_ref[0]
    logit = logit_ref[...]
    inv_x = inv_ref[...]
    expo, comb = softmax(logit)
    dcomb = dot(ys, grad_ref[0], ((1,), (1,)))
    ddisp = dot(dxs, tok, ((1,), (1,)))
    dlc = comb * (dcomb - jnp.sum(comb * dcomb, 0, keepdims=True))
    grad_l = expo / den * (ddisp - corr) + dlc
    product = grad_l * logit
    grad_q = (grad_l * inv_x * (inv_p * scale)).astype(BF)
    outer = dot(grad_q, tok, ((1,), (0,)))
    total = jnp.sum(product, 1, keepdims=True)
    local = outer - inv_p * inv_p * total * router_f
    sums_ref[...] = jnp.concatenate([local, total / scale * lane_factor((experts, LANES))], 1)
    outs_ref[...] = ys
    coef_ref[...] = jnp.concatenate([expo, grad_q.astype(F32)], 0).astype(BF)
    mix_ref[...] = jnp.concatenate([dxs.astype(F32) / den, router_f], 0).astype(BF)
    signal_ref[...] = inv_x * inv_x * jnp.sum(product, 0, keepdims=True)


def tail_kernel(tok_ref, logit_ref, outs_ref, coef_ref, mix_ref, signal_ref, combined_ref, grads_ref):
    _, comb = softmax(logit_ref[...])
    combined_ref[0] = dot(comb.astype(BF), outs_ref[...], ((0,), (0,))).astype(BF)
    signal = signal_ref[...]
    column = jnp.transpose(jnp.broadcast_to(signal, (LANES, signal.shape[1])))[:, :1]
    grads = dot(coef_ref[...], mix_ref[...], ((0,), (0,)))
    grads_ref[0] = (grads - column * tok_ref[0].astype(F32)).astype(BF)


def last_kernel(own_ref, other_ref, *refs):
    *more, router_ref, scale_ref = refs
    sums = own_ref[...].astype(F32) + other_ref[...].astype(F32)
    if more:
        sums = sums + (more[0][...].astype(F32) + more[1][...].astype(F32))
    experts, width = router_ref.shape
    router_ref[...] = sums[:, :width]
    eye = iota((experts, experts), 0) == iota((experts, experts), 1)
    scale = jnp.sum(sums[:, width:] / lane_factor((experts, LANES)), 1, keepdims=True) * (1.0 / LANES)
    scale_ref[...] = jnp.sum(jnp.where(eye, scale, 0.0), 0, keepdims=True)


def call(kernel, outs, *args, stays=(), buffers=(), flops=10**7, room=24 * 2**20, home=pltpu.VMEM):
    specs = [pl.BlockSpec(memory_space=pltpu.VMEM)] * len(args)
    args = list(args)
    for place in stays:
        specs[place] = pl.BlockSpec(memory_space=pltpu.HBM)
        args[place] = pltpu.with_memory_space_constraint(args[place], pltpu.HBM)
    return pl.pallas_call(
        kernel,
        out_shape=[jax.ShapeDtypeStruct(shape, dtype) for shape, dtype in outs],
        in_specs=specs,
        out_specs=[pl.BlockSpec(memory_space=home)] * len(outs),
        scratch_shapes=buffers,
        compiler_params=pltpu.CompilerParams(vmem_limit_bytes=room),
        cost_estimate=pl.CostEstimate(
            flops=flops, bytes_accessed=sum(a.size * a.dtype.itemsize for a in args), transcendentals=0
        ),
    )(*args)


def weight_grad(left, right):
    size = 256
    shape = (1, left.shape[1], right.shape[1])
    (out,) = call(
        functools.partial(outer_kernel, size), [(shape, BF)], left, right,
        buffers=[pltpu.VMEM(shape, BF), pltpu.SemaphoreType.DMA((shape[1] // size,))],
        flops=10**9, home=pltpu.HBM,
    )
    return out


def exchange(block, axes):
    return lax.all_to_all(block, axes, split_axis=0, concat_axis=0, tiled=True)


def pair(term, mask, devices):
    return lax.ppermute(term, BOTH, [(d, d ^ mask) for d in range(devices)])


def sum_everywhere(term, devices, beside):
    done = []

    def together(value):
        if len(done) < len(beside):
            value, ready = lax.optimization_barrier((value, beside[len(done)]))
            done.append(ready)
        return value

    term = term + together(pair(term, 2, devices))
    masks = [1] + [1 << place for place in range(2, log2(devices))]
    rounds = [masks[place : place + 2] for place in range(0, len(masks), 2)]
    for group in rounds:
        if group is not rounds[0]:
            term = (terms[0].astype(F32) + terms[1].astype(F32)) + (
                terms[2].astype(F32) + terms[3].astype(F32)
            )
        own = term.astype(BF)
        steps = [group[1], group[0], group[0] ^ group[1]] if len(group) == 2 else group
        terms = [own] + [pair(own, mask, devices) for mask in steps]
        terms[-1] = together(terms[-1])
    return terms, done + beside[len(done) :]


def shards(images, halves, tokens, grad_out, router, slot_scale, w_in, w_out):
    devices = images * halves
    tok_rows, width = tokens.shape[1:]
    experts = router.shape[1]
    plan = (images // experts, halves)
    hidden_dev = w_in.shape[2]
    long = width + LANES
    router_t = router.T
    scale_row = slot_scale.reshape(1, experts)
    inputs = (tokens, grad_out, router_t, scale_row)
    sent, logit, inv_x = call(
        functools.partial(front_kernel, plan),
        [((devices, 2, long), BF), ((experts, tok_rows), F32), ((1, tok_rows), F32)],
        *inputs,
        stays=range(4),
        buffers=[pltpu.VMEM(a.shape, a.dtype) for a in inputs] + [pltpu.SemaphoreType.DMA((4,))],
        flops=FRONT,
    )
    got = exchange(sent, ("tok", "img"))
    back, rows, grad_rows, hidden, dact = call(
        functools.partial(expert_kernel, images, halves),
        [((devices, 2, long), BF), ((images, width), BF), ((images, width), BF),
         ((images, hidden_dev), BF), ((images, hidden_dev), BF)],
        got, w_in, w_out,
        flops=10**9,
    )
    back = exchange(back, BOTH)
    grad_w_in = weight_grad(rows, dact)
    grad_w_out = weight_grad(hidden, grad_rows)
    sums, ys, coef, mix, signal = call(
        functools.partial(middle_kernel, plan),
        [((experts, long), F32), ((experts, width), BF), ((2 * experts, tok_rows), BF),
         ((2 * experts, width), BF), ((1, tok_rows), F32)],
        back, tokens, grad_out, logit, inv_x, router_t, scale_row,
    )
    combined, grad_tokens = call(
        tail_kernel,
        [(tokens.shape, BF), (tokens.shape, BF)],
        tokens, logit, ys, coef, mix, signal,
    )
    terms, ((combined, grad_tokens), grad_w_in, grad_w_out) = sum_everywhere(
        sums, devices, [(combined, grad_tokens), grad_w_in, grad_w_out]
    )
    grad_router, grad_scale = call(
        last_kernel, [((experts, width), F32), ((1, experts), F32)], *terms
    )
    return (combined, grad_tokens, grad_router.T, grad_scale[0], grad_w_in, grad_w_out)


def solution(mesh):
    images, halves = mesh.shape["img"], mesh.shape["tok"]

    def body(*args):
        return shards(images, halves, *args)

    return jax.shard_map(
        body,
        mesh=mesh,
        in_specs=(
            P("img", "tok", None),
            P("img", "tok", None),
            P(),
            P(),
            P("img", None, "tok"),
            P("img", "tok", None),
        ),
        out_specs=(
            P("img", "tok", None),
            P("img", "tok", None),
            P(),
            P(),
            P("img", None, "tok"),
            P("img", "tok", None),
        ),
        check_vma=False,
    )
```

```python
import functools

import jax
import jax.numpy as jnp
from jax import lax
from jax.experimental import pallas as pl
from jax.experimental.pallas import tpu as pltpu
from jax.sharding import PartitionSpec as P

EPSILON = 1e-06
ROOT_HALF = 0.7071067811865476
DENSITY = 0.3989422804014327
BF = jnp.bfloat16
F32 = jnp.float32
BOTH = ("far", "near", "tok")
OUT_ORDER = ("tok", "near", "far")
BACK_ORDER = ("tok", "far", "near")
LANES = 128
FRONT = 4 * 10**9


def dot(left, right, dims):
    return lax.dot_general(left, right, (dims, ((), ())), preferred_element_type=F32)


def log2(size):
    assert size & (size - 1) == 0
    return size.bit_length() - 1


def iota(shape, axis):
    return lax.broadcasted_iota(jnp.int32, shape, axis)


def digits(row, sizes):
    out = []
    for size in reversed(sizes):
        out.append(row & (size - 1))
        row = row >> log2(size)
    return out[::-1]


def selection(shape, row_key, column_key):
    hit = row_key(iota(shape, 0)) == column_key(iota(shape, 1))
    return jnp.where(hit, 1.0, 0.0).astype(BF)


def pick(left_key, left_size, right, right_key):
    return dot(selection((left_size, right.shape[0]), left_key, right_key), right, ((1,), (0,)))


def store_blocks(ref, rows):
    ref[...] = rows.astype(BF).reshape(ref.shape)


def load_blocks(ref):
    return ref[...].reshape(2 * ref.shape[0], ref.shape[2])


def itself(row):
    return row


def as_column(row):
    size = row.shape[1]
    eye = iota((size, size), 0) == iota((size, size), 1)
    return jnp.sum(jnp.where(eye, row, 0.0), 1, keepdims=True)


def row_of(column):
    return jnp.transpose(jnp.broadcast_to(column, (column.shape[0], LANES)))[:1]


def stack_rows(first, second, extras):
    lane = iota((first.shape[0], LANES), 1)
    high = jnp.zeros(lane.shape, F32)
    low = jnp.zeros(lane.shape, F32)
    for place, value in enumerate(extras):
        top = value.astype(BF).astype(F32)
        high = jnp.where(lane == place, top, high)
        low = jnp.where(lane == place, value - top, low)
    return jnp.concatenate(
        [jnp.concatenate([first, high], 1), jnp.concatenate([second, low], 1)], 0
    ).astype(BF)


def slot_column(router_ref, scale_ref):
    router_f = router_ref[...].astype(F32)
    inv_p = lax.rsqrt(jnp.sum(router_f * router_f, 1, keepdims=True) + EPSILON)
    scale = as_column(scale_ref[...])
    return router_f, inv_p, scale


def softmax(logit):
    expo = jnp.exp(logit)
    return expo, expo / jnp.sum(expo, 0, keepdims=True)


def fetch(sources, targets, sems):
    copies = [
        pltpu.make_async_copy(source, target, sems.at[place])
        for place, (source, target) in enumerate(zip(sources, targets))
    ]
    for copy in copies:
        copy.start()
    return copies


def expert_rows(plan, experts):
    copies, halves = plan

    def key(row):
        _, place, _, kind = digits(row, (copies, experts, halves, 2))
        return kind * experts + place

    return key


def in_order(key, order, sizes):
    def moved(row):
        *places, kind = digits(row, [sizes[axis] for axis in order] + [2])
        at = dict(zip(order, places))
        place = (at["far"] * sizes["near"] + at["near"]) * sizes["tok"] + at["tok"]
        return key(place * 2 + kind)

    return moved


def image_rows(images, halves):
    def key(row):
        place, _, kind = digits(row, (images, halves, 2))
        return kind * images + place

    return key


def lane_factor(shape):
    return 1.0 + iota(shape, 1).astype(F32) * (1.0 / LANES)


def front_kernel(
    plan, sizes, tok_hbm, grad_hbm, router_hbm, scale_hbm, sent_ref, logit_ref, inv_ref,
    tok_ref, grad_ref, router_ref, scale_ref, sems,
):
    arrived = fetch(
        [tok_hbm, router_hbm, scale_hbm, grad_hbm], [tok_ref, router_ref, scale_ref, grad_ref], sems
    )
    for copy in arrived[:3]:
        copy.wait()
    tok = tok_ref[0]
    tok_f = tok.astype(F32)
    inv_x = row_of(lax.rsqrt(jnp.sum(tok_f * tok_f, 1, keepdims=True) + EPSILON))
    _, inv_p, scale = slot_column(router_ref, scale_ref)
    raw = dot(router_ref[...], tok, ((1,), (1,)))
    logit = raw * inv_x * (inv_p * scale)
    expo, comb = softmax(logit)
    numer = dot(expo.astype(BF), tok, ((1,), (0,)))
    arrived[3].wait()
    dys = dot(comb.astype(BF), grad_ref[0], ((1,), (0,)))
    rows = stack_rows(numer, dys, [jnp.sum(expo, 1, keepdims=True)])
    experts = router_ref.shape[0]
    key = in_order(expert_rows(plan, experts), OUT_ORDER, sizes)
    store_blocks(sent_ref, pick(key, 2 * sent_ref.shape[0], rows, itself))
    logit_ref[...] = logit
    inv_ref[...] = inv_x


def expert_kernel(
    images, halves, sizes, got_ref, one_ref, two_ref, back_ref, rows_ref, grad_rows_ref, hidden_ref, dact_ref
):
    width = one_ref.shape[1]
    key = image_rows(images, halves)
    sums = pick(itself, 2 * images, load_blocks(got_ref), in_order(key, OUT_ORDER, sizes))
    den = sums[:images, width : width + 1] + sums[images:, width : width + 1]
    rows = (sums[:images, :width] / den).astype(BF)
    grad_rows = sums[images:, :width].astype(BF)
    act = dot(rows, one_ref[0], ((1,), (0,)))
    grad_h = dot(grad_rows, two_ref[0], ((1,), (1,)))
    phi = 0.5 * (1.0 + lax.erf(act * ROOT_HALF))
    hidden = (act * phi).astype(BF)
    dact = (grad_h * (phi + act * jnp.exp(-0.5 * act * act) * DENSITY)).astype(BF)
    out_part = dot(hidden, two_ref[0], ((1,), (0,)))
    in_part = dot(dact, one_ref[0], ((1,), (1,)))
    corr = jnp.sum(dact.astype(F32) * act, 1, keepdims=True)
    packed = stack_rows(out_part, in_part, [den, corr])
    back_key = in_order(key, BACK_ORDER, sizes)
    store_blocks(back_ref, pick(back_key, 2 * back_ref.shape[0], packed, itself))
    rows_ref[...] = rows
    grad_rows_ref[...] = grad_rows
    hidden_ref[...] = hidden
    dact_ref[...] = dact


def outer_kernel(size, left_ref, right_ref, out_hbm, out_ref, sems):
    copies = []
    for place in range(left_ref.shape[1] // size):
        part = slice(place * size, (place + 1) * size)
        out_ref[0, part] = dot(left_ref[:, part], right_ref[...], ((0,), (0,))).astype(BF)
        copy = pltpu.make_async_copy(
            out_ref.at[:, pl.ds(place * size, size)], out_hbm.at[:, pl.ds(place * size, size)],
            sems.at[place],
        )
        copy.start()
        copies.append(copy)
    for copy in copies:
        copy.wait()


def middle_kernel(
    plan, sizes, back_ref, tok_ref, grad_ref, logit_ref, inv_ref, router_ref, scale_ref,
    sums_ref, outs_ref, coef_ref, mix_ref, signal_ref,
):
    experts, width = router_ref.shape
    sums = pick(itself, 2 * experts, load_blocks(back_ref), in_order(expert_rows(plan, experts), BACK_ORDER, sizes))
    extras = sums[:experts, width:] + sums[experts:, width:]
    den = extras[:, :1] * (1.0 / (plan[0] * plan[1]))
    corr = extras[:, 1:2]
    ys = sums[:experts, :width].astype(BF)
    dxs = sums[experts:, :width].astype(BF)
    router_f, inv_p, scale = slot_column(router_ref, scale_ref)
    tok = tok_ref[0]
    logit = logit_ref[...]
    inv_x = inv_ref[...]
    expo, comb = softmax(logit)
    dcomb = dot(ys, grad_ref[0], ((1,), (1,)))
    ddisp = dot(dxs, tok, ((1,), (1,)))
    dlc = comb * (dcomb - jnp.sum(comb * dcomb, 0, keepdims=True))
    grad_l = expo / den * (ddisp - corr) + dlc
    product = grad_l * logit
    grad_q = (grad_l * inv_x * (inv_p * scale)).astype(BF)
    outer = dot(grad_q, tok, ((1,), (0,)))
    total = jnp.sum(product, 1, keepdims=True)
    local = outer - inv_p * inv_p * total * router_f
    sums_ref[...] = jnp.concatenate([local, total / scale * lane_factor((experts, LANES))], 1)
    outs_ref[...] = ys
    coef_ref[...] = jnp.concatenate([expo, grad_q.astype(F32)], 0).astype(BF)
    mix_ref[...] = jnp.concatenate([dxs.astype(F32) / den, router_f], 0).astype(BF)
    signal_ref[...] = inv_x * inv_x * jnp.sum(product, 0, keepdims=True)


def tail_kernel(tok_ref, logit_ref, outs_ref, coef_ref, mix_ref, signal_ref, combined_ref, grads_ref):
    _, comb = softmax(logit_ref[...])
    combined_ref[0] = dot(comb.astype(BF), outs_ref[...], ((0,), (0,))).astype(BF)
    signal = signal_ref[...]
    column = jnp.transpose(jnp.broadcast_to(signal, (LANES, signal.shape[1])))[:, :1]
    grads = dot(coef_ref[...], mix_ref[...], ((0,), (0,)))
    grads_ref[0] = (grads - column * tok_ref[0].astype(F32)).astype(BF)


def last_kernel(own_ref, other_ref, *refs):
    *more, router_ref, scale_ref = refs
    sums = own_ref[...].astype(F32) + other_ref[...].astype(F32)
    if more:
        sums = sums + (more[0][...].astype(F32) + more[1][...].astype(F32))
    experts, width = router_ref.shape
    router_ref[...] = sums[:, :width]
    eye = iota((experts, experts), 0) == iota((experts, experts), 1)
    scale = jnp.sum(sums[:, width:] / lane_factor((experts, LANES)), 1, keepdims=True) * (1.0 / LANES)
    scale_ref[...] = jnp.sum(jnp.where(eye, scale, 0.0), 0, keepdims=True)


def call(kernel, outs, *args, stays=(), buffers=(), flops=10**7, room=24 * 2**20, home=pltpu.VMEM):
    specs = [pl.BlockSpec(memory_space=pltpu.VMEM)] * len(args)
    args = list(args)
    for place in stays:
        specs[place] = pl.BlockSpec(memory_space=pltpu.HBM)
        args[place] = pltpu.with_memory_space_constraint(args[place], pltpu.HBM)
    return pl.pallas_call(
        kernel,
        out_shape=[jax.ShapeDtypeStruct(shape, dtype) for shape, dtype in outs],
        in_specs=specs,
        out_specs=[pl.BlockSpec(memory_space=home)] * len(outs),
        scratch_shapes=buffers,
        compiler_params=pltpu.CompilerParams(vmem_limit_bytes=room),
        cost_estimate=pl.CostEstimate(
            flops=flops, bytes_accessed=sum(a.size * a.dtype.itemsize for a in args), transcendentals=0
        ),
    )(*args)


def weight_grad(left, right):
    size = 256
    shape = (1, left.shape[1], right.shape[1])
    (out,) = call(
        functools.partial(outer_kernel, size), [(shape, BF)], left, right,
        buffers=[pltpu.VMEM(shape, BF), pltpu.SemaphoreType.DMA((shape[1] // size,))],
        flops=10**9, home=pltpu.HBM,
    )
    return out


def exchange(block, axes):
    return lax.all_to_all(block, axes, split_axis=0, concat_axis=0, tiled=True)


def pair(term, mask, devices):
    return lax.ppermute(term, BOTH, [(d, d ^ mask) for d in range(devices)])


def sum_everywhere(term, devices, beside):
    done = []

    def together(value):
        if len(done) < len(beside):
            value, ready = lax.optimization_barrier((value, beside[len(done)]))
            done.append(ready)
        return value

    term = term + together(pair(term, 2, devices))
    masks = [1] + [1 << place for place in range(2, log2(devices))]
    rounds = [masks[place : place + 2] for place in range(0, len(masks), 2)]
    for group in rounds:
        if group is not rounds[0]:
            term = (terms[0].astype(F32) + terms[1].astype(F32)) + (
                terms[2].astype(F32) + terms[3].astype(F32)
            )
        own = term.astype(BF)
        steps = [group[1], group[0], group[0] ^ group[1]] if len(group) == 2 else group
        terms = [own] + [pair(own, mask, devices) for mask in steps]
        terms[-1] = together(terms[-1])
    return terms, done + beside[len(done) :]


def shards(sizes, tokens, grad_out, router, slot_scale, w_in, w_out):
    images, halves = sizes["far"] * sizes["near"], sizes["tok"]
    devices = images * halves
    tok_rows, width = tokens.shape[1:]
    experts = router.shape[1]
    plan = (images // experts, halves)
    hidden_dev = w_in.shape[2]
    long = width + LANES
    router_t = router.T
    scale_row = slot_scale.reshape(1, experts)
    inputs = (tokens, grad_out, router_t, scale_row)
    sent, logit, inv_x = call(
        functools.partial(front_kernel, plan, sizes),
        [((devices, 2, long), BF), ((experts, tok_rows), F32), ((1, tok_rows), F32)],
        *inputs,
        stays=range(4),
        buffers=[pltpu.VMEM(a.shape, a.dtype) for a in inputs] + [pltpu.SemaphoreType.DMA((4,))],
        flops=FRONT,
    )
    got = exchange(sent, OUT_ORDER)
    back, rows, grad_rows, hidden, dact = call(
        functools.partial(expert_kernel, images, halves, sizes),
        [((devices, 2, long), BF), ((images, width), BF), ((images, width), BF),
         ((images, hidden_dev), BF), ((images, hidden_dev), BF)],
        got, w_in, w_out,
        flops=10**9,
    )
    back = exchange(back, BACK_ORDER)
    grad_w_in = weight_grad(rows, dact)
    grad_w_out = weight_grad(hidden, grad_rows)
    sums, ys, coef, mix, signal = call(
        functools.partial(middle_kernel, plan, sizes),
        [((experts, long), F32), ((experts, width), BF), ((2 * experts, tok_rows), BF),
         ((2 * experts, width), BF), ((1, tok_rows), F32)],
        back, tokens, grad_out, logit, inv_x, router_t, scale_row,
    )
    combined, grad_tokens = call(
        tail_kernel,
        [(tokens.shape, BF), (tokens.shape, BF)],
        tokens, logit, ys, coef, mix, signal,
    )
    terms, ((combined, grad_tokens), grad_w_in, grad_w_out) = sum_everywhere(
        sums, devices, [(combined, grad_tokens), grad_w_in, grad_w_out]
    )
    grad_router, grad_scale = call(
        last_kernel, [((experts, width), F32), ((1, experts), F32)], *terms
    )
    return (combined, grad_tokens, grad_router.T, grad_scale[0], grad_w_in, grad_w_out)


def solution(mesh):
    images, halves = mesh.shape["img"], mesh.shape["tok"]
    near = min(4, images)
    sizes = {"far": images // near, "near": near, "tok": halves}
    split = jax.sharding.Mesh(mesh.devices.reshape(tuple(sizes.values())), BOTH)
    img = ("far", "near")

    def body(*args):
        return shards(sizes, *args)

    placed = (
        P(img, "tok", None),
        P(img, "tok", None),
        P(),
        P(),
        P(img, None, "tok"),
        P(img, "tok", None),
    )
    return jax.shard_map(body, mesh=split, in_specs=placed, out_specs=placed, check_vma=False)
```

```python
import functools

import jax
import jax.numpy as jnp
from jax import lax
from jax.experimental import pallas as pl
from jax.experimental.pallas import tpu as pltpu
from jax.sharding import PartitionSpec as P

EPSILON = 1e-06
ROOT_HALF = 0.7071067811865476
DENSITY = 0.3989422804014327
BF = jnp.bfloat16
F32 = jnp.float32
BOTH = ("img", "tok")
LANES = 128
FRONT = 4 * 10**9


def dot(left, right, dims):
    return lax.dot_general(left, right, (dims, ((), ())), preferred_element_type=F32)


def log2(size):
    assert size & (size - 1) == 0
    return size.bit_length() - 1


def iota(shape, axis):
    return lax.broadcasted_iota(jnp.int32, shape, axis)


def digits(row, sizes):
    out = []
    for size in reversed(sizes):
        out.append(row & (size - 1))
        row = row >> log2(size)
    return out[::-1]


def selection(shape, row_key, column_key):
    hit = row_key(iota(shape, 0)) == column_key(iota(shape, 1))
    return jnp.where(hit, 1.0, 0.0).astype(BF)


def pick(left_key, left_size, right, right_key):
    return dot(selection((left_size, right.shape[0]), left_key, right_key), right, ((1,), (0,)))


def store_copies(ref, rows):
    pairs = rows.astype(BF).reshape(rows.shape[0] // 2, 2, rows.shape[1])
    for start in range(0, ref.shape[0], pairs.shape[0]):
        ref[start : start + pairs.shape[0]] = pairs


def load_blocks(ref):
    return ref[...].reshape(2 * ref.shape[0], ref.shape[2])


def itself(row):
    return row


def as_column(row):
    size = row.shape[1]
    eye = iota((size, size), 0) == iota((size, size), 1)
    return jnp.sum(jnp.where(eye, row, 0.0), 1, keepdims=True)


def lane_pair(extras):
    lane = iota((extras[0].shape[0], LANES), 1)
    high = jnp.zeros(lane.shape, F32)
    low = jnp.zeros(lane.shape, F32)
    for place, value in enumerate(extras):
        top = value.astype(BF).astype(F32)
        high = jnp.where(lane == place, top, high)
        low = jnp.where(lane == place, value - top, low)
    return high, low


def pick_pairs(rows, kind):
    hit = iota((2 * rows.shape[0], rows.shape[0]), 0) == 2 * iota((2 * rows.shape[0], rows.shape[0]), 1) + kind
    return dot(jnp.where(hit, 1.0, 0.0).astype(BF), rows, ((1,), (0,)))


def slot_column(router_ref, scale_ref):
    router_f = router_ref[...].astype(F32)
    inv_p = lax.rsqrt(jnp.sum(router_f * router_f, 1, keepdims=True) + EPSILON)
    scale = as_column(scale_ref[...])
    return router_f, inv_p, scale


def softmax(logit):
    expo = jnp.exp(logit)
    return expo, expo / jnp.sum(expo, 0, keepdims=True)


def fetch(sources, targets, sems):
    copies = [
        pltpu.make_async_copy(source, target, sems.at[place])
        for place, (source, target) in enumerate(zip(sources, targets))
    ]
    for copy in copies:
        copy.start()
    return copies


def expert_rows(plan, experts):
    copies, halves = plan

    def key(row):
        _, place, _, kind = digits(row, (copies, experts, halves, 2))
        return kind * experts + place

    return key


def half_first(key, inner, halves):
    def moved(row):
        half, place, kind = digits(row, (halves, inner, 2))
        return key((place * halves + half) * 2 + kind)

    return moved


def image_rows(images, halves):
    def key(row):
        place, _, kind = digits(row, (images, halves, 2))
        return kind * images + place

    return key


def lane_factor(shape):
    return 1.0 + iota(shape, 1).astype(F32) * (1.0 / LANES)


def front_kernel(
    plan, tok_hbm, grad_hbm, router_hbm, scale_hbm, sent_ref, logit_ref, inv_ref,
    tok_ref, grad_ref, router_ref, scale_ref, sems,
):
    arrived = fetch(
        [tok_hbm, router_hbm, scale_hbm, grad_hbm], [tok_ref, router_ref, scale_ref, grad_ref], sems
    )
    for copy in arrived[:3]:
        copy.wait()
    tok = tok_ref[0]
    experts = router_ref.shape[0]
    square = tok.astype(F32) * tok.astype(F32)
    top = square.astype(BF)
    ones = jnp.ones((8, tok.shape[1]), BF)
    norm = dot(ones, top, ((1,), (1,))) + dot(ones, (square - top.astype(F32)).astype(BF), ((1,), (1,)))
    inv_x = lax.rsqrt(norm[:1] + EPSILON)
    _, inv_p, scale = slot_column(router_ref, scale_ref)
    raw = dot(router_ref[...], tok, ((1,), (1,)))
    logit = raw * inv_x * (inv_p * scale)
    expo, comb = softmax(logit)
    first = pick_pairs(expo.astype(BF), 0)
    second = pick_pairs(comb.astype(BF), 1)
    high, low = lane_pair([jnp.sum(expo, 1, keepdims=True)])
    extras = pick_pairs(high.astype(BF), 0) + pick_pairs(low.astype(BF), 1)
    numer = dot(first.astype(BF), tok, ((1,), (0,)))
    arrived[3].wait()
    dys = dot(second.astype(BF), grad_ref[0], ((1,), (0,)))
    store_copies(sent_ref, jnp.concatenate([numer + dys, extras], 1))
    logit_ref[...] = logit
    inv_ref[...] = inv_x


def expert_kernel(
    images, halves, got_ref, one_ref, two_ref, back_ref, rows_ref, grad_rows_ref, hidden_ref, dact_ref
):
    width = one_ref.shape[1]
    key = image_rows(images, halves)
    sums = pick(itself, 2 * images, load_blocks(got_ref), half_first(key, images, halves))
    den = sums[:images, width : width + 1] + sums[images:, width : width + 1]
    rows = (sums[:images, :width] / den).astype(BF)
    grad_rows = sums[images:, :width].astype(BF)
    act = dot(rows, one_ref[0], ((1,), (0,)))
    grad_h = dot(grad_rows, two_ref[0], ((1,), (1,)))
    phi = 0.5 * (1.0 + lax.erf(act * ROOT_HALF))
    hidden = (act * phi).astype(BF)
    dact = (grad_h * (phi + act * jnp.exp(-0.5 * act * act) * DENSITY)).astype(BF)
    out_part = dot(hidden, two_ref[0], ((1,), (0,)))
    in_part = dot(dact, one_ref[0], ((1,), (1,)))
    corr = jnp.sum(dact.astype(F32) * act, 1, keepdims=True)
    high, low = lane_pair([den, corr])
    first = jnp.concatenate([out_part, high], 1).astype(BF)
    second = jnp.concatenate([in_part, low], 1).astype(BF)
    store_copies(back_ref, pick_pairs(first, 0) + pick_pairs(second, 1))
    rows_ref[...] = rows
    grad_rows_ref[...] = grad_rows
    hidden_ref[...] = hidden
    dact_ref[...] = dact


def outer_kernel(size, left_ref, right_ref, out_hbm, out_ref, sems):
    copies = []
    for place in range(left_ref.shape[1] // size):
        part = slice(place * size, (place + 1) * size)
        out_ref[0, part] = dot(left_ref[:, part], right_ref[...], ((0,), (0,))).astype(BF)
        copy = pltpu.make_async_copy(
            out_ref.at[:, pl.ds(place * size, size)], out_hbm.at[:, pl.ds(place * size, size)],
            sems.at[place],
        )
        copy.start()
        copies.append(copy)
    for copy in copies:
        copy.wait()


def middle_kernel(
    plan, back_ref, tok_ref, grad_ref, logit_ref, inv_ref, router_ref, scale_ref,
    sums_ref, outs_ref, coef_ref, mix_ref, signal_ref,
):
    experts, width = router_ref.shape
    source = half_first(expert_rows(plan, experts), plan[0] * experts, plan[1])
    sums = pick(itself, 2 * experts, load_blocks(back_ref), source)
    extras = sums[:experts, width:] + sums[experts:, width:]
    den = extras[:, :1] * (1.0 / (plan[0] * plan[1]))
    corr = extras[:, 1:2]
    ys = sums[:experts, :width].astype(BF)
    dxs = sums[experts:, :width].astype(BF)
    router_f, inv_p, scale = slot_column(router_ref, scale_ref)
    tok = tok_ref[0]
    logit = logit_ref[...]
    inv_x = inv_ref[...]
    expo, comb = softmax(logit)
    dcomb = dot(ys, grad_ref[0], ((1,), (1,)))
    ddisp = dot(dxs, tok, ((1,), (1,)))
    dlc = comb * (dcomb - jnp.sum(comb * dcomb, 0, keepdims=True))
    grad_l = expo / den * (ddisp - corr) + dlc
    product = grad_l * logit
    grad_q = (grad_l * inv_x * (inv_p * scale)).astype(BF)
    outer = dot(grad_q, tok, ((1,), (0,)))
    total = jnp.sum(product, 1, keepdims=True)
    local = outer - inv_p * inv_p * total * router_f
    sums_ref[...] = jnp.concatenate([local, total / scale * lane_factor((experts, LANES))], 1)
    outs_ref[...] = ys
    coef_ref[...] = jnp.concatenate([expo, grad_q.astype(F32)], 0).astype(BF)
    mix_ref[...] = jnp.concatenate([dxs.astype(F32) / den, router_f], 0).astype(BF)
    signal_ref[...] = inv_x * inv_x * jnp.sum(product, 0, keepdims=True)


def tail_kernel(tok_ref, logit_ref, outs_ref, coef_ref, mix_ref, signal_ref, combined_ref, grads_ref):
    _, comb = softmax(logit_ref[...])
    combined_ref[0] = dot(comb.astype(BF), outs_ref[...], ((0,), (0,))).astype(BF)
    signal = signal_ref[...]
    column = jnp.transpose(jnp.broadcast_to(signal, (LANES, signal.shape[1])))[:, :1]
    grads = dot(coef_ref[...], mix_ref[...], ((0,), (0,)))
    grads_ref[0] = (grads - column * tok_ref[0].astype(F32)).astype(BF)


def last_kernel(own_ref, other_ref, *refs):
    *more, router_ref, scale_ref = refs
    sums = own_ref[...].astype(F32) + other_ref[...].astype(F32)
    if more:
        sums = sums + (more[0][...].astype(F32) + more[1][...].astype(F32))
    experts, width = router_ref.shape
    router_ref[...] = sums[:, :width]
    eye = iota((experts, experts), 0) == iota((experts, experts), 1)
    scale = jnp.sum(sums[:, width:] / lane_factor((experts, LANES)), 1, keepdims=True) * (1.0 / LANES)
    scale_ref[...] = jnp.sum(jnp.where(eye, scale, 0.0), 0, keepdims=True)


def call(kernel, outs, *args, stays=(), buffers=(), flops=10**7, room=24 * 2**20, home=pltpu.VMEM):
    specs = [pl.BlockSpec(memory_space=pltpu.VMEM)] * len(args)
    args = list(args)
    for place in stays:
        specs[place] = pl.BlockSpec(memory_space=pltpu.HBM)
        args[place] = pltpu.with_memory_space_constraint(args[place], pltpu.HBM)
    return pl.pallas_call(
        kernel,
        out_shape=[jax.ShapeDtypeStruct(shape, dtype) for shape, dtype in outs],
        in_specs=specs,
        out_specs=[pl.BlockSpec(memory_space=home)] * len(outs),
        scratch_shapes=buffers,
        compiler_params=pltpu.CompilerParams(vmem_limit_bytes=room),
        cost_estimate=pl.CostEstimate(
            flops=flops, bytes_accessed=sum(a.size * a.dtype.itemsize for a in args), transcendentals=0
        ),
    )(*args)


def weight_grad(left, right):
    size = 256
    shape = (1, left.shape[1], right.shape[1])
    (out,) = call(
        functools.partial(outer_kernel, size), [(shape, BF)], left, right,
        buffers=[pltpu.VMEM(shape, BF), pltpu.SemaphoreType.DMA((shape[1] // size,))],
        flops=10**9, home=pltpu.HBM,
    )
    return out


def exchange(block, axes):
    return lax.all_to_all(block, axes, split_axis=0, concat_axis=0, tiled=True)


def pair(term, mask, devices):
    return lax.ppermute(term, BOTH, [(d, d ^ mask) for d in range(devices)])


def sum_everywhere(term, devices, beside):
    done = []

    def together(value):
        if len(done) < len(beside):
            value, ready = lax.optimization_barrier((value, beside[len(done)]))
            done.append(ready)
        return value

    term = term + together(pair(term, 2, devices))
    masks = [1] + [1 << place for place in range(2, log2(devices))]
    rounds = [masks[place : place + 2] for place in range(0, len(masks), 2)]
    for group in rounds:
        if group is not rounds[0]:
            term = (terms[0].astype(F32) + terms[1].astype(F32)) + (
                terms[2].astype(F32) + terms[3].astype(F32)
            )
        own = term.astype(BF)
        steps = [group[1], group[0], group[0] ^ group[1]] if len(group) == 2 else group
        terms = [own] + [pair(own, mask, devices) for mask in steps]
        terms[-1] = together(terms[-1])
    return terms, done + beside[len(done) :]


def shards(images, halves, tokens, grad_out, router, slot_scale, w_in, w_out):
    devices = images * halves
    tok_rows, width = tokens.shape[1:]
    experts = router.shape[1]
    plan = (images // experts, halves)
    hidden_dev = w_in.shape[2]
    long = width + LANES
    router_t = router.T
    scale_row = slot_scale.reshape(1, experts)
    inputs = (tokens, grad_out, router_t, scale_row)
    sent, logit, inv_x = call(
        functools.partial(front_kernel, plan),
        [((devices, 2, long), BF), ((experts, tok_rows), F32), ((1, tok_rows), F32)],
        *inputs,
        stays=range(4),
        buffers=[pltpu.VMEM(a.shape, a.dtype) for a in inputs] + [pltpu.SemaphoreType.DMA((4,))],
        flops=FRONT,
    )
    got = exchange(sent, ("tok", "img"))
    back, rows, grad_rows, hidden, dact = call(
        functools.partial(expert_kernel, images, halves),
        [((devices, 2, long), BF), ((images, width), BF), ((images, width), BF),
         ((images, hidden_dev), BF), ((images, hidden_dev), BF)],
        got, w_in, w_out,
        flops=10**9,
    )
    back = exchange(back, ("tok", "img"))
    grad_w_in = weight_grad(rows, dact)
    grad_w_out = weight_grad(hidden, grad_rows)
    sums, ys, coef, mix, signal = call(
        functools.partial(middle_kernel, plan),
        [((experts, long), F32), ((experts, width), BF), ((2 * experts, tok_rows), BF),
         ((2 * experts, width), BF), ((1, tok_rows), F32)],
        back, tokens, grad_out, logit, inv_x, router_t, scale_row,
    )
    combined, grad_tokens = call(
        tail_kernel,
        [(tokens.shape, BF), (tokens.shape, BF)],
        tokens, logit, ys, coef, mix, signal,
    )
    terms, ((combined, grad_tokens), grad_w_in, grad_w_out) = sum_everywhere(
        sums, devices, [(combined, grad_tokens), grad_w_in, grad_w_out]
    )
    grad_router, grad_scale = call(
        last_kernel, [((experts, width), F32), ((1, experts), F32)], *terms
    )
    return (combined, grad_tokens, grad_router.T, grad_scale[0], grad_w_in, grad_w_out)


def solution(mesh):
    images, halves = mesh.shape["img"], mesh.shape["tok"]

    def body(*args):
        return shards(images, halves, *args)

    return jax.shard_map(
        body,
        mesh=mesh,
        in_specs=(
            P("img", "tok", None),
            P("img", "tok", None),
            P(),
            P(),
            P("img", None, "tok"),
            P("img", "tok", None),
        ),
        out_specs=(
            P("img", "tok", None),
            P("img", "tok", None),
            P(),
            P(),
            P("img", None, "tok"),
            P("img", "tok", None),
        ),
        check_vma=False,
    )
```

```python
import functools

import jax
import jax.numpy as jnp
from jax import lax
from jax.experimental import pallas as pl
from jax.experimental.pallas import tpu as pltpu
from jax.sharding import PartitionSpec as P

EPSILON = 1e-06
ROOT_HALF = 0.7071067811865476
DENSITY = 0.3989422804014327
BF = jnp.bfloat16
F32 = jnp.float32
BOTH = ("img", "tok")
LANES = 128
FRONT = 4 * 10**9


def dot(left, right, dims):
    return lax.dot_general(left, right, (dims, ((), ())), preferred_element_type=F32)


def log2(size):
    assert size & (size - 1) == 0
    return size.bit_length() - 1


def iota(shape, axis):
    return lax.broadcasted_iota(jnp.int32, shape, axis)


def digits(row, sizes):
    out = []
    for size in reversed(sizes):
        out.append(row & (size - 1))
        row = row >> log2(size)
    return out[::-1]


def selection(shape, row_key, column_key):
    hit = row_key(iota(shape, 0)) == column_key(iota(shape, 1))
    return jnp.where(hit, 1.0, 0.0).astype(BF)


def pick(left_key, left_size, right, right_key):
    return dot(selection((left_size, right.shape[0]), left_key, right_key), right, ((1,), (0,)))


def store_blocks(ref, rows):
    ref[...] = rows.astype(BF).reshape(ref.shape)


def load_blocks(ref):
    return ref[...].reshape(2 * ref.shape[0], ref.shape[2])


def itself(row):
    return row


def as_column(row):
    size = row.shape[1]
    eye = iota((size, size), 0) == iota((size, size), 1)
    return jnp.sum(jnp.where(eye, row, 0.0), 1, keepdims=True)


def row_of(column):
    return jnp.transpose(jnp.broadcast_to(column, (column.shape[0], LANES)))[:1]


def stack_rows(first, second, extras):
    lane = iota((first.shape[0], LANES), 1)
    high = jnp.zeros(lane.shape, F32)
    low = jnp.zeros(lane.shape, F32)
    for place, value in enumerate(extras):
        top = value.astype(BF).astype(F32)
        high = jnp.where(lane == place, top, high)
        low = jnp.where(lane == place, value - top, low)
    return jnp.concatenate(
        [jnp.concatenate([first, high], 1), jnp.concatenate([second, low], 1)], 0
    ).astype(BF)


def slot_column(router_ref, scale_ref):
    router_f = router_ref[...].astype(F32)
    inv_p = lax.rsqrt(jnp.sum(router_f * router_f, 1, keepdims=True) + EPSILON)
    scale = as_column(scale_ref[...])
    return router_f, inv_p, scale


def softmax(logit):
    expo = jnp.exp(logit)
    return expo, expo / jnp.sum(expo, 0, keepdims=True)


def fetch(sources, targets, sems):
    copies = [
        pltpu.make_async_copy(source, target, sems.at[place])
        for place, (source, target) in enumerate(zip(sources, targets))
    ]
    for copy in copies:
        copy.start()
    return copies


def expert_rows(plan, experts):
    copies, halves = plan

    def key(row):
        _, place, _, kind = digits(row, (copies, experts, halves, 2))
        return kind * experts + place

    return key


def half_first(key, inner, halves):
    def moved(row):
        half, place, kind = digits(row, (halves, inner, 2))
        return key((place * halves + half) * 2 + kind)

    return moved


def image_rows(images, halves):
    def key(row):
        place, _, kind = digits(row, (images, halves, 2))
        return kind * images + place

    return key


def lane_factor(shape):
    return 1.0 + iota(shape, 1).astype(F32) * (1.0 / LANES)


def front_kernel(
    plan, tok_hbm, grad_hbm, router_hbm, scale_hbm, sent_ref, logit_ref, inv_ref,
    tok_ref, grad_ref, router_ref, scale_ref, sems,
):
    arrived = fetch(
        [tok_hbm, router_hbm, scale_hbm, grad_hbm], [tok_ref, router_ref, scale_ref, grad_ref], sems
    )
    for copy in arrived[:3]:
        copy.wait()
    tok = tok_ref[0]
    tok_f = tok.astype(F32)
    inv_x = row_of(lax.rsqrt(jnp.sum(tok_f * tok_f, 1, keepdims=True) + EPSILON))
    _, inv_p, scale = slot_column(router_ref, scale_ref)
    raw = dot(router_ref[...], tok, ((1,), (1,)))
    logit = raw * inv_x * (inv_p * scale)
    expo, comb = softmax(logit)
    numer = dot(expo.astype(BF), tok, ((1,), (0,)))
    arrived[3].wait()
    dys = dot(comb.astype(BF), grad_ref[0], ((1,), (0,)))
    rows = stack_rows(numer, dys, [jnp.sum(expo, 1, keepdims=True)])
    experts = router_ref.shape[0]
    key = half_first(expert_rows(plan, experts), plan[0] * experts, plan[1])
    store_blocks(sent_ref, pick(key, 2 * sent_ref.shape[0], rows, itself))
    logit_ref[...] = logit
    inv_ref[...] = inv_x


def expert_kernel(
    images, halves, got_ref, one_ref, two_ref, back_ref, rows_ref, grad_rows_ref, hidden_ref, dact_ref
):
    width = one_ref.shape[1]
    key = half_first(image_rows(images, halves), images, halves)
    sums = pick(itself, 2 * images, load_blocks(got_ref), key)
    den = sums[:images, width : width + 1] + sums[images:, width : width + 1]
    rows = (sums[:images, :width] / den).astype(BF)
    grad_rows = sums[images:, :width].astype(BF)
    act = dot(rows, one_ref[0], ((1,), (0,)))
    grad_h = dot(grad_rows, two_ref[0], ((1,), (1,)))
    phi = 0.5 * (1.0 + lax.erf(act * ROOT_HALF))
    hidden = (act * phi).astype(BF)
    dact = (grad_h * (phi + act * jnp.exp(-0.5 * act * act) * DENSITY)).astype(BF)
    out_part = dot(hidden, two_ref[0], ((1,), (0,)))
    in_part = dot(dact, one_ref[0], ((1,), (1,)))
    corr = jnp.sum(dact.astype(F32) * act, 1, keepdims=True)
    packed = stack_rows(out_part, in_part, [den, corr])
    store_blocks(back_ref, pick(key, 2 * back_ref.shape[0], packed, itself))
    rows_ref[...] = rows
    grad_rows_ref[...] = grad_rows
    hidden_ref[...] = hidden
    dact_ref[...] = dact


def outer_kernel(size, left_ref, right_ref, out_hbm, out_ref, sems):
    copies = []
    for place in range(left_ref.shape[1] // size):
        part = slice(place * size, (place + 1) * size)
        out_ref[0, part] = dot(left_ref[:, part], right_ref[...], ((0,), (0,))).astype(BF)
        copy = pltpu.make_async_copy(
            out_ref.at[:, pl.ds(place * size, size)], out_hbm.at[:, pl.ds(place * size, size)],
            sems.at[place],
        )
        copy.start()
        copies.append(copy)
    for copy in copies:
        copy.wait()


def middle_kernel(
    plan, back_ref, tok_ref, grad_ref, logit_ref, inv_ref, router_ref, scale_ref,
    sums_ref, outs_ref, coef_ref, mix_ref, signal_ref,
):
    experts, width = router_ref.shape
    source = half_first(expert_rows(plan, experts), plan[0] * experts, plan[1])
    sums = pick(itself, 2 * experts, load_blocks(back_ref), source)
    extras = sums[:experts, width:] + sums[experts:, width:]
    den = extras[:, :1] * (1.0 / (plan[0] * plan[1]))
    corr = extras[:, 1:2]
    ys = sums[:experts, :width].astype(BF)
    dxs = sums[experts:, :width].astype(BF)
    router_f, inv_p, scale = slot_column(router_ref, scale_ref)
    tok = tok_ref[0]
    logit = logit_ref[...]
    inv_x = inv_ref[...]
    expo, comb = softmax(logit)
    dcomb = dot(ys, grad_ref[0], ((1,), (1,)))
    ddisp = dot(dxs, tok, ((1,), (1,)))
    dlc = comb * (dcomb - jnp.sum(comb * dcomb, 0, keepdims=True))
    grad_l = expo / den * (ddisp - corr) + dlc
    product = grad_l * logit
    grad_q = (grad_l * inv_x * (inv_p * scale)).astype(BF)
    outer = dot(grad_q, tok, ((1,), (0,)))
    total = jnp.sum(product, 1, keepdims=True)
    local = outer - inv_p * inv_p * total * router_f
    sums_ref[...] = jnp.concatenate([local, total / scale * lane_factor((experts, LANES))], 1)
    outs_ref[...] = ys
    coef_ref[...] = jnp.concatenate([expo, grad_q.astype(F32)], 0).astype(BF)
    mix_ref[...] = jnp.concatenate([dxs.astype(F32) / den, router_f], 0).astype(BF)
    signal_ref[...] = inv_x * inv_x * jnp.sum(product, 0, keepdims=True)


def tail_kernel(tok_ref, logit_ref, outs_ref, coef_ref, mix_ref, signal_ref, combined_ref, grads_ref):
    _, comb = softmax(logit_ref[...])
    combined_ref[0] = dot(comb.astype(BF), outs_ref[...], ((0,), (0,))).astype(BF)
    signal = signal_ref[...]
    column = jnp.transpose(jnp.broadcast_to(signal, (LANES, signal.shape[1])))[:, :1]
    grads = dot(coef_ref[...], mix_ref[...], ((0,), (0,)))
    grads_ref[0] = (grads - column * tok_ref[0].astype(F32)).astype(BF)


def last_kernel(own_ref, other_ref, *refs):
    *more, router_ref, scale_ref = refs
    sums = own_ref[...].astype(F32) + other_ref[...].astype(F32)
    if more:
        sums = sums + (more[0][...].astype(F32) + more[1][...].astype(F32))
    experts, width = router_ref.shape
    router_ref[...] = sums[:, :width]
    eye = iota((experts, experts), 0) == iota((experts, experts), 1)
    scale = jnp.sum(sums[:, width:] / lane_factor((experts, LANES)), 1, keepdims=True) * (1.0 / LANES)
    scale_ref[...] = jnp.sum(jnp.where(eye, scale, 0.0), 0, keepdims=True)


def call(kernel, outs, *args, stays=(), buffers=(), flops=10**7, room=24 * 2**20, home=pltpu.VMEM):
    specs = [pl.BlockSpec(memory_space=pltpu.VMEM)] * len(args)
    args = list(args)
    for place in stays:
        specs[place] = pl.BlockSpec(memory_space=pltpu.HBM)
        args[place] = pltpu.with_memory_space_constraint(args[place], pltpu.HBM)
    return pl.pallas_call(
        kernel,
        out_shape=[jax.ShapeDtypeStruct(shape, dtype) for shape, dtype in outs],
        in_specs=specs,
        out_specs=[pl.BlockSpec(memory_space=home)] * len(outs),
        scratch_shapes=buffers,
        compiler_params=pltpu.CompilerParams(vmem_limit_bytes=room),
        cost_estimate=pl.CostEstimate(
            flops=flops, bytes_accessed=sum(a.size * a.dtype.itemsize for a in args), transcendentals=0
        ),
    )(*args)


def weight_grad(left, right):
    size = 256
    shape = (1, left.shape[1], right.shape[1])
    (out,) = call(
        functools.partial(outer_kernel, size), [(shape, BF)], left, right,
        buffers=[pltpu.VMEM(shape, BF), pltpu.SemaphoreType.DMA((shape[1] // size,))],
        flops=10**9, home=pltpu.HBM,
    )
    return out


def exchange(block, axes):
    return lax.all_to_all(block, axes, split_axis=0, concat_axis=0, tiled=True)


def pair(term, mask, devices):
    return lax.ppermute(term, BOTH, [(d, d ^ mask) for d in range(devices)])


def sum_everywhere(term, devices, beside):
    done = []

    def together(value):
        if len(done) < len(beside):
            value, ready = lax.optimization_barrier((value, beside[len(done)]))
            done.append(ready)
        return value

    term = term + together(pair(term, 2, devices))
    masks = [1] + [1 << place for place in range(2, log2(devices))]
    rounds = [masks[place : place + 2] for place in range(0, len(masks), 2)]
    for group in rounds:
        if group is not rounds[0]:
            term = (terms[0].astype(F32) + terms[1].astype(F32)) + (
                terms[2].astype(F32) + terms[3].astype(F32)
            )
        own = term.astype(BF)
        steps = [group[1], group[0], group[0] ^ group[1]] if len(group) == 2 else group
        terms = [own] + [pair(own, mask, devices) for mask in steps]
        terms[-1] = together(terms[-1])
    return terms, done + beside[len(done) :]


def shards(images, halves, tokens, grad_out, router, slot_scale, w_in, w_out):
    devices = images * halves
    tok_rows, width = tokens.shape[1:]
    experts = router.shape[1]
    plan = (images // experts, halves)
    hidden_dev = w_in.shape[2]
    long = width + LANES
    router_t = router.T
    scale_row = slot_scale.reshape(1, experts)
    inputs = (tokens, grad_out, router_t, scale_row)
    sent, logit, inv_x = call(
        functools.partial(front_kernel, plan),
        [((devices, 2, long), BF), ((experts, tok_rows), F32), ((1, tok_rows), F32)],
        *inputs,
        stays=range(4),
        buffers=[pltpu.VMEM(a.shape, a.dtype) for a in inputs] + [pltpu.SemaphoreType.DMA((4,))],
        flops=FRONT,
    )
    got = exchange(sent, ("tok", "img"))
    back, rows, grad_rows, hidden, dact = call(
        functools.partial(expert_kernel, images, halves),
        [((devices, 2, long), BF), ((images, width), BF), ((images, width), BF),
         ((images, hidden_dev), BF), ((images, hidden_dev), BF)],
        got, w_in, w_out,
        flops=10**9,
    )
    back = exchange(back, ("tok", "img"))
    grad_w_in = weight_grad(rows, dact)
    grad_w_out = weight_grad(hidden, grad_rows)
    sums, ys, coef, mix, signal = call(
        functools.partial(middle_kernel, plan),
        [((experts, long), F32), ((experts, width), BF), ((2 * experts, tok_rows), BF),
         ((2 * experts, width), BF), ((1, tok_rows), F32)],
        back, tokens, grad_out, logit, inv_x, router_t, scale_row,
    )
    combined, grad_tokens = call(
        tail_kernel,
        [(tokens.shape, BF), (tokens.shape, BF)],
        tokens, logit, ys, coef, mix, signal,
    )
    terms, ((combined, grad_tokens), grad_w_in, grad_w_out) = sum_everywhere(
        sums, devices, [(combined, grad_tokens), grad_w_in, grad_w_out]
    )
    grad_router, grad_scale = call(
        last_kernel, [((experts, width), F32), ((1, experts), F32)], *terms
    )
    return (combined, grad_tokens, grad_router.T, grad_scale[0], grad_w_in, grad_w_out)


def solution(mesh):
    images, halves = mesh.shape["img"], mesh.shape["tok"]

    def body(*args):
        return shards(images, halves, *args)

    return jax.shard_map(
        body,
        mesh=mesh,
        in_specs=(
            P("img", "tok", None),
            P("img", "tok", None),
            P(),
            P(),
            P("img", None, "tok"),
            P("img", "tok", None),
        ),
        out_specs=(
            P("img", "tok", None),
            P("img", "tok", None),
            P(),
            P(),
            P("img", None, "tok"),
            P("img", "tok", None),
        ),
        check_vma=False,
    )
```

```python
import functools

import jax
import jax.numpy as jnp
from jax import lax
from jax.experimental import pallas as pl
from jax.experimental.pallas import tpu as pltpu
from jax.sharding import PartitionSpec as P

EPSILON = 1e-06
ROOT_HALF = 0.7071067811865476
DENSITY = 0.3989422804014327
BF = jnp.bfloat16
F32 = jnp.float32
BOTH = ("img", "tok")
LANES = 128
FRONT = 4 * 10**9


def dot(left, right, dims):
    return lax.dot_general(left, right, (dims, ((), ())), preferred_element_type=F32)


def log2(size):
    assert size & (size - 1) == 0
    return size.bit_length() - 1


def iota(shape, axis):
    return lax.broadcasted_iota(jnp.int32, shape, axis)


def digits(row, sizes):
    out = []
    for size in reversed(sizes):
        out.append(row & (size - 1))
        row = row >> log2(size)
    return out[::-1]


def selection(shape, row_key, column_key):
    hit = row_key(iota(shape, 0)) == column_key(iota(shape, 1))
    return jnp.where(hit, 1.0, 0.0).astype(BF)


def pick(left_key, left_size, right, right_key):
    return dot(selection((left_size, right.shape[0]), left_key, right_key), right, ((1,), (0,)))


def store_blocks(ref, rows):
    ref[...] = rows.astype(BF).reshape(ref.shape)


def load_blocks(ref):
    return ref[...].reshape(2 * ref.shape[0], ref.shape[2])


def itself(row):
    return row


def as_column(row):
    size = row.shape[1]
    eye = iota((size, size), 0) == iota((size, size), 1)
    return jnp.sum(jnp.where(eye, row, 0.0), 1, keepdims=True)


def row_of(column):
    return jnp.transpose(jnp.broadcast_to(column, (column.shape[0], LANES)))[:1]


def stack_rows(first, second, extras):
    lane = iota((first.shape[0], LANES), 1)
    high = jnp.zeros(lane.shape, F32)
    low = jnp.zeros(lane.shape, F32)
    for place, value in enumerate(extras):
        top = value.astype(BF).astype(F32)
        high = jnp.where(lane == place, top, high)
        low = jnp.where(lane == place, value - top, low)
    return jnp.concatenate(
        [jnp.concatenate([first, high], 1), jnp.concatenate([second, low], 1)], 0
    ).astype(BF)


def slot_column(router_ref, scale_ref):
    router_f = router_ref[...].astype(F32)
    inv_p = lax.rsqrt(jnp.sum(router_f * router_f, 1, keepdims=True) + EPSILON)
    scale = as_column(scale_ref[...])
    return router_f, inv_p, scale


def softmax(logit):
    expo = jnp.exp(logit)
    return expo, expo / jnp.sum(expo, 0, keepdims=True)


def fetch(sources, targets, sems):
    copies = [
        pltpu.make_async_copy(source, target, sems.at[place])
        for place, (source, target) in enumerate(zip(sources, targets))
    ]
    for copy in copies:
        copy.start()
    return copies


def expert_rows(plan, experts):
    copies, halves = plan

    def key(row):
        _, place, _, kind = digits(row, (copies, experts, halves, 2))
        return kind * experts + place

    return key


def half_first(key, inner, halves):
    def moved(row):
        half, place, kind = digits(row, (halves, inner, 2))
        return key((place * halves + half) * 2 + kind)

    return moved


def image_rows(images, halves):
    def key(row):
        place, _, kind = digits(row, (images, halves, 2))
        return kind * images + place

    return key


def lane_factor(shape):
    return 1.0 + iota(shape, 1).astype(F32) * (1.0 / LANES)


def front_kernel(
    plan, tok_hbm, grad_hbm, router_hbm, scale_hbm, sent_ref, logit_ref, inv_ref,
    tok_ref, grad_ref, router_ref, scale_ref, sems,
):
    arrived = fetch(
        [tok_hbm, router_hbm, scale_hbm, grad_hbm], [tok_ref, router_ref, scale_ref, grad_ref], sems
    )
    for copy in arrived[:3]:
        copy.wait()
    tok = tok_ref[0]
    tok_f = tok.astype(F32)
    inv_x = row_of(lax.rsqrt(jnp.sum(tok_f * tok_f, 1, keepdims=True) + EPSILON))
    _, inv_p, scale = slot_column(router_ref, scale_ref)
    raw = dot(router_ref[...], tok, ((1,), (1,)))
    logit = raw * inv_x * (inv_p * scale)
    expo, comb = softmax(logit)
    numer = dot(expo.astype(BF), tok, ((1,), (0,)))
    arrived[3].wait()
    dys = dot(comb.astype(BF), grad_ref[0], ((1,), (0,)))
    rows = stack_rows(numer, dys, [jnp.sum(expo, 1, keepdims=True)])
    experts = router_ref.shape[0]
    key = half_first(expert_rows(plan, experts), plan[0] * experts, plan[1])
    store_blocks(sent_ref, pick(key, 2 * sent_ref.shape[0], rows, itself))
    logit_ref[...] = logit
    inv_ref[...] = inv_x


def expert_kernel(
    images, halves, got_ref, one_ref, two_ref, back_ref, rows_ref, grad_rows_ref, hidden_ref, dact_ref
):
    width = one_ref.shape[1]
    key = half_first(image_rows(images, halves), images, halves)
    sums = pick(itself, 2 * images, load_blocks(got_ref), key)
    den = sums[:images, width : width + 1] + sums[images:, width : width + 1]
    rows = (sums[:images, :width] / den).astype(BF)
    grad_rows = sums[images:, :width].astype(BF)
    act = dot(rows, one_ref[0], ((1,), (0,)))
    grad_h = dot(grad_rows, two_ref[0], ((1,), (1,)))
    phi = 0.5 * (1.0 + lax.erf(act * ROOT_HALF))
    hidden = (act * phi).astype(BF)
    dact = (grad_h * (phi + act * jnp.exp(-0.5 * act * act) * DENSITY)).astype(BF)
    out_part = dot(hidden, two_ref[0], ((1,), (0,)))
    in_part = dot(dact, one_ref[0], ((1,), (1,)))
    corr = jnp.sum(dact.astype(F32) * act, 1, keepdims=True)
    packed = stack_rows(out_part, in_part, [den, corr])
    store_blocks(back_ref, pick(key, 2 * back_ref.shape[0], packed, itself))
    rows_ref[...] = rows
    grad_rows_ref[...] = grad_rows
    hidden_ref[...] = hidden
    dact_ref[...] = dact


def outer_kernel(size, left_ref, right_ref, out_hbm, out_ref, sems):
    copies = []
    for place in range(left_ref.shape[1] // size):
        part = slice(place * size, (place + 1) * size)
        out_ref[0, part] = dot(left_ref[:, part], right_ref[...], ((0,), (0,))).astype(BF)
        copy = pltpu.make_async_copy(
            out_ref.at[:, pl.ds(place * size, size)], out_hbm.at[:, pl.ds(place * size, size)],
            sems.at[place],
        )
        copy.start()
        copies.append(copy)
    for copy in copies:
        copy.wait()


def middle_kernel(
    plan, back_ref, tok_ref, grad_ref, logit_ref, inv_ref, router_ref, scale_ref,
    sums_ref, outs_ref, coef_ref, mix_ref, signal_ref,
):
    experts, width = router_ref.shape
    source = half_first(expert_rows(plan, experts), plan[0] * experts, plan[1])
    sums = pick(itself, 2 * experts, load_blocks(back_ref), source)
    extras = sums[:experts, width:] + sums[experts:, width:]
    den = extras[:, :1] * (1.0 / (plan[0] * plan[1]))
    corr = extras[:, 1:2]
    ys = sums[:experts, :width].astype(BF)
    dxs = sums[experts:, :width].astype(BF)
    router_f, inv_p, scale = slot_column(router_ref, scale_ref)
    tok = tok_ref[0]
    logit = logit_ref[...]
    inv_x = inv_ref[...]
    expo, comb = softmax(logit)
    dcomb = dot(ys, grad_ref[0], ((1,), (1,)))
    ddisp = dot(dxs, tok, ((1,), (1,)))
    dlc = comb * (dcomb - jnp.sum(comb * dcomb, 0, keepdims=True))
    grad_l = expo / den * (ddisp - corr) + dlc
    product = grad_l * logit
    grad_q = (grad_l * inv_x * (inv_p * scale)).astype(BF)
    outer = dot(grad_q, tok, ((1,), (0,)))
    total = jnp.sum(product, 1, keepdims=True)
    local = outer - inv_p * inv_p * total * router_f
    sums_ref[...] = jnp.concatenate([local, total / scale * lane_factor((experts, LANES))], 1)
    outs_ref[...] = ys
    coef_ref[...] = jnp.concatenate([expo, grad_q.astype(F32)], 0).astype(BF)
    mix_ref[...] = jnp.concatenate([dxs.astype(F32) / den, router_f], 0).astype(BF)
    signal_ref[...] = inv_x * inv_x * jnp.sum(product, 0, keepdims=True)


def tail_kernel(tok_ref, logit_ref, outs_ref, coef_ref, mix_ref, signal_ref, combined_ref, grads_ref):
    _, comb = softmax(logit_ref[...])
    combined_ref[0] = dot(comb.astype(BF), outs_ref[...], ((0,), (0,))).astype(BF)
    signal = signal_ref[...]
    column = jnp.transpose(jnp.broadcast_to(signal, (LANES, signal.shape[1])))[:, :1]
    grads = dot(coef_ref[...], mix_ref[...], ((0,), (0,)))
    grads_ref[0] = (grads - column * tok_ref[0].astype(F32)).astype(BF)


def last_kernel(mine_ref, other_ref, router_ref, scale_ref):
    sums = mine_ref[...] + other_ref[...]
    experts, width = router_ref.shape
    router_ref[...] = sums[:, :width]
    eye = iota((experts, experts), 0) == iota((experts, experts), 1)
    scale = jnp.sum(sums[:, width:] / lane_factor((experts, LANES)), 1, keepdims=True) * (1.0 / LANES)
    scale_ref[...] = jnp.sum(jnp.where(eye, scale, 0.0), 0, keepdims=True)


def call(kernel, outs, *args, stays=(), buffers=(), flops=10**7, room=24 * 2**20, home=pltpu.VMEM):
    specs = [pl.BlockSpec(memory_space=pltpu.VMEM)] * len(args)
    args = list(args)
    for place in stays:
        specs[place] = pl.BlockSpec(memory_space=pltpu.HBM)
        args[place] = pltpu.with_memory_space_constraint(args[place], pltpu.HBM)
    return pl.pallas_call(
        kernel,
        out_shape=[jax.ShapeDtypeStruct(shape, dtype) for shape, dtype in outs],
        in_specs=specs,
        out_specs=[pl.BlockSpec(memory_space=home)] * len(outs),
        scratch_shapes=buffers,
        compiler_params=pltpu.CompilerParams(vmem_limit_bytes=room),
        cost_estimate=pl.CostEstimate(
            flops=flops, bytes_accessed=sum(a.size * a.dtype.itemsize for a in args), transcendentals=0
        ),
    )(*args)


def weight_grad(left, right):
    size = 256
    shape = (1, left.shape[1], right.shape[1])
    (out,) = call(
        functools.partial(outer_kernel, size), [(shape, BF)], left, right,
        buffers=[pltpu.VMEM(shape, BF), pltpu.SemaphoreType.DMA((shape[1] // size,))],
        flops=10**9, home=pltpu.HBM,
    )
    return out


def exchange(block, axes):
    return lax.all_to_all(block, axes, split_axis=0, concat_axis=0, tiled=True)


def pair(term, mask, devices):
    return lax.ppermute(term, BOTH, [(d, d ^ mask) for d in range(devices)])


def sum_everywhere(term, devices, beside):
    masks = [1] + [1 << place for place in range(2, log2(devices))]
    rounds = [masks[place : place + 2] for place in range(0, len(masks), 2)]
    done = []

    def together(value):
        if len(done) < len(beside):
            value, ready = lax.optimization_barrier((value, beside[len(done)]))
            done.append(ready)
        return value

    for group in rounds:
        own = term.astype(BF)
        steps = [group[1], group[0], group[0] ^ group[1]] if len(group) == 2 else group
        terms = [own] + [pair(own, mask, devices) for mask in steps]
        terms[-1] = together(terms[-1])
        terms = [value.astype(F32) for value in terms]
        term = terms[0] + terms[1]
        if len(terms) == 4:
            term = term + (terms[2] + terms[3])
    other = together(pair(term, 2, devices))
    return term, other, done + beside[len(done) :]


def shards(images, halves, tokens, grad_out, router, slot_scale, w_in, w_out):
    devices = images * halves
    tok_rows, width = tokens.shape[1:]
    experts = router.shape[1]
    plan = (images // experts, halves)
    hidden_dev = w_in.shape[2]
    long = width + LANES
    router_t = router.T
    scale_row = slot_scale.reshape(1, experts)
    inputs = (tokens, grad_out, router_t, scale_row)
    sent, logit, inv_x = call(
        functools.partial(front_kernel, plan),
        [((devices, 2, long), BF), ((experts, tok_rows), F32), ((1, tok_rows), F32)],
        *inputs,
        stays=range(4),
        buffers=[pltpu.VMEM(a.shape, a.dtype) for a in inputs] + [pltpu.SemaphoreType.DMA((4,))],
        flops=FRONT,
    )
    got = exchange(sent, ("tok", "img"))
    back, rows, grad_rows, hidden, dact = call(
        functools.partial(expert_kernel, images, halves),
        [((devices, 2, long), BF), ((images, width), BF), ((images, width), BF),
         ((images, hidden_dev), BF), ((images, hidden_dev), BF)],
        got, w_in, w_out,
        flops=10**9,
    )
    back = exchange(back, ("tok", "img"))
    grad_w_in = weight_grad(rows, dact)
    grad_w_out = weight_grad(hidden, grad_rows)
    sums, ys, coef, mix, signal = call(
        functools.partial(middle_kernel, plan),
        [((experts, long), F32), ((experts, width), BF), ((2 * experts, tok_rows), BF),
         ((2 * experts, width), BF), ((1, tok_rows), F32)],
        back, tokens, grad_out, logit, inv_x, router_t, scale_row,
    )
    combined, grad_tokens = call(
        tail_kernel,
        [(tokens.shape, BF), (tokens.shape, BF)],
        tokens, logit, ys, coef, mix, signal,
    )
    mine, other, (grad_w_in, grad_w_out, (combined, grad_tokens)) = sum_everywhere(
        sums, devices, [grad_w_in, grad_w_out, (combined, grad_tokens)]
    )
    grad_router, grad_scale = call(
        last_kernel, [((experts, width), F32), ((1, experts), F32)], mine, other
    )
    return (combined, grad_tokens, grad_router.T, grad_scale[0], grad_w_in, grad_w_out)


def solution(mesh):
    images, halves = mesh.shape["img"], mesh.shape["tok"]

    def body(*args):
        return shards(images, halves, *args)

    return jax.shard_map(
        body,
        mesh=mesh,
        in_specs=(
            P("img", "tok", None),
            P("img", "tok", None),
            P(),
            P(),
            P("img", None, "tok"),
            P("img", "tok", None),
        ),
        out_specs=(
            P("img", "tok", None),
            P("img", "tok", None),
            P(),
            P(),
            P("img", None, "tok"),
            P("img", "tok", None),
        ),
        check_vma=False,
    )
```

```python
import functools

import jax
import jax.numpy as jnp
from jax import lax
from jax.experimental import pallas as pl
from jax.experimental.pallas import tpu as pltpu
from jax.sharding import PartitionSpec as P

EPSILON = 1e-06
ROOT_HALF = 0.7071067811865476
DENSITY = 0.3989422804014327
BF = jnp.bfloat16
F32 = jnp.float32
BOTH = ("img", "tok")
LANES = 128
FRONT = 4 * 10**9


def dot(left, right, dims):
    return lax.dot_general(left, right, (dims, ((), ())), preferred_element_type=F32)


def log2(size):
    assert size & (size - 1) == 0
    return size.bit_length() - 1


def iota(shape, axis):
    return lax.broadcasted_iota(jnp.int32, shape, axis)


def digits(row, sizes):
    out = []
    for size in reversed(sizes):
        out.append(row & (size - 1))
        row = row >> log2(size)
    return out[::-1]


def selection(shape, row_key, column_key):
    hit = row_key(iota(shape, 0)) == column_key(iota(shape, 1))
    return jnp.where(hit, 1.0, 0.0).astype(BF)


def pick(left_key, left_size, right, right_key):
    return dot(selection((left_size, right.shape[0]), left_key, right_key), right, ((1,), (0,)))


def store_blocks(ref, rows):
    ref[...] = rows.astype(BF).reshape(ref.shape)


def load_blocks(ref):
    return ref[...].reshape(2 * ref.shape[0], ref.shape[2])


def itself(row):
    return row


def as_column(row):
    size = row.shape[1]
    eye = iota((size, size), 0) == iota((size, size), 1)
    return jnp.sum(jnp.where(eye, row, 0.0), 1, keepdims=True)


def row_of(column):
    return jnp.transpose(jnp.broadcast_to(column, (column.shape[0], LANES)))[:1]


def stack_rows(first, second, extras):
    lane = iota((first.shape[0], LANES), 1)
    high = jnp.zeros(lane.shape, F32)
    low = jnp.zeros(lane.shape, F32)
    for place, value in enumerate(extras):
        top = value.astype(BF).astype(F32)
        high = jnp.where(lane == place, top, high)
        low = jnp.where(lane == place, value - top, low)
    return jnp.concatenate(
        [jnp.concatenate([first, high], 1), jnp.concatenate([second, low], 1)], 0
    ).astype(BF)


def slot_column(router_ref, scale_ref):
    router_f = router_ref[...].astype(F32)
    inv_p = lax.rsqrt(jnp.sum(router_f * router_f, 1, keepdims=True) + EPSILON)
    scale = as_column(scale_ref[...])
    return router_f, inv_p, scale


def softmax(logit):
    expo = jnp.exp(logit)
    return expo, expo / jnp.sum(expo, 0, keepdims=True)


def fetch(sources, targets, sems):
    copies = [
        pltpu.make_async_copy(source, target, sems.at[place])
        for place, (source, target) in enumerate(zip(sources, targets))
    ]
    for copy in copies:
        copy.start()
    return copies


def expert_rows(plan, experts):
    copies, halves = plan

    def key(row):
        _, place, _, kind = digits(row, (copies, experts, halves, 2))
        return kind * experts + place

    return key


def half_first(key, inner, halves):
    def moved(row):
        half, place, kind = digits(row, (halves, inner, 2))
        return key((place * halves + half) * 2 + kind)

    return moved


def image_rows(images, halves):
    def key(row):
        place, _, kind = digits(row, (images, halves, 2))
        return kind * images + place

    return key


def lane_factor(shape):
    return 1.0 + iota(shape, 1).astype(F32) * (1.0 / LANES)


def front_kernel(
    plan, tok_hbm, grad_hbm, router_hbm, scale_hbm, sent_ref, logit_ref, inv_ref,
    tok_ref, grad_ref, router_ref, scale_ref, sems,
):
    arrived = fetch(
        [tok_hbm, router_hbm, scale_hbm, grad_hbm], [tok_ref, router_ref, scale_ref, grad_ref], sems
    )
    for copy in arrived[:3]:
        copy.wait()
    tok = tok_ref[0]
    tok_f = tok.astype(F32)
    inv_x = row_of(lax.rsqrt(jnp.sum(tok_f * tok_f, 1, keepdims=True) + EPSILON))
    _, inv_p, scale = slot_column(router_ref, scale_ref)
    raw = dot(router_ref[...], tok, ((1,), (1,)))
    logit = raw * inv_x * (inv_p * scale)
    expo, comb = softmax(logit)
    numer = dot(expo.astype(BF), tok, ((1,), (0,)))
    arrived[3].wait()
    dys = dot(comb.astype(BF), grad_ref[0], ((1,), (0,)))
    rows = stack_rows(numer, dys, [jnp.sum(expo, 1, keepdims=True)])
    experts = router_ref.shape[0]
    key = half_first(expert_rows(plan, experts), plan[0] * experts, plan[1])
    store_blocks(sent_ref, pick(key, 2 * sent_ref.shape[0], rows, itself))
    logit_ref[...] = logit
    inv_ref[...] = inv_x


def expert_kernel(
    images, halves, got_ref, one_ref, two_ref, back_ref, rows_ref, grad_rows_ref, hidden_ref, dact_ref
):
    width = one_ref.shape[1]
    key = half_first(image_rows(images, halves), images, halves)
    sums = pick(itself, 2 * images, load_blocks(got_ref), key)
    den = sums[:images, width : width + 1] + sums[images:, width : width + 1]
    rows = (sums[:images, :width] / den).astype(BF)
    grad_rows = sums[images:, :width].astype(BF)
    act = dot(rows, one_ref[0], ((1,), (0,)))
    grad_h = dot(grad_rows, two_ref[0], ((1,), (1,)))
    phi = 0.5 * (1.0 + lax.erf(act * ROOT_HALF))
    hidden = (act * phi).astype(BF)
    dact = (grad_h * (phi + act * jnp.exp(-0.5 * act * act) * DENSITY)).astype(BF)
    out_part = dot(hidden, two_ref[0], ((1,), (0,)))
    in_part = dot(dact, one_ref[0], ((1,), (1,)))
    corr = jnp.sum(dact.astype(F32) * act, 1, keepdims=True)
    packed = stack_rows(out_part, in_part, [den, corr])
    store_blocks(back_ref, pick(key, 2 * back_ref.shape[0], packed, itself))
    rows_ref[...] = rows
    grad_rows_ref[...] = grad_rows
    hidden_ref[...] = hidden
    dact_ref[...] = dact


def outer_kernel(size, left_ref, right_ref, out_hbm, out_ref, sems):
    copies = []
    for place in range(left_ref.shape[1] // size):
        part = slice(place * size, (place + 1) * size)
        out_ref[0, part] = dot(left_ref[:, part], right_ref[...], ((0,), (0,))).astype(BF)
        copy = pltpu.make_async_copy(
            out_ref.at[:, pl.ds(place * size, size)], out_hbm.at[:, pl.ds(place * size, size)],
            sems.at[place],
        )
        copy.start()
        copies.append(copy)
    for copy in copies:
        copy.wait()


def middle_kernel(
    plan, back_ref, tok_ref, grad_ref, logit_ref, inv_ref, router_ref, scale_ref,
    sums_ref, outs_ref, coef_ref, mix_ref, signal_ref,
):
    experts, width = router_ref.shape
    source = half_first(expert_rows(plan, experts), plan[0] * experts, plan[1])
    sums = pick(itself, 2 * experts, load_blocks(back_ref), source)
    extras = sums[:experts, width:] + sums[experts:, width:]
    den = extras[:, :1] * (1.0 / (plan[0] * plan[1]))
    corr = extras[:, 1:2]
    ys = sums[:experts, :width].astype(BF)
    dxs = sums[experts:, :width].astype(BF)
    router_f, inv_p, scale = slot_column(router_ref, scale_ref)
    tok = tok_ref[0]
    logit = logit_ref[...]
    inv_x = inv_ref[...]
    expo, comb = softmax(logit)
    dcomb = dot(ys, grad_ref[0], ((1,), (1,)))
    ddisp = dot(dxs, tok, ((1,), (1,)))
    dlc = comb * (dcomb - jnp.sum(comb * dcomb, 0, keepdims=True))
    grad_l = expo / den * (ddisp - corr) + dlc
    product = grad_l * logit
    grad_q = (grad_l * inv_x * (inv_p * scale)).astype(BF)
    outer = dot(grad_q, tok, ((1,), (0,)))
    total = jnp.sum(product, 1, keepdims=True)
    local = outer - inv_p * inv_p * total * router_f
    sums_ref[...] = jnp.concatenate([local, total / scale * lane_factor((experts, LANES))], 1)
    outs_ref[...] = ys
    coef_ref[...] = jnp.concatenate([expo, grad_q.astype(F32)], 0).astype(BF)
    mix_ref[...] = jnp.concatenate([dxs.astype(F32) / den, router_f], 0).astype(BF)
    signal_ref[...] = inv_x * inv_x * jnp.sum(product, 0, keepdims=True)


def combined_kernel(logit_ref, outs_ref, combined_ref):
    _, comb = softmax(logit_ref[...])
    combined_ref[0] = dot(comb.astype(BF), outs_ref[...], ((0,), (0,))).astype(BF)


def tail_kernel(tok_ref, coef_ref, mix_ref, signal_ref, grads_ref):
    signal = signal_ref[...]
    column = jnp.transpose(jnp.broadcast_to(signal, (LANES, signal.shape[1])))[:, :1]
    grads = dot(coef_ref[...], mix_ref[...], ((0,), (0,)))
    grads_ref[0] = (grads - column * tok_ref[0].astype(F32)).astype(BF)


def last_kernel(mine_ref, other_ref, router_ref, scale_ref):
    sums = mine_ref[...] + other_ref[...]
    experts, width = router_ref.shape
    router_ref[...] = sums[:, :width]
    eye = iota((experts, experts), 0) == iota((experts, experts), 1)
    scale = jnp.sum(sums[:, width:] / lane_factor((experts, LANES)), 1, keepdims=True) * (1.0 / LANES)
    scale_ref[...] = jnp.sum(jnp.where(eye, scale, 0.0), 0, keepdims=True)


def call(kernel, outs, *args, stays=(), buffers=(), flops=10**7, room=24 * 2**20, home=pltpu.VMEM):
    specs = [pl.BlockSpec(memory_space=pltpu.VMEM)] * len(args)
    args = list(args)
    for place in stays:
        specs[place] = pl.BlockSpec(memory_space=pltpu.HBM)
        args[place] = pltpu.with_memory_space_constraint(args[place], pltpu.HBM)
    return pl.pallas_call(
        kernel,
        out_shape=[jax.ShapeDtypeStruct(shape, dtype) for shape, dtype in outs],
        in_specs=specs,
        out_specs=[pl.BlockSpec(memory_space=home)] * len(outs),
        scratch_shapes=buffers,
        compiler_params=pltpu.CompilerParams(vmem_limit_bytes=room),
        cost_estimate=pl.CostEstimate(
            flops=flops, bytes_accessed=sum(a.size * a.dtype.itemsize for a in args), transcendentals=0
        ),
    )(*args)


def weight_grad(left, right):
    size = 256
    shape = (1, left.shape[1], right.shape[1])
    (out,) = call(
        functools.partial(outer_kernel, size), [(shape, BF)], left, right,
        buffers=[pltpu.VMEM(shape, BF), pltpu.SemaphoreType.DMA((shape[1] // size,))],
        flops=10**9, home=pltpu.HBM,
    )
    return out


def exchange(block, axes):
    return lax.all_to_all(block, axes, split_axis=0, concat_axis=0, tiled=True)


def pair(term, mask, devices):
    return lax.ppermute(term, BOTH, [(d, d ^ mask) for d in range(devices)])


def sum_everywhere(term, devices, beside):
    masks = [1] + [1 << place for place in range(2, log2(devices))]
    rounds = [masks[place : place + 2] for place in range(0, len(masks), 2)]
    done = []

    def together(value):
        if len(done) < len(beside):
            value, ready = lax.optimization_barrier((value, beside[len(done)]))
            done.append(ready)
        return value

    for group in rounds:
        own = term.astype(BF)
        steps = [group[1], group[0], group[0] ^ group[1]] if len(group) == 2 else group
        terms = [own] + [pair(own, mask, devices) for mask in steps]
        terms[-1] = together(terms[-1])
        terms = [value.astype(F32) for value in terms]
        term = terms[0] + terms[1]
        if len(terms) == 4:
            term = term + (terms[2] + terms[3])
    other = together(pair(term, 2, devices))
    return term, other, done + beside[len(done) :]


def shards(images, halves, tokens, grad_out, router, slot_scale, w_in, w_out):
    devices = images * halves
    tok_rows, width = tokens.shape[1:]
    experts = router.shape[1]
    plan = (images // experts, halves)
    hidden_dev = w_in.shape[2]
    long = width + LANES
    router_t = router.T
    scale_row = slot_scale.reshape(1, experts)
    inputs = (tokens, grad_out, router_t, scale_row)
    sent, logit, inv_x = call(
        functools.partial(front_kernel, plan),
        [((devices, 2, long), BF), ((experts, tok_rows), F32), ((1, tok_rows), F32)],
        *inputs,
        stays=range(4),
        buffers=[pltpu.VMEM(a.shape, a.dtype) for a in inputs] + [pltpu.SemaphoreType.DMA((4,))],
        flops=FRONT,
    )
    got = exchange(sent, ("tok", "img"))
    back, rows, grad_rows, hidden, dact = call(
        functools.partial(expert_kernel, images, halves),
        [((devices, 2, long), BF), ((images, width), BF), ((images, width), BF),
         ((images, hidden_dev), BF), ((images, hidden_dev), BF)],
        got, w_in, w_out,
        flops=10**9,
    )
    back = exchange(back, ("tok", "img"))
    grad_w_in = weight_grad(rows, dact)
    grad_w_out = weight_grad(hidden, grad_rows)
    sums, ys, coef, mix, signal = call(
        functools.partial(middle_kernel, plan),
        [((experts, long), F32), ((experts, width), BF), ((2 * experts, tok_rows), BF),
         ((2 * experts, width), BF), ((1, tok_rows), F32)],
        back, tokens, grad_out, logit, inv_x, router_t, scale_row,
    )
    (combined,) = call(combined_kernel, [(tokens.shape, BF)], logit, ys)
    (grad_tokens,) = call(tail_kernel, [(tokens.shape, BF)], tokens, coef, mix, signal)
    mine, other, ((grad_w_in, combined), grad_w_out, grad_tokens) = sum_everywhere(
        sums, devices, [(grad_w_in, combined), grad_w_out, grad_tokens]
    )
    grad_router, grad_scale = call(
        last_kernel, [((experts, width), F32), ((1, experts), F32)], mine, other
    )
    return (combined, grad_tokens, grad_router.T, grad_scale[0], grad_w_in, grad_w_out)


def solution(mesh):
    images, halves = mesh.shape["img"], mesh.shape["tok"]

    def body(*args):
        return shards(images, halves, *args)

    return jax.shard_map(
        body,
        mesh=mesh,
        in_specs=(
            P("img", "tok", None),
            P("img", "tok", None),
            P(),
            P(),
            P("img", None, "tok"),
            P("img", "tok", None),
        ),
        out_specs=(
            P("img", "tok", None),
            P("img", "tok", None),
            P(),
            P(),
            P("img", None, "tok"),
            P("img", "tok", None),
        ),
        check_vma=False,
    )
```
